32 devices in a mesh: dp: 8 (over z, core), tensor: 4 (over y, x).
Axes of the slice: x: 2, y: 2, z: 4, core: 2. Of those that a mesh axis runs over, the one named last changes fastest.
Arguments:
- hidden_in: bfloat16 [6144, 2048], P(('dp', 'tensor')), may hold values from -6 to 6
- attn_gain: float32 [2048], replicated, may hold values from 0.5 to 1.5
- q_weight: bfloat16 [2048, 2048], P(None, 'tensor'), may hold values from -0.125 to 0.125
- q_bias: float32 [2048], P('tensor'), may hold values from -1.75 to 1.75
- k_weight: bfloat16 [2048, 2048], P(None, 'tensor'), may hold values from -0.125 to 0.125
- k_bias: float32 [2048], P('tensor'), may hold values from -1.75 to 1.75
- v_weight: bfloat16 [2048, 2048], P(None, 'tensor'), may hold values from -0.125 to 0.125
- v_bias: float32 [2048], P('tensor'), may hold values from -1.75 to 1.75
- o_weight: bfloat16 [2048, 2048], P('tensor'), may hold values from -0.75 to 0.75
- mlp_gain: float32 [2048], replicated, may hold values from 0.5 to 1.5
- expert_gate: bfloat16 [8, 2048, 1408], P('dp', None, 'tensor'), may hold values from -0.125 to 0.125
- expert_up: bfloat16 [8, 2048, 1408], P('dp', None, 'tensor'), may hold values from -0.125 to 0.125
- expert_down: bfloat16 [8, 1408, 2048], P('dp', 'tensor'), may hold values from -0.4375 to 0.4375
- shared_gate: bfloat16 [2048, 5632], P(None, 'tensor'), may hold values from -0.125 to 0.125
- shared_up: bfloat16 [2048, 5632], P(None, 'tensor'), may hold values from -0.125 to 0.125
- shared_down: bfloat16 [5632, 2048], P('tensor'), may hold values from -0.15625 to 0.15625
- shared_router: bfloat16 [2048], replicated, may hold values from -0.125 to 0.125
- routes: int32 [6144, 4], P('dp'), may hold values from 0 to 7, all different within a row; in each aligned block of 768 rows (0 to 767, 768 to 1535, ...) at most 480 rows name the same one
- gate_weights: float32 [6144, 4], P('dp'), may hold values from 0.1 to 0.4
- lengths: int32 [8, 2], replicated, may hold values from 1 to 128, 224 in all within a row
- loss_mask: int32 [6144], replicated, may hold values 0 or 1
- teacher: bfloat16 [6144, 2048], P(('dp', 'tensor')), may hold values from -9 to 9
- cotangent: bfloat16 [6144, 2048], P(('dp', 'tensor')), may hold values from -6 to 6
Outputs:
- block_out: bfloat16 [6144, 2048], P(('dp', 'tensor'))
- teacher_loss: float32 [], replicated
- input_grad: float32 [6144, 2048], P(('dp', 'tensor'))
- attn_gain_grad: float32 [2048], replicated
- q_weight_grad: float32 [2048, 2048], P(None, 'tensor')
- q_bias_grad: float32 [2048], P('tensor')
- k_weight_grad: float32 [2048, 2048], P(None, 'tensor')
- k_bias_grad: float32 [2048], P('tensor')
- v_weight_grad: float32 [2048, 2048], P(None, 'tensor')
- v_bias_grad: float32 [2048], P('tensor')
- o_weight_grad: float32 [2048, 2048], P('tensor')
- mlp_gain_grad: float32 [2048], replicated
- expert_gate_grad: float32 [8, 2048, 1408], P('dp', None, 'tensor')
- expert_up_grad: float32 [8, 2048, 1408], P('dp', None, 'tensor')
- expert_down_grad: float32 [8, 1408, 2048], P('dp', 'tensor')
- shared_gate_grad: float32 [2048, 5632], P(None, 'tensor')
- shared_up_grad: float32 [2048, 5632], P(None, 'tensor')
- shared_down_grad: float32 [5632, 2048], P('tensor')
- shared_router_grad: float32 [2048], replicated
The draws below stay inside these ranges and needn't reach their ends.
Inputs may be any that keep to these rules, and one draw needn't show every extreme that they name: `routes`: in each aligned block of 768 rows (one group), no expert is named by more than 480 rows, a bound that some block reaches; a row names different experts.
All inputs are finite; a program needn't handle non-finite values.
Results may differ from the reference program's by a relative error of at most 0.035.
Values may be sent and summed in bfloat16 or wider, within the bound.
No kernel may reach another device: no remote copies, remote signals or barrier semaphores. Data moves between devices by JAX's collectives and lax.ppermute only.
A program may use at most 384 MiB of HBM per device.

```python
import math
import jax
import jax.numpy as jnp
import numpy as np
from jax import lax

D = 2048
H = 16
HD = 128
FE = 1408
FS = 5632
TOPK = 4
PROMPT = 512
SLOT = 128
CONTS = 2
GROUP = 768
TOKENS = 6144
EXPERTS = 8
CAPG = 480
N_DP = 8
N_TENSOR = 4


def draw_teacher(key, part):
    key = jax.random.fold_in(key, 7)
    ramp = jnp.arange(TOKENS, dtype=jnp.float32)[:, None] / (TOKENS - 1)
    base = jax.random.truncated_normal(key, -3.0, 3.0, (TOKENS, D), jnp.float32)
    return (base * (1.0 + 2.0 * ramp)).astype(jnp.bfloat16)


def touch_ends(drawn, stream_key, least, high):
    longest = drawn.shape.index(max(drawn.shape))
    spots = []
    for shift in (0, 1):
        where = [jax.random.randint(jax.random.fold_in(stream_key, axis), (), 0, length) for axis, length in enumerate(drawn.shape)]
        where[longest] = (where[longest] + shift) % drawn.shape[longest]
        spots.append(tuple(where))
    return drawn.at[spots[0]].set(least).at[spots[1]].set(high)


def block_scale(stream_key, extent, pieces, least, top_value):
    level, own = 1.0, jax.random.fold_in(stream_key, 6)
    for axis_at, blocks in pieces:
        heights = jnp.exp(jax.random.uniform(jax.random.fold_in(own, axis_at), (blocks,), jnp.float32, least / len(pieces), top_value / len(pieces)))
        level = level * jnp.repeat(heights, extent[axis_at] // blocks).reshape([-1 if axis == axis_at else 1 for axis in range(len(extent))])
    return level


def profile(amount, total, bound, skew):
    portions = [(1 << 20) // math.isqrt(rank ** skew) + 1 for rank in range(2, amount + 1)]
    rest, holding = total - bound - (amount - 1), [1] * (amount - 1)
    while rest > 0:
        candidates = [i for i in range(amount - 1) if holding[i] < bound]
        mass, budget = sum([portions[i] for i in candidates]), rest
        for i in candidates:
            more = min(bound - holding[i], max(1, budget * portions[i] // mass), rest)
            holding[i] = holding[i] + more
            rest = rest - more
    return np.array([bound] + holding)


def ragged_sizes(key, amount, total, most, skew):
    if amount == 2:
        one = jax.random.randint(key, (), max(1, total - most), min(most, total - 1) + 1)
        return jnp.stack([one, total - one])
    tallies = jnp.asarray(profile(amount, total, most, skew), jnp.int32)
    couples = (amount - 1) // 2
    source_of, taker = tallies[1:1 + 2 * couples:2], tallies[2:2 + 2 * couples:2]
    slack = jnp.minimum(source_of - 1, most - taker)
    shifted = jax.random.randint(jax.random.fold_in(key, 1), (couples,), 0, 1 << 20) % (slack + 1)
    tallies = tallies.at[1:1 + 2 * couples:2].set(source_of - shifted).at[2:2 + 2 * couples:2].set(taker + shifted)
    return tallies[jax.random.permutation(jax.random.fold_in(key, 2), amount)]


def assign_block(rng, own, number, rows, amount, top, most, skew):
    order = jax.random.permutation(rng, amount)
    heavy_load, ordinary = shares(amount, rows * top, most, skew, True), shares(amount, rows * top, most, skew, False)
    places = jnp.arange(amount)

    def named(tallies, turn):
        used = int((tallies > 0).sum())
        fixed = max(1, used // 4)
        shifted = fixed + (places - fixed + turn * (used - fixed)) % max(1, amount - fixed)
        return jnp.zeros((amount,), jnp.int32).at[order[jnp.where(places < fixed, places, shifted)]].set(jnp.asarray(tallies, jnp.int32))

    tallies = jnp.where(number % 4 == 0, named(heavy_load, number // 4), named(ordinary, number - number // 4 - 1))
    mixed = jax.random.permutation(jax.random.fold_in(own, 3), amount)
    source_of, taker = mixed[0:amount // 2 * 2:2], mixed[1:amount // 2 * 2:2]
    slack = jnp.minimum(tallies[source_of] - 1, most - tallies[taker]) // 2
    slack = jnp.where((source_of == order[0]) | (taker == order[0]) | (tallies[taker] == 0), 0, jnp.maximum(slack, 0))
    shifted = jax.random.randint(jax.random.fold_in(own, 4), (amount // 2,), 0, 1 << 20) % (slack + 1)
    tallies = tallies.at[source_of].add(-shifted).at[taker].add(shifted)
    members = jnp.searchsorted(jnp.cumsum(tallies), jnp.arange(rows * top), side="right").astype(jnp.int32)
    grid = members.reshape(top, rows).T
    grid = grid[jax.random.permutation(jax.random.fold_in(own, 1), rows)]
    turn = jax.random.randint(jax.random.fold_in(own, 2), (rows, 1), 0, top)
    return jnp.take_along_axis(grid, (jnp.arange(top)[None, :] + turn) % top, axis=1)


def shares(number_of, total, limit, lean, full):
    loads = [(1 << 20) // math.isqrt(grade ** lean) + 1 for grade in range(1, number_of + 1)]
    largest = limit if full else min(limit, max(-(-total // number_of), total * loads[0] // sum(loads)))
    least = 1 if total - largest >= number_of - 1 else 0
    holding, spare = [largest] + [least] * (number_of - 1), total - largest - least * (number_of - 1)
    while spare > 0:
        movable = [i for i in range(1, number_of) if holding[i] < largest] or [i for i in range(1, number_of) if holding[i] < limit]
        pool, remaining = sum([loads[i] for i in movable]), spare
        for i in movable:
            extra = min(limit - holding[i], max(1, remaining * loads[i] // pool), spare)
            holding[i] = holding[i] + extra
            spare = spare - extra
    return np.array(holding)


def normal_values(key, shape, deviation, bound, shards=(), held_as=jnp.bfloat16):
    drawn = jax.random.normal(key, shape, jnp.float32) * deviation
    if len(shards) > 0:
        drawn = block_scale(key, shape, shards, -0.22, 0.18) * drawn
    return jnp.clip(drawn, min=-bound, max=bound).astype(held_as)


def setup_inputs(seed: int = 0) -> dict:
    seeds = jax.random.split(jax.random.key(seed), 24)
    hidden_in = normal_values(seeds[0], (TOKENS, D), 1.0, 6.0, ((0, 32),))
    attn_gain = jnp.clip(1.0 + 0.1 * jax.random.normal(seeds[1], (D,), jnp.float32), 0.5, 1.5)
    q_weight = normal_values(seeds[2], (D, H * HD), D ** -0.5, 0.125, ((1, 4),))
    q_bias = normal_values(seeds[3], (H * HD,), 0.3, 1.75, ((0, 4),), jnp.float32)
    k_weight = normal_values(seeds[4], (D, H * HD), D ** -0.5, 0.125, ((1, 4),))
    k_bias = normal_values(seeds[5], (H * HD,), 0.3, 1.75, ((0, 4),), jnp.float32)
    v_weight = normal_values(seeds[6], (D, H * HD), D ** -0.5, 0.125, ((1, 4),))
    v_bias = normal_values(seeds[7], (H * HD,), 0.3, 1.75, ((0, 4),), jnp.float32)
    o_weight = normal_values(seeds[8], (H * HD, D), (H * HD // 32) ** -0.5, 0.75, ((0, 4),))
    mlp_gain = jnp.clip(1.0 + 0.1 * jax.random.normal(seeds[9], (D,), jnp.float32), 0.5, 1.5)
    expert_gate = normal_values(seeds[10], (EXPERTS, D, FE), D ** -0.5, 0.125, ((0, 8), (2, 4)))
    expert_up = normal_values(seeds[11], (EXPERTS, D, FE), D ** -0.5, 0.125, ((0, 8), (2, 4)))
    expert_down = normal_values(seeds[12], (EXPERTS, FE, D), (FE // 8) ** -0.5, 0.4375, ((0, 8), (1, 4)))
    shared_gate = normal_values(seeds[13], (D, FS), D ** -0.5, 0.125, ((1, 4),))
    shared_up = normal_values(seeds[14], (D, FS), D ** -0.5, 0.125, ((1, 4),))
    shared_down = normal_values(seeds[15], (FS, D), (FS // 4) ** -0.5, 0.15625, ((0, 4),))
    shared_router = normal_values(seeds[16], (D,), D ** -0.5, 0.125)
    routes_keys = jax.random.split(jax.random.fold_in(seeds[17], 1), TOKENS // GROUP)
    routes_turns = jax.random.permutation(jax.random.fold_in(seeds[17], 3), TOKENS // GROUP)
    routes = jax.vmap(lambda own, number: assign_block(jax.random.fold_in(seeds[17], 2), own, number, GROUP, EXPERTS, TOPK, CAPG, 2))(routes_keys, routes_turns).reshape((TOKENS, TOPK))
    gate_weights = jnp.clip(jnp.exp(math.log(0.4) - 1.3862944 * jax.random.uniform(seeds[18], (TOKENS, TOPK), jnp.float32) ** block_scale(seeds[18], (TOKENS, TOPK), ((0, 8),), -0.2, 0.2)), 0.1, 0.4)
    lengths = jax.vmap(lambda own: ragged_sizes(own, CONTS, (3 * CONTS + 1) * SLOT // 4, SLOT, 2))(jax.random.split(seeds[19], N_DP)).reshape((N_DP, CONTS)).astype(jnp.int32)
    loss_mask = touch_ends((jax.random.randint(seeds[20], (TOKENS,), 0, 2) < 1).astype(jnp.int32), jax.random.fold_in(seeds[20], 1), 0, 1)
    teacher = draw_teacher(jax.random.fold_in(seeds[23], 71), 0)
    cotangent = normal_values(seeds[22], (TOKENS, D), 1.0, 6.0, ((0, 32),))
    return {"hidden_in": hidden_in, "attn_gain": attn_gain, "q_weight": q_weight, "q_bias": q_bias, "k_weight": k_weight, "k_bias": k_bias, "v_weight": v_weight, "v_bias": v_bias, "o_weight": o_weight, "mlp_gain": mlp_gain, "expert_gate": expert_gate, "expert_up": expert_up, "expert_down": expert_down, "shared_gate": shared_gate, "shared_up": shared_up, "shared_down": shared_down, "shared_router": shared_router, "routes": routes, "gate_weights": gate_weights, "lengths": lengths, "loss_mask": loss_mask, "teacher": teacher, "cotangent": cotangent}


EPSILON = 1e-06
ROTARY_BASE = 1000000.0
HIGHEST = lax.Precision.HIGHEST

@jax.custom_vjp
def low(v):
    return lax.optimization_barrier(v.astype(jnp.bfloat16)).astype(jnp.float32)

@jax.custom_vjp
def low_back(v):
    return v

def low_keep(v):
    return (low(v), None)

def low_pass(kept, grad):
    return (grad,)

def back_keep(v):
    return (v, None)

def back_low(kept, grad):
    return (low(grad),)
low.defvjp(low_keep, low_pass)
low_back.defvjp(back_keep, back_low)

def slot_layout(lengths_row):
    position = jnp.arange(GROUP, dtype=jnp.int32)
    offset = jnp.maximum(position - PROMPT, 0)
    in_prompt = position < PROMPT
    segment = jnp.where(in_prompt, 0, 1 + offset // SLOT)
    rotary_place = jnp.where(in_prompt, position, PROMPT + offset % SLOT)
    matches = segment[:, None] - 1 == jnp.arange(CONTS, dtype=jnp.int32)[None, :]
    length_here = lax.optimization_barrier(jnp.sum(jnp.where(matches, lengths_row[None, :], 0), axis=1))
    living = in_prompt | (offset % SLOT < length_here)
    return (segment, rotary_place, living)

def visible_keys(segment, living):
    position = jnp.arange(GROUP, dtype=jnp.int32)
    causal = position[None, :] <= position[:, None]
    same_part = (segment[None, :] == segment[:, None]) | (segment[None, :] == 0)
    return causal & same_part & living[None, :]

def rotary_tables(rotary_place):
    freqs = jnp.exp(jnp.arange(HD // 2, dtype=jnp.float32) * (-2.0 * math.log(ROTARY_BASE) / HD))
    angles = rotary_place.astype(jnp.float32)[:, None] * freqs[None, :]
    angles = jnp.concatenate([angles, angles], axis=1)
    return (jnp.cos(angles), jnp.sin(angles))

def rotate(values, cosine, sine):
    half = values.shape[-1] // 2
    flipped = jnp.concatenate([-values[..., half:], values[..., :half]], axis=-1)
    return values * cosine[:, None, :] + flipped * sine[:, None, :]

def product(left, right):
    return jnp.dot(left, right, precision=HIGHEST, preferred_element_type=jnp.float32)

def layer_group(group_in, group_gates, group_routes, lengths_row, params):
    attn_gain, q_weight, q_bias, k_weight, k_bias, v_weight, v_bias, o_weight, mlp_gain, expert_gate, expert_up, expert_down, shared_gate, shared_up, shared_down, shared_router = params
    segment, rotary_place, living = slot_layout(lengths_row)
    visible = visible_keys(segment, living)
    cosine, sine = rotary_tables(rotary_place)
    normed_one = low(group_in * lax.rsqrt(lax.optimization_barrier(jnp.mean(group_in * group_in, axis=1, keepdims=True)) + EPSILON) * attn_gain)
    query_lin = low_back(product(normed_one, q_weight) + q_bias).reshape(GROUP, H, HD)
    key_lin = low_back(product(normed_one, k_weight) + k_bias).reshape(GROUP, H, HD)
    value = low(low_back(product(normed_one, v_weight) + v_bias)).reshape(GROUP, H, HD)
    query = low(rotate(query_lin, cosine, sine))
    key = low(rotate(key_lin, cosine, sine))
    scores = jnp.einsum('thd,shd->hts', query, key, precision=HIGHEST) * (1.0 / math.sqrt(HD))
    scores = low_back(jnp.where(visible[None], scores, -1e+30))
    top_score = lax.optimization_barrier(jnp.max(scores, axis=2, keepdims=True))
    expo = jnp.exp(scores - top_score)
    probs = low(expo / lax.optimization_barrier(jnp.sum(expo, axis=2, keepdims=True)))
    mixed = jnp.einsum('hts,shd->thd', probs, value, precision=HIGHEST).reshape(GROUP, H * HD)
    mixed = low(low_back(mixed))
    width = H * HD // N_TENSOR
    parts = jnp.einsum('tsk,skd->tsd', mixed.reshape(GROUP, N_TENSOR, width), o_weight.reshape(N_TENSOR, width, D), precision=HIGHEST)
    hidden_mid = group_in + lax.optimization_barrier(jnp.sum(low(low_back(parts)), axis=1))
    normed_two = low(hidden_mid * lax.rsqrt(lax.optimization_barrier(jnp.mean(hidden_mid * hidden_mid, axis=1, keepdims=True)) + EPSILON) * mlp_gain)
    shared_gate_in = low_back(product(normed_two, shared_gate))
    shared_up_in = low_back(product(normed_two, shared_up))
    shared_hidden = low(jax.nn.silu(shared_gate_in) * shared_up_in)
    shared_out = low_back(product(shared_hidden, shared_down))
    router_gate = jax.nn.sigmoid(product(normed_two, shared_router))
    mixing = lax.optimization_barrier(jnp.sum(jnp.where(group_routes[:, :, None] == jnp.arange(EXPERTS, dtype=jnp.int32)[None, None, :], group_gates[:, :, None], 0.0), axis=1))
    gate_in = low_back(jnp.einsum('td,edf->etf', normed_two, expert_gate, precision=HIGHEST))
    up_in = low_back(jnp.einsum('td,edf->etf', normed_two, expert_up, precision=HIGHEST))
    expert_hidden = low(jax.nn.silu(gate_in) * up_in)
    expert_out = low_back(jnp.einsum('etf,efd->etd', expert_hidden, expert_down, precision=HIGHEST))
    expert_mix = jnp.einsum('te,etd->td', mixing, expert_out, precision=HIGHEST)
    return low_back(hidden_mid + router_gate[:, None] * shared_out + expert_mix)

def reference(hidden_in, attn_gain, q_weight, q_bias, k_weight, k_bias, v_weight, v_bias, o_weight, mlp_gain, expert_gate, expert_up, expert_down, shared_gate, shared_up, shared_down, shared_router, routes, gate_weights, lengths, loss_mask, teacher, cotangent):
    params = tuple((item.astype(jnp.float32) for item in (attn_gain, q_weight, q_bias, k_weight, k_bias, v_weight, v_bias, o_weight, mlp_gain, expert_gate, expert_up, expert_down, shared_gate, shared_up, shared_down, shared_router)))
    inputs = hidden_in.astype(jnp.float32)
    group_routes = routes.reshape(N_DP, GROUP, TOPK)
    group_gates = gate_weights.astype(jnp.float32).reshape(N_DP, GROUP, TOPK)
    living = jax.vmap(slot_layout)(lengths)[2].reshape(-1)
    valid = living & (loss_mask == 1)
    valid_count = jnp.sum(valid.astype(jnp.float32))
    target = teacher.astype(jnp.float32)

    def forward(weights, layer_in):

        def one_group(item):
            return layer_group(item[0], item[1], item[2], item[3], weights)
        result = lax.map(jax.checkpoint(one_group), (layer_in.reshape(N_DP, GROUP, D), group_gates, group_routes, lengths))
        result = result.reshape(N_DP * GROUP, D)
        difference = result - target
        loss_value = jnp.sum(jnp.where(valid[:, None], difference * difference, 0.0)) / (valid_count * D)
        return (result, loss_value)
    (result, loss_value), pull = jax.vjp(forward, params, inputs)
    grads, input_grad = pull((cotangent.astype(jnp.float32), jnp.ones((), jnp.float32)))
    return (result.astype(jnp.bfloat16), loss_value, input_grad, grads[0], grads[1], grads[2], grads[3], grads[4], grads[5], grads[6], grads[7], grads[8], grads[9], grads[10], grads[11], grads[12], grads[13], grads[14], grads[15])
```

```python
import math

import jax
import jax.numpy as jnp
from jax import lax
from jax.sharding import PartitionSpec as P

D = 2048
HD = 128
PROMPT = 512
SLOT = 128
CONTS = 2
GROUP = 768


EPSILON = 1e-06
ROTARY_BASE = 1000000.0
WIDE = jnp.float32
NARROW = jnp.bfloat16


def slot_layout(lengths_row, position):
    offset = jnp.maximum(position - PROMPT, 0)
    in_prompt = position < PROMPT
    segment = jnp.where(in_prompt, 0, 1 + offset // SLOT)
    rotary_place = jnp.where(in_prompt, position, PROMPT + offset % SLOT)
    matches = segment[:, None] - 1 == jnp.arange(CONTS, dtype=jnp.int32)[None, :]
    length_here = jnp.sum(jnp.where(matches, lengths_row[None, :], 0), axis=1)
    living = in_prompt | (offset % SLOT < length_here)
    return (segment, rotary_place, living)


def visible_keys(position, segment, living):
    causal = position[None, :] <= position[:, None]
    same_part = (segment[None, :] == segment[:, None]) | (segment[None, :] == 0)
    return causal & same_part & living[None, :]


def rotary_tables(rotary_place):
    freqs = jnp.exp(jnp.arange(HD // 2, dtype=jnp.float32) * (-2.0 * math.log(ROTARY_BASE) / HD))
    angles = rotary_place.astype(jnp.float32)[:, None] * freqs[None, :]
    angles = jnp.concatenate([angles, angles], axis=1)
    return (jnp.cos(angles), jnp.sin(angles))


def rotate(values, cosine, sine):
    half = values.shape[-1] // 2
    flipped = jnp.concatenate([-values[..., half:], values[..., :half]], axis=-1)
    return values * cosine[:, None, :] + flipped * sine[:, None, :]


def rotate_back(grads, cosine, sine):
    half = grads.shape[-1] // 2
    turned = grads * sine[:, None, :]
    flipped = jnp.concatenate([turned[..., half:], -turned[..., :half]], axis=-1)
    return grads * cosine[:, None, :] + flipped


def attention_scores(query_low, key_low, visible, scale):
    scores = (
        jnp.einsum("thd,shd->hts", query_low, key_low, preferred_element_type=jnp.float32) * scale
    )
    return jnp.where(visible[None], scores, -1e30)


def dot_nt(left, right):
    return lax.dot_general(left, right, (((1,), (1,)), ((), ())), preferred_element_type=WIDE)


def dot_nn(left, right):
    return lax.dot_general(left, right, (((1,), (0,)), ((), ())), preferred_element_type=WIDE)


def dot_tn(left, right):
    return lax.dot_general(left, right, (((0,), (0,)), ((), ())), preferred_element_type=WIDE)


def after(value, *others):
    return lax.optimization_barrier((value,) + others)[0]


def flip(value, bit):
    size = lax.axis_size("tensor")
    return lax.ppermute(value, "tensor", [(i, i ^ bit) for i in range(size)])


def split_at(rows):
    return rows // 32 * 16


def plane_gather(value):
    size = lax.axis_size("tensor")
    if size == 4:
        cut = split_at(value.shape[0])
        one, two = flip(value, 1), flip(value, 2)
        low, high = flip(two[:cut], 1), flip(one[cut:], 2)
        return [value, one, two, jnp.concatenate([low, high], axis=0)]
    blocks, bit = [value], 1
    while bit < size:
        blocks = blocks + [flip(block, bit) for block in blocks]
        bit *= 2
    return blocks


def plane_scatter(parts):
    size = lax.axis_size("tensor")
    if size == 4:
        cut = split_at(parts[3].shape[0])
        far = parts[3].astype(NARROW)
        low, high = flip(far[:cut], 1), flip(far[cut:], 2)
        two = jnp.concatenate(
            [(parts[2][:cut].astype(WIDE) + low.astype(WIDE)).astype(NARROW), parts[2][cut:].astype(NARROW)], axis=0
        )
        one = jnp.concatenate(
            [parts[1][:cut].astype(NARROW), (parts[1][cut:].astype(WIDE) + high.astype(WIDE)).astype(NARROW)], axis=0
        )
        return parts[0].astype(WIDE) + flip(one, 1).astype(WIDE) + flip(two, 2).astype(WIDE)
    parts = [part.astype(WIDE) for part in parts]
    bit = size // 2
    while bit >= 1:
        parts = [parts[j] + flip(parts[bit + j].astype(NARROW), bit).astype(WIDE) for j in range(bit)]
        bit //= 2
    return parts[0]


def ring_order(chips):
    odd = list(range(1, chips, 2))
    even = list(range(2, chips, 2))
    return [0] + odd + even[::-1]


def ring_next(value):
    chips = lax.axis_size("dp") // 2
    order = ring_order(chips)
    pairs = [
        (2 * order[i] + c, 2 * order[(i + 1) % chips] + c) for i in range(chips) for c in range(2)
    ]
    return lax.ppermute(value, "dp", pairs)


def swap_core(value):
    size = lax.axis_size("dp")
    return lax.ppermute(value, "dp", [(i, i ^ 1) for i in range(size)])


def ring_sources():
    chips = lax.axis_size("dp") // 2
    order = ring_order(chips)
    index = lax.axis_index("dp")
    chip, core = index // 2, index % 2
    sources = []
    for step in range(chips):
        table = [0] * chips
        for place, here in enumerate(order):
            table[here] = order[(place - step) % chips]
        source = jnp.asarray(table, jnp.int32)[chip]
        sources.append((2 * source + core, 2 * source + 1 - core))
    return sources


def ring_gather(value):
    chips = lax.axis_size("dp") // 2
    held = [value]
    for _ in range(chips - 1):
        held.append(ring_next(held[-1]))
    return [(block, swap_core(block)) for block in held]


def ring_scatter(parts):
    chips = len(parts)
    total = None
    for step in list(range(1, chips)) + [0]:
        mine, other = parts[step]
        here = mine.astype(WIDE) + swap_core(other.astype(NARROW)).astype(WIDE)
        if total is not None:
            here = here + total.astype(WIDE)
        if step == 0:
            return here
        total = ring_next(here.astype(NARROW))


def shards(
    hidden_in,
    attn_gain,
    q_weight,
    q_bias,
    k_weight,
    k_bias,
    v_weight,
    v_bias,
    o_weight,
    mlp_gain,
    expert_gate,
    expert_up,
    expert_down,
    shared_gate,
    shared_up,
    shared_down,
    shared_router,
    routes,
    gate_weights,
    lengths,
    loss_mask,
    teacher,
    cotangent,
):
    wide = WIDE
    narrow = NARROW
    data_index = lax.axis_index("dp")
    slice_index = lax.axis_index("tensor")
    n_dp = lax.axis_size("dp")
    n_tensor = lax.axis_size("tensor")
    rows = hidden_in.shape[0]
    heads = q_weight.shape[1] // HD
    f_expert = expert_gate.shape[2]
    f_shared = shared_gate.shape[1] // n_dp
    scale = 1.0 / math.sqrt(HD)

    position = jnp.concatenate(
        [(slice_index ^ j) * rows + jnp.arange(rows, dtype=jnp.int32) for j in range(n_tensor)]
    )
    own_lengths = lax.dynamic_index_in_dim(lengths, data_index, 0, keepdims=False)
    segment, rotary_place, living = slot_layout(own_lengths, position)
    visible = visible_keys(position, segment, living)
    cosine, sine = rotary_tables(rotary_place)
    every = jnp.arange(GROUP, dtype=jnp.int32)
    living_all = jax.vmap(lambda row: slot_layout(row, every)[2])(lengths)
    valid_count = jnp.sum((living_all.reshape(-1) & (loss_mask == 1)).astype(wide))
    own_mask = lax.dynamic_slice_in_dim(loss_mask, data_index * GROUP + slice_index * rows, rows, 0)
    valid_own = living[:rows] & (own_mask == 1)

    own_routes = lax.dynamic_slice_in_dim(routes, slice_index * rows, rows, 0)
    own_gates = lax.dynamic_slice_in_dim(gate_weights, slice_index * rows, rows, 0)
    mixing = jnp.sum(
        jnp.where(
            own_routes[:, :, None] == jnp.arange(n_dp, dtype=jnp.int32)[None, None, :],
            own_gates[:, :, None],
            0.0,
        ),
        axis=1,
    )
    mixing_all = lax.all_gather(mixing.T, "dp", axis=0)
    mixing_here = lax.dynamic_index_in_dim(mixing_all, data_index, 1, keepdims=False)
    sources = ring_sources()
    mix_steps = [
        jnp.concatenate(
            [lax.dynamic_index_in_dim(mixing_here, s, 0, keepdims=False) for s in pair]
        )
        for pair in sources
    ]

    own_input = hidden_in.astype(wide)
    inverse_one = lax.rsqrt(jnp.mean(own_input * own_input, axis=1, keepdims=True) + EPSILON)
    hat_one = own_input * inverse_one
    normed_one_blocks = plane_gather((hat_one * attn_gain).astype(narrow))
    normed_one = jnp.concatenate(normed_one_blocks, axis=0)

    def pack(expert_rows, shared_rows):
        return jnp.concatenate([expert_rows, shared_rows], axis=0)

    shared_at = data_index * f_shared
    own_gate = pack(
        expert_gate[0].T, lax.dynamic_slice_in_dim(shared_gate, shared_at, f_shared, 1).T
    )
    own_up = pack(expert_up[0].T, lax.dynamic_slice_in_dim(shared_up, shared_at, f_shared, 1).T)
    own_down = pack(expert_down[0], lax.dynamic_slice_in_dim(shared_down, shared_at, f_shared, 0))

    def unpack(blocks):
        return jnp.concatenate(
            [block[:f_expert] for block in blocks] + [block[f_expert:] for block in blocks], axis=0
        )

    own_gate = after(own_gate, normed_one_blocks[-1])
    gate_blocks = plane_gather(own_gate)
    own_up = after(own_up, gate_blocks[-1])
    up_blocks = plane_gather(own_up)

    query_lin = dot_nn(normed_one, q_weight) + q_bias
    key_lin = dot_nn(normed_one, k_weight) + k_bias
    value_low = (dot_nn(normed_one, v_weight) + v_bias).astype(narrow).reshape(GROUP, heads, HD)
    query_low = rotate(query_lin.reshape(GROUP, heads, HD), cosine, sine).astype(narrow)
    key_low = rotate(key_lin.reshape(GROUP, heads, HD), cosine, sine).astype(narrow)
    scores = attention_scores(query_low, key_low, visible, scale)
    top_score = jnp.max(scores, axis=2, keepdims=True)
    expo = jnp.exp(scores - top_score)
    total_expo = jnp.sum(expo, axis=2, keepdims=True)
    log_total = top_score + jnp.log(total_expo)
    probs_low = (expo / total_expo).astype(narrow)
    mixed = jnp.einsum("hts,shd->thd", probs_low, value_low, preferred_element_type=wide)
    mixed_low = mixed.reshape(GROUP, heads * HD).astype(narrow)
    head_part = dot_nn(mixed_low, o_weight).astype(narrow)
    attn_own = plane_scatter([head_part[j * rows : (j + 1) * rows] for j in range(n_tensor)])

    hidden_mid = own_input + attn_own
    inverse_two = lax.rsqrt(jnp.mean(hidden_mid * hidden_mid, axis=1, keepdims=True) + EPSILON)
    hat_two = hidden_mid * inverse_two
    normed_two = (hat_two * mlp_gain).astype(narrow)

    own_down = after(own_down, up_blocks[-1])
    down_blocks = plane_gather(own_down)
    w_gate, w_up, w_down = unpack(gate_blocks), unpack(up_blocks), unpack(down_blocks)
    f_all = w_gate.shape[0]
    f_cut = f_expert * n_tensor

    router_wide = shared_router.astype(wide)
    x_steps, gate_steps, up_steps, hidden_steps, factor_steps, router_steps, out_steps = (
        [] for _ in range(7)
    )
    for step, pair in enumerate(ring_gather(normed_two)):
        x = jnp.concatenate(pair, axis=0)
        router_gate = jax.nn.sigmoid(jnp.sum(x.astype(wide) * router_wide, axis=1))
        gate_in = dot_nt(x, w_gate)
        up_in = dot_nt(x, w_up)
        is_expert = lax.broadcasted_iota(jnp.int32, (1, f_all), 1) < f_cut
        factor = jnp.where(is_expert, mix_steps[step][:, None], router_gate[:, None])
        hidden = (jax.nn.silu(gate_in) * up_in * factor).astype(narrow)
        out = dot_nn(hidden, w_down).astype(narrow)
        x_steps.append(x)
        gate_steps.append(gate_in)
        up_steps.append(up_in)
        hidden_steps.append(hidden)
        factor_steps.append(factor)
        router_steps.append(router_gate)
        out_steps.append((out[:rows], out[rows:]))
    branch_own = ring_scatter(out_steps)
    result = hidden_mid + branch_own

    difference = result - teacher.astype(wide)
    squared_own = jnp.sum(jnp.where(valid_own[:, None], difference * difference, 0.0))
    result_grad = cotangent.astype(wide) + jnp.where(
        valid_own[:, None], difference * (2.0 / (valid_count * D)), 0.0
    )
    grad_own = result_grad.astype(narrow)

    router_grad_part = jnp.zeros((D,), wide)
    g_steps, gate_grads, up_grads, dx_steps = ([] for _ in range(4))
    for step, pair in enumerate(ring_gather(grad_own)):
        g = jnp.concatenate(pair, axis=0)
        gate_in, up_in = gate_steps[step], up_steps[step]
        grad_plain = dot_nt(g, w_down)
        squash = jax.nn.sigmoid(gate_in)
        grad_hidden = grad_plain * factor_steps[step]
        gate_grad = (grad_hidden * up_in * squash * (1.0 + gate_in * (1.0 - squash))).astype(narrow)
        up_grad = (grad_hidden * gate_in * squash).astype(narrow)
        shared_cols = lax.broadcasted_iota(jnp.int32, (1, f_all), 1) >= f_cut
        logit_part = jnp.sum(
            jnp.where(shared_cols, grad_hidden * gate_in * squash * up_in, 0.0), axis=1
        ) * (1.0 - router_steps[step])
        dx = dot_nn(gate_grad, w_gate) + dot_nn(up_grad, w_up)
        dx = (dx + logit_part[:, None] * router_wide[None, :]).astype(narrow)
        router_grad_part = router_grad_part + jnp.sum(
            logit_part[:, None] * x_steps[step].astype(wide), axis=0
        )
        g_steps.append(g)
        gate_grads.append(gate_grad)
        up_grads.append(up_grad)
        dx_steps.append((dx[:rows], dx[rows:]))
    normed_two_grad = ring_scatter(dx_steps)

    x_all = jnp.concatenate(x_steps, axis=0)
    g_all = jnp.concatenate(g_steps, axis=0)
    down_full = dot_tn(jnp.concatenate(hidden_steps, axis=0), g_all).astype(narrow)
    gate_full = dot_tn(jnp.concatenate(gate_grads, axis=0), x_all).astype(narrow)
    up_full = dot_tn(jnp.concatenate(up_grads, axis=0), x_all).astype(narrow)

    def shared_sum(full):
        own = plane_scatter(
            [full[f_cut + j * f_shared : f_cut + (j + 1) * f_shared] for j in range(n_tensor)]
        ).astype(narrow)
        whole = jnp.zeros((n_dp * f_shared, D), narrow)
        for pair, at in zip(ring_gather(own), sources):
            for block, source in zip(pair, at):
                whole = lax.dynamic_update_slice_in_dim(whole, block, source * f_shared, 0)
        return whole

    def expert_sum(full):
        return plane_scatter([full[j * f_expert : (j + 1) * f_expert] for j in range(n_tensor)])

    shared_down_grad = shared_sum(down_full).astype(wide)
    shared_gate_grad = shared_sum(gate_full).T.astype(wide)
    shared_up_grad = shared_sum(up_full).T.astype(wide)

    grad_wide = grad_own.astype(wide)
    mlp_gain_part = jnp.sum(normed_two_grad * hat_two, axis=0)
    scaled_two = normed_two_grad * mlp_gain
    hidden_grad = grad_wide + inverse_two * (
        scaled_two - hat_two * jnp.mean(scaled_two * hat_two, axis=1, keepdims=True)
    )
    hidden_grad_low = jnp.concatenate(plane_gather(hidden_grad.astype(narrow)), axis=0)

    o_grad = dot_tn(hidden_grad_low, mixed_low)
    mixed_grad = dot_nt(hidden_grad_low, o_weight).astype(narrow).reshape(GROUP, heads, HD)
    scores_again = attention_scores(query_low, key_low, visible, scale)
    probs = jnp.exp(scores_again - log_total)
    probs_grad = jnp.einsum("thd,shd->hts", mixed_grad, value_low, preferred_element_type=wide)
    value_grad = jnp.einsum(
        "hts,thd->shd", probs.astype(narrow), mixed_grad, preferred_element_type=wide
    )
    inner = jnp.sum(probs * probs_grad, axis=2, keepdims=True)
    scores_grad = (probs * (probs_grad - inner)).astype(narrow)
    query_grad = (
        jnp.einsum("hts,shd->thd", scores_grad, key_low, preferred_element_type=wide) * scale
    )
    key_grad = (
        jnp.einsum("hts,thd->shd", scores_grad, query_low, preferred_element_type=wide) * scale
    )
    query_lin_grad = rotate_back(query_grad, cosine, sine).reshape(GROUP, heads * HD).astype(narrow)
    key_lin_grad = rotate_back(key_grad, cosine, sine).reshape(GROUP, heads * HD).astype(narrow)
    value_lin_grad = value_grad.reshape(GROUP, heads * HD).astype(narrow)
    norm_one_part = (
        dot_nt(query_lin_grad, q_weight)
        + dot_nt(key_lin_grad, k_weight)
        + dot_nt(value_lin_grad, v_weight)
    ).astype(narrow)
    normed_one_grad = plane_scatter(
        [norm_one_part[j * rows : (j + 1) * rows] for j in range(n_tensor)]
    )
    attn_gain_part = jnp.sum(normed_one_grad * hat_one, axis=0)
    scaled_one = normed_one_grad * attn_gain
    input_grad = hidden_grad + inverse_one * (
        scaled_one - hat_one * jnp.mean(scaled_one * hat_one, axis=1, keepdims=True)
    )

    width = heads * HD
    attn_grads = jnp.concatenate(
        [
            dot_tn(normed_one, query_lin_grad).astype(narrow),
            dot_tn(normed_one, key_lin_grad).astype(narrow),
            dot_tn(normed_one, value_lin_grad).astype(narrow),
            o_grad.astype(narrow),
        ],
        axis=1,
    )
    piece = D // n_dp
    attn_sum = ring_scatter(
        [
            tuple(lax.dynamic_slice_in_dim(attn_grads, s * piece, piece, 0) for s in pair)
            for pair in sources
        ]
    ).astype(narrow)
    attn_whole = jnp.zeros((D, 4 * width), narrow)
    for pair, at in zip(ring_gather(attn_sum), sources):
        for block, source in zip(pair, at):
            attn_whole = lax.dynamic_update_slice_in_dim(attn_whole, block, source * piece, 0)
    attn_whole = attn_whole.astype(wide)

    expert_down_grad = expert_sum(down_full)[None]
    expert_gate_grad = expert_sum(gate_full).T[None]
    expert_up_grad = expert_sum(up_full).T[None]

    bias_part = jnp.concatenate(
        [
            jnp.sum(query_lin_grad.astype(wide), axis=0),
            jnp.sum(key_lin_grad.astype(wide), axis=0),
            jnp.sum(value_lin_grad.astype(wide), axis=0),
        ]
    )
    bias_spread = lax.dynamic_update_slice_in_dim(
        jnp.zeros((n_tensor, 3 * width), wide), bias_part[None], slice_index, 0
    )
    small = lax.psum(
        jnp.concatenate(
            [
                attn_gain_part,
                mlp_gain_part,
                router_grad_part,
                jnp.broadcast_to(squared_own, (128,)),
                bias_spread.reshape(-1),
            ]
        ),
        ("dp", "tensor"),
    )
    attn_gain_grad, mlp_gain_grad, shared_router_grad = (small[i * D : (i + 1) * D] for i in range(3))
    teacher_loss = small[3 * D] / (valid_count * D)
    biases = lax.dynamic_index_in_dim(
        small[3 * D + 128 :].reshape(n_tensor, 3 * width), slice_index, 0, keepdims=False
    )
    return (
        result.astype(narrow),
        teacher_loss,
        input_grad,
        attn_gain_grad,
        attn_whole[:, :width],
        biases[:width],
        attn_whole[:, width : 2 * width],
        biases[width : 2 * width],
        attn_whole[:, 2 * width : 3 * width],
        biases[2 * width :],
        attn_whole[:, 3 * width :].T,
        mlp_gain_grad,
        expert_gate_grad,
        expert_up_grad,
        expert_down_grad,
        shared_gate_grad,
        shared_up_grad,
        shared_down_grad,
        shared_router_grad,
    )


def solution(mesh):
    return jax.shard_map(
        shards,
        mesh=mesh,
        in_specs=(
            P(("dp", "tensor"), None),
            P(),
            P(None, "tensor"),
            P("tensor"),
            P(None, "tensor"),
            P("tensor"),
            P(None, "tensor"),
            P("tensor"),
            P("tensor", None),
            P(),
            P("dp", None, "tensor"),
            P("dp", None, "tensor"),
            P("dp", "tensor", None),
            P(None, "tensor"),
            P(None, "tensor"),
            P("tensor", None),
            P(),
            P("dp", None),
            P("dp", None),
            P(),
            P(),
            P(("dp", "tensor"), None),
            P(("dp", "tensor"), None),
        ),
        out_specs=(
            P(("dp", "tensor"), None),
            P(),
            P(("dp", "tensor"), None),
            P(),
            P(None, "tensor"),
            P("tensor"),
            P(None, "tensor"),
            P("tensor"),
            P(None, "tensor"),
            P("tensor"),
            P("tensor", None),
            P(),
            P("dp", None, "tensor"),
            P("dp", None, "tensor"),
            P("dp", "tensor", None),
            P(None, "tensor"),
            P(None, "tensor"),
            P("tensor", None),
            P(),
        ),
        check_vma=False,
    )
```

```python
import functools
import math

import jax
import jax.numpy as jnp
from jax import lax
from jax.experimental import pallas as pl
from jax.experimental.pallas import tpu as pltpu
from jax.sharding import PartitionSpec as P

D = 2048
HD = 128
PROMPT = 512
SLOT = 128
CONTS = 2
GROUP = 768


EPSILON = 1e-06
ROTARY_BASE = 1000000.0
WIDE = jnp.float32
NARROW = jnp.bfloat16
VMEM_BYTES = 60 * 1024 * 1024


def slot_layout(lengths_row, position):
    offset = jnp.maximum(position - PROMPT, 0)
    in_prompt = position < PROMPT
    segment = jnp.where(in_prompt, 0, 1 + offset // SLOT)
    rotary_place = jnp.where(in_prompt, position, PROMPT + offset % SLOT)
    matches = segment[:, None] - 1 == jnp.arange(CONTS, dtype=jnp.int32)[None, :]
    length_here = jnp.sum(jnp.where(matches, lengths_row[None, :], 0), axis=1)
    living = in_prompt | (offset % SLOT < length_here)
    return (segment, rotary_place, living)


def visible_keys(position, segment, living):
    causal = position[None, :] <= position[:, None]
    same_part = (segment[None, :] == segment[:, None]) | (segment[None, :] == 0)
    return causal & same_part & living[None, :]


def rotary_tables(rotary_place):
    freqs = jnp.exp(jnp.arange(HD // 2, dtype=jnp.float32) * (-2.0 * math.log(ROTARY_BASE) / HD))
    angles = rotary_place.astype(jnp.float32)[:, None] * freqs[None, :]
    angles = jnp.concatenate([angles, angles], axis=1)
    return (jnp.cos(angles), jnp.sin(angles))


def rotate(values, cosine, sine):
    half = values.shape[-1] // 2
    flipped = jnp.concatenate([-values[..., half:], values[..., :half]], axis=-1)
    return values * cosine[:, None, :] + flipped * sine[:, None, :]


def rotate_back(grads, cosine, sine):
    half = grads.shape[-1] // 2
    turned = grads * sine[:, None, :]
    flipped = jnp.concatenate([turned[..., half:], -turned[..., :half]], axis=-1)
    return grads * cosine[:, None, :] + flipped


def attention_scores(query_low, key_low, visible, scale):
    scores = (
        jnp.einsum("thd,shd->hts", query_low, key_low, preferred_element_type=jnp.float32) * scale
    )
    return jnp.where(visible[None], scores, -1e30)


def dot_nt(left, right):
    return lax.dot_general(left, right, (((1,), (1,)), ((), ())), preferred_element_type=WIDE)


def dot_nn(left, right):
    return lax.dot_general(left, right, (((1,), (0,)), ((), ())), preferred_element_type=WIDE)


def dot_tn(left, right):
    return lax.dot_general(left, right, (((0,), (0,)), ((), ())), preferred_element_type=WIDE)


def after(value, *others):
    return lax.optimization_barrier((value,) + others)[0]


def flip(value, bit):
    size = lax.axis_size("tensor")
    return lax.ppermute(value, "tensor", [(i, i ^ bit) for i in range(size)])


def split_at(rows):
    return rows // 32 * 16


def plane_gather(value):
    size = lax.axis_size("tensor")
    if size == 4:
        cut = split_at(value.shape[0])
        one, two = flip(value, 1), flip(value, 2)
        low, high = flip(two[:cut], 1), flip(one[cut:], 2)
        return [value, one, two, jnp.concatenate([low, high], axis=0)]
    blocks, bit = [value], 1
    while bit < size:
        blocks = blocks + [flip(block, bit) for block in blocks]
        bit *= 2
    return blocks


def plane_scatter(parts):
    size = lax.axis_size("tensor")
    if size == 4:
        cut = split_at(parts[3].shape[0])
        far = parts[3].astype(NARROW)
        low, high = flip(far[:cut], 1), flip(far[cut:], 2)
        two = jnp.concatenate(
            [(parts[2][:cut].astype(WIDE) + low.astype(WIDE)).astype(NARROW), parts[2][cut:].astype(NARROW)], axis=0
        )
        one = jnp.concatenate(
            [parts[1][:cut].astype(NARROW), (parts[1][cut:].astype(WIDE) + high.astype(WIDE)).astype(NARROW)], axis=0
        )
        return parts[0].astype(WIDE) + flip(one, 1).astype(WIDE) + flip(two, 2).astype(WIDE)
    parts = [part.astype(WIDE) for part in parts]
    bit = size // 2
    while bit >= 1:
        parts = [parts[j] + flip(parts[bit + j].astype(NARROW), bit).astype(WIDE) for j in range(bit)]
        bit //= 2
    return parts[0]


def ring_order(chips):
    odd = list(range(1, chips, 2))
    even = list(range(2, chips, 2))
    return [0] + odd + even[::-1]


def ring_next(value):
    chips = lax.axis_size("dp") // 2
    order = ring_order(chips)
    pairs = [
        (2 * order[i] + c, 2 * order[(i + 1) % chips] + c) for i in range(chips) for c in range(2)
    ]
    return lax.ppermute(value, "dp", pairs)


def swap_core(value):
    size = lax.axis_size("dp")
    return lax.ppermute(value, "dp", [(i, i ^ 1) for i in range(size)])


def ring_chips():
    chips = lax.axis_size("dp") // 2
    order = ring_order(chips)
    chip = lax.axis_index("dp") // 2
    sources = []
    for step in range(chips):
        table = [0] * chips
        for place, here in enumerate(order):
            table[here] = order[(place - step) % chips]
        sources.append(jnp.asarray(table, jnp.int32)[chip])
    return sources


def ring_sources():
    core = lax.axis_index("dp") % 2
    return [(2 * chip + core, 2 * chip + 1 - core) for chip in ring_chips()]


def ring_gather(value):
    chips = lax.axis_size("dp") // 2
    held = [value]
    for _ in range(chips - 1):
        held.append(ring_next(held[-1]))
    return [(block, swap_core(block)) for block in held]


def ring_scatter(parts):
    chips = len(parts)
    total = None
    for step in list(range(1, chips)) + [0]:
        mine, other = parts[step]
        here = mine.astype(WIDE) + swap_core(other.astype(NARROW)).astype(WIDE)
        if total is not None:
            here = here + total.astype(WIDE)
        if step == 0:
            return here
        total = ring_next(here.astype(NARROW))


def plane_bits():
    size = lax.axis_size("tensor")
    bits = [1 << i for i in range(size.bit_length() - 1)]
    return bits[:1] + bits[2:], bits[1:2]


def bits_gather(value, bits):
    blocks = [value]
    for bit in bits:
        blocks = blocks + [flip(block, bit) for block in blocks]
    return blocks


def bits_scatter(parts, bits):
    for bit in bits[::-1]:
        half = len(parts) // 2
        parts = [
            parts[j].astype(WIDE) + flip(parts[half + j].astype(NARROW), bit).astype(WIDE)
            for j in range(half)
        ]
    return parts[0]


def bits_offsets(bits):
    offsets = [0]
    for bit in bits:
        offsets = offsets + [offset ^ bit for offset in offsets]
    return offsets


def chain_gather(value):
    held = [value]
    for _ in range(lax.axis_size("dp") // 2 - 1):
        held.append(ring_next(held[-1]))
    return held


def chain_scatter(parts):
    total = None
    for step in list(range(1, len(parts))) + [0]:
        here = parts[step].astype(WIDE)
        if total is not None:
            here = here + total.astype(WIDE)
        if step == 0:
            return here
        total = ring_next(here.astype(NARROW))


def sum_over_dp(vector):
    both = vector + swap_core(vector)
    chips = lax.axis_size("dp") // 2
    held = [both]
    for _ in range(chips - 1):
        held.append(ring_next(held[-1]))
    stacked = jnp.stack(held)
    places = jnp.stack(ring_chips())
    ordered = [
        jnp.sum(jnp.where((places == chip)[:, None], stacked, 0.0), axis=0) for chip in range(chips)
    ]
    return sum(ordered[1:], ordered[0])


def sum_over_plane(vector):
    bit = 1
    while bit < lax.axis_size("tensor"):
        vector = vector + flip(vector, bit)
        bit *= 2
    return vector


class Copies:
    def __init__(self, sems):
        self.sems, self.used = sems, 0

    def start(self, source, target):
        copy = pltpu.make_async_copy(source, target, self.sems.at[self.used])
        self.used += 1
        copy.start()
        return copy


def weight_places(parts, count, cut):
    half = count // 2
    left = parts - cut
    chunks = [
        [(b, 0, cut, b * cut) for b in range(half)],
        [(b, 0, cut, (b - half) * cut) for b in range(half, count)],
        [(b, cut, left, b * left) for b in range(count)],
    ]
    sizes = [half * cut, half * cut, count * left]
    starts = [0, half * cut, count * cut]
    return [
        (start, size, [(b, at, n, start + place) for b, at, n, place in chunk])
        for start, size, chunk in zip(starts, sizes, chunks)
    ]


def forward_body(rows, count, places, blocks, *refs):
    x_refs, refs = refs[:count], refs[count:]
    weights, refs = [refs[n * blocks : (n + 1) * blocks] for n in range(3)], refs[3 * blocks :]
    mix_one, mix_two, router = refs[:3]
    out_refs, refs = refs[3 : 3 + count], refs[3 + count :]
    gate_ref, up_ref, hidden_ref, factor_ref = refs[:4]
    xs, gate_s, up_s, down_s, ys, gs, us, hs, sems = refs[4:]
    copies = Copies(sems)
    x_in = [copies.start(x_refs[i], xs.at[pl.ds(i * rows, rows)]) for i in range(count)]
    w_in = [
        [
            [
                copies.start(weights[n][b].at[pl.ds(at, size)], held.at[pl.ds(place, size)])
                for b, at, size, place in pieces
            ]
            for n, held in enumerate((gate_s, up_s, down_s))
        ]
        for _, _, pieces in places
    ]
    for copy in x_in:
        copy.wait()
    x = xs[...]
    router_gate = jax.nn.sigmoid(jnp.sum(x.astype(WIDE) * router[...], axis=1, keepdims=True))
    factor_ref[...] = router_gate
    total, away = None, []
    for (start, size, _), arriving, factor in zip(
        places, w_in, (mix_one[...], mix_two[...], router_gate)
    ):
        span = pl.ds(start, size)
        for copy in arriving[0]:
            copy.wait()
        gate_in = dot_nt(x, gate_s[span])
        for copy in arriving[1]:
            copy.wait()
        up_in = dot_nt(x, up_s[span])
        hidden = (gate_in * jax.nn.sigmoid(gate_in) * up_in * factor).astype(NARROW)
        gs[:, start : start + size] = gate_in.astype(NARROW)
        us[:, start : start + size] = up_in.astype(NARROW)
        hs[:, start : start + size] = hidden
        for copy in arriving[2]:
            copy.wait()
        part = dot_nn(hidden, down_s[span])
        total = part if total is None else total + part
    ys[...] = total.astype(NARROW)
    away = [copies.start(ys.at[pl.ds(i * rows, rows)], out_refs[i]) for i in range(count)]
    away += [copies.start(gs, gate_ref), copies.start(us, up_ref), copies.start(hs, hidden_ref)]
    for copy in away:
        copy.wait()


def forward_step(x_blocks, weights, mix_one, mix_two, router, cut):
    count, (rows, width) = len(x_blocks), x_blocks[0].shape
    blocks, parts = len(weights[0]), weights[0][0].shape[0]
    places = weight_places(parts, blocks, cut)
    total, hidden = count * rows, blocks * parts
    anywhere, local = pl.BlockSpec(memory_space=pl.ANY), pl.BlockSpec(memory_space=pltpu.VMEM)
    shape = jax.ShapeDtypeStruct
    outs = pl.pallas_call(
        functools.partial(forward_body, rows, count, places, blocks),
        out_shape=[shape((rows, width), NARROW)] * count
        + [shape((total, hidden), NARROW)] * 3
        + [shape((total, 1), WIDE)],
        in_specs=[anywhere] * (count + 3 * blocks) + [local] * 3,
        out_specs=[anywhere] * (count + 3) + [local],
        scratch_shapes=[pltpu.VMEM((total, width), NARROW)]
        + [pltpu.VMEM((hidden, width), NARROW)] * 3
        + [pltpu.VMEM((total, width), NARROW)]
        + [pltpu.VMEM((total, hidden), NARROW)] * 3
        + [pltpu.SemaphoreType.DMA((2 * count + 6 * blocks + 3,))],
        compiler_params=pltpu.CompilerParams(vmem_limit_bytes=VMEM_BYTES),
        cost_estimate=pl.CostEstimate(
            flops=6 * total * hidden * width,
            bytes_accessed=6 * hidden * width + 4 * total * width + 6 * total * hidden,
            transcendentals=total * hidden,
        ),
        name="ffn_forward",
    )(*x_blocks, *[w for held in weights for w in held], mix_one, mix_two, router)
    return outs[:count], outs[count], outs[count + 1], outs[count + 2], outs[count + 3]


def backward_body(rows, count, places, blocks, *refs):
    g_refs, refs = refs[:count], refs[count:]
    weights, refs = [refs[n * blocks : (n + 1) * blocks] for n in range(3)], refs[3 * blocks :]
    (gate_ref, up_ref, mix_one, mix_two, rg, router), refs = refs[:6], refs[6:]
    out_refs, refs = refs[:count], refs[count:]
    gate_out, up_out, logit_ref = refs[:3]
    xs, gate_s, up_s, down_s, ys, gs, us, sems = refs[3:]
    copies = Copies(sems)
    g_in = [copies.start(g_refs[i], xs.at[pl.ds(i * rows, rows)]) for i in range(count)]
    w_in, kept = [], []
    for start, size, pieces in places:
        arriving = [
            [
                copies.start(weights[n][b].at[pl.ds(at, n_rows)], held.at[pl.ds(place, n_rows)])
                for b, at, n_rows, place in pieces
            ]
            for n, held in ((2, down_s), (0, gate_s), (1, up_s))
        ]
        w_in.append(arriving)
        if not kept:
            kept = [copies.start(gate_ref, gs), copies.start(up_ref, us)]
    for copy in g_in:
        copy.wait()
    grad = xs[...]
    total = None
    for (start, size, _), arriving, factor in zip(
        places, w_in, (mix_one[...], mix_two[...], rg[...])
    ):
        span = pl.ds(start, size)
        for copy in arriving[0]:
            copy.wait()
        grad_hidden = dot_nt(grad, down_s[span]) * factor
        if total is None:
            for copy in kept:
                copy.wait()
        gate_in = gs[:, start : start + size].astype(WIDE)
        up_in = us[:, start : start + size].astype(WIDE)
        squash = jax.nn.sigmoid(gate_in)
        up_grad = grad_hidden * gate_in * squash
        gate_grad = grad_hidden * up_in * squash * (1.0 + gate_in * (1.0 - squash))
        logit = jnp.sum(up_grad * up_in, axis=1, keepdims=True)
        gate_grad, up_grad = gate_grad.astype(NARROW), up_grad.astype(NARROW)
        gs[:, start : start + size] = gate_grad
        us[:, start : start + size] = up_grad
        for copy in arriving[1] + arriving[2]:
            copy.wait()
        part = dot_nn(gate_grad, gate_s[span]) + dot_nn(up_grad, up_s[span])
        total = part if total is None else total + part
    logit = logit * (1.0 - rg[...])
    logit_ref[...] = logit
    ys[...] = (total + logit * router[...]).astype(NARROW)
    away = [copies.start(ys.at[pl.ds(i * rows, rows)], out_refs[i]) for i in range(count)]
    away += [copies.start(gs, gate_out), copies.start(us, up_out)]
    for copy in away:
        copy.wait()


def backward_step(g_blocks, weights, gate_in, up_in, mix_one, mix_two, rg, router, cut):
    count, (rows, width) = len(g_blocks), g_blocks[0].shape
    blocks, parts = len(weights[0]), weights[0][0].shape[0]
    places = weight_places(parts, blocks, cut)
    total, hidden = count * rows, blocks * parts
    anywhere, local = pl.BlockSpec(memory_space=pl.ANY), pl.BlockSpec(memory_space=pltpu.VMEM)
    shape = jax.ShapeDtypeStruct
    outs = pl.pallas_call(
        functools.partial(backward_body, rows, count, places, blocks),
        out_shape=[shape((rows, width), NARROW)] * count
        + [shape((total, hidden), NARROW)] * 2
        + [shape((total, 1), WIDE)],
        in_specs=[anywhere] * (count + 3 * blocks + 2) + [local] * 4,
        out_specs=[anywhere] * (count + 2) + [local],
        scratch_shapes=[pltpu.VMEM((total, width), NARROW)]
        + [pltpu.VMEM((hidden, width), NARROW)] * 3
        + [pltpu.VMEM((total, width), NARROW)]
        + [pltpu.VMEM((total, hidden), NARROW)] * 2
        + [pltpu.SemaphoreType.DMA((2 * count + 6 * blocks + 4,))],
        compiler_params=pltpu.CompilerParams(vmem_limit_bytes=VMEM_BYTES),
        cost_estimate=pl.CostEstimate(
            flops=6 * total * hidden * width,
            bytes_accessed=6 * hidden * width + 4 * total * width + 8 * total * hidden,
            transcendentals=total * hidden,
        ),
        name="ffn_backward",
    )(
        *g_blocks,
        *[w for held in weights for w in held],
        gate_in,
        up_in,
        mix_one,
        mix_two,
        rg,
        router,
    )
    return outs[:count], outs[count], outs[count + 1], outs[count + 2]


def weight_body(rows, steps, blocks, places, tiles, parts, *refs):
    x_refs, refs = refs[: steps * blocks], refs[steps * blocks :]
    left_refs, refs = refs[:steps], refs[steps:]
    mine_ref, other_ref, xs, ls, os, sems = refs
    copies = Copies(sems)
    part = blocks * rows
    arrived = []
    for s in range(steps):
        for i in range(blocks):
            place = pl.ds((s * blocks + i) * rows, rows)
            arrived.append(copies.start(x_refs[s * blocks + i], xs.at[place]))
        arrived.append(copies.start(left_refs[s], ls.at[pl.ds(s * part, part)]))
    for copy in arrived:
        copy.wait()
    moves = [
        (place, n_rows, b, at)
        for _, _, chunk in places
        for b, at, n_rows, place in chunk
    ]
    half = (1 + max(b for _, _, b, _ in moves)) // 2
    away, ready = [], 0
    for start, size in tiles:
        os[pl.ds(start, size)] = dot_tn(ls[:, start : start + size], xs[...]).astype(NARROW)
        for at, n_rows, b, offset in moves:
            if ready < at + n_rows <= start + size:
                target = mine_ref if b < half else other_ref
                goal = target.at[pl.ds((b % half) * parts + offset, n_rows)]
                away.append(copies.start(os.at[pl.ds(at, n_rows)], goal))
        ready = start + size
    for copy in away:
        copy.wait()


def weight_grads(x_blocks, lefts, parts, cut, blocks_of):
    steps, blocks = len(x_blocks), len(x_blocks[0])
    rows, width = x_blocks[0][0].shape
    total, hidden = steps * blocks * rows, lefts[0].shape[1]
    places = weight_places(parts, blocks_of, cut)
    tiles = [(at, min(512, hidden - at)) for at in range(0, hidden, 512)]
    anywhere = pl.BlockSpec(memory_space=pl.ANY)
    return pl.pallas_call(
        functools.partial(weight_body, rows, steps, blocks, places, tiles, parts),
        out_shape=[jax.ShapeDtypeStruct((hidden // 2, width), NARROW)] * 2,
        in_specs=[anywhere] * (steps * (blocks + 1)),
        out_specs=[anywhere] * 2,
        scratch_shapes=[
            pltpu.VMEM((total, width), NARROW),
            pltpu.VMEM((total, hidden), NARROW),
            pltpu.VMEM((hidden, width), NARROW),
            pltpu.SemaphoreType.DMA((steps * (blocks + 1) + 2 * blocks_of,)),
        ],
        compiler_params=pltpu.CompilerParams(vmem_limit_bytes=VMEM_BYTES),
        cost_estimate=pl.CostEstimate(
            flops=2 * total * hidden * width,
            bytes_accessed=2 * total * width + 2 * (total + width) * hidden,
            transcendentals=0,
        ),
        name="weight_grads",
    )(*[b for step in x_blocks for b in step], *lefts)


def assemble_body(count, splits, *refs):
    places, blocks, outs = refs[0], refs[1 : 1 + count], refs[1 + count : 1 + count + splits]
    held, sems = refs[1 + count + splits :]
    rows = blocks[0].shape[0]
    copies = Copies(sems)
    moved = []
    for i in range(count):
        place = pl.multiple_of(places[i], rows)
        moved.append(copies.start(blocks[i], held.at[pl.ds(place, rows)]))
    for copy in moved:
        copy.wait()
    width = held.shape[1] // splits
    for j in range(splits):
        outs[j][...] = held[:, j * width : (j + 1) * width].astype(WIDE)


def assemble(blocks, places, splits):
    count, (rows, width) = len(blocks), blocks[0].shape
    shape = jax.ShapeDtypeStruct((count * rows, width // splits), WIDE)
    local = pl.BlockSpec(memory_space=pltpu.VMEM)
    return pl.pallas_call(
        functools.partial(assemble_body, count, splits),
        out_shape=[shape] * splits,
        in_specs=[pl.BlockSpec(memory_space=pltpu.SMEM)]
        + [pl.BlockSpec(memory_space=pl.ANY)] * count,
        out_specs=[local] * splits,
        scratch_shapes=[
            pltpu.VMEM((count * rows, width), NARROW),
            pltpu.SemaphoreType.DMA((count,)),
        ],
        compiler_params=pltpu.CompilerParams(vmem_limit_bytes=VMEM_BYTES),
        name="assemble",
    )(places, *blocks)


def turn_body(x_ref, out_ref):
    out_ref[...] = x_ref[...].astype(WIDE).T


def turn(value):
    rows, width = value.shape
    if rows % 128:
        return value.T.astype(WIDE)
    return pl.pallas_call(
        turn_body,
        grid=(width // 256,),
        out_shape=jax.ShapeDtypeStruct((width, rows), WIDE),
        in_specs=[pl.BlockSpec((rows, 256), lambda i: (0, i))],
        out_specs=pl.BlockSpec((256, rows), lambda i: (i, 0)),
        compiler_params=pltpu.CompilerParams(vmem_limit_bytes=VMEM_BYTES),
        name="turn",
    )(value)


def shards(
    hidden_in,
    attn_gain,
    q_weight,
    q_bias,
    k_weight,
    k_bias,
    v_weight,
    v_bias,
    o_weight,
    mlp_gain,
    expert_gate,
    expert_up,
    expert_down,
    shared_gate,
    shared_up,
    shared_down,
    shared_router,
    routes,
    gate_weights,
    lengths,
    loss_mask,
    teacher,
    cotangent,
):
    wide = WIDE
    narrow = NARROW
    data_index = lax.axis_index("dp")
    slice_index = lax.axis_index("tensor")
    n_dp = lax.axis_size("dp")
    n_tensor = lax.axis_size("tensor")
    rows = hidden_in.shape[0]
    heads = q_weight.shape[1] // HD
    f_expert = expert_gate.shape[2]
    f_shared = shared_gate.shape[1] // n_dp
    f_pad = -(-f_shared // 16) * 16
    scale = 1.0 / math.sqrt(HD)

    position = jnp.concatenate(
        [(slice_index ^ j) * rows + jnp.arange(rows, dtype=jnp.int32) for j in range(n_tensor)]
    )
    own_lengths = lax.dynamic_index_in_dim(lengths, data_index, 0, keepdims=False)
    segment, rotary_place, living = slot_layout(own_lengths, position)
    visible = visible_keys(position, segment, living)
    cosine, sine = rotary_tables(rotary_place)
    every = jnp.arange(GROUP, dtype=jnp.int32)
    living_all = jax.vmap(lambda row: slot_layout(row, every)[2])(lengths)
    valid_count = jnp.sum((living_all.reshape(-1) & (loss_mask == 1)).astype(wide))
    own_mask = lax.dynamic_slice_in_dim(loss_mask, data_index * GROUP + slice_index * rows, rows, 0)
    valid_own = living[:rows] & (own_mask == 1)

    own_input = hidden_in.astype(wide)
    inverse_one = lax.rsqrt(jnp.mean(own_input * own_input, axis=1, keepdims=True) + EPSILON)
    hat_one = own_input * inverse_one
    normed_one_blocks = plane_gather((hat_one * attn_gain).astype(narrow))
    normed_one = jnp.concatenate(normed_one_blocks, axis=0)

    def pack(expert_rows, shared_rows):
        if f_pad != f_shared:
            shared_rows = jnp.pad(shared_rows, ((0, f_pad - f_shared), (0, 0)))
        return jnp.concatenate([expert_rows, shared_rows], axis=0)

    shared_at = data_index * f_shared
    own_gate = pack(
        expert_gate[0].T, lax.dynamic_slice_in_dim(shared_gate, shared_at, f_shared, 1).T
    )
    own_up = pack(expert_up[0].T, lax.dynamic_slice_in_dim(shared_up, shared_at, f_shared, 1).T)
    own_down = pack(expert_down[0], lax.dynamic_slice_in_dim(shared_down, shared_at, f_shared, 0))

    w_bits, r_bits = plane_bits()

    def both_cores(blocks):
        return blocks + [swap_core(block) for block in blocks]

    own_gate, own_up, normed_one = lax.optimization_barrier((own_gate, own_up, normed_one))
    gate_blocks = bits_gather(own_gate, w_bits)
    up_blocks = bits_gather(own_up, w_bits)

    row_slices = [slice_index ^ offset for offset in bits_offsets(r_bits)]
    mixing = jnp.sum(
        jnp.where(
            routes[None, :, :] == jnp.arange(n_dp, dtype=jnp.int32)[:, None, None],
            gate_weights[None, :, :],
            0.0,
        ),
        axis=2,
    )
    mixing = after(mixing, normed_one_blocks[-1])
    mixing_all = jnp.stack(chain_gather(mixing))
    experts = jnp.arange(n_dp, dtype=jnp.int32)
    slices = jnp.arange(n_tensor, dtype=jnp.int32)

    def mixing_of(expert):
        chosen = jnp.sum(
            jnp.where((experts == expert)[None, :, None], mixing_all, 0.0), axis=1
        ).reshape(-1, n_tensor, rows)
        chosen = jnp.stack(
            [jnp.sum(jnp.where((slices == at)[None, :, None], chosen, 0.0), axis=1) for at in row_slices],
            axis=1,
        )
        return chosen.reshape(-1, len(row_slices) * rows, 1)

    mix_one, mix_two = mixing_of(data_index), mixing_of(data_index ^ 1)

    query_lin = dot_nn(normed_one, q_weight) + q_bias
    key_lin = dot_nn(normed_one, k_weight) + k_bias
    value_low = (dot_nn(normed_one, v_weight) + v_bias).astype(narrow).reshape(GROUP, heads, HD)
    query_low = rotate(query_lin.reshape(GROUP, heads, HD), cosine, sine).astype(narrow)
    key_low = rotate(key_lin.reshape(GROUP, heads, HD), cosine, sine).astype(narrow)
    scores = attention_scores(query_low, key_low, visible, scale)
    top_score = jnp.max(scores, axis=2, keepdims=True)
    expo = jnp.exp(scores - top_score)
    total_expo = jnp.sum(expo, axis=2, keepdims=True)
    log_total = top_score + jnp.log(total_expo)
    probs_low = (expo / total_expo).astype(narrow)
    mixed = jnp.einsum("hts,shd->thd", probs_low, value_low, preferred_element_type=wide)
    mixed_low = mixed.reshape(GROUP, heads * HD).astype(narrow)
    mixed_low = after(mixed_low, *gate_blocks, *up_blocks)
    head_part = dot_nn(mixed_low, o_weight).astype(narrow)
    attn_own = plane_scatter([head_part[j * rows : (j + 1) * rows] for j in range(n_tensor)])

    attn_own, own_down = lax.optimization_barrier((attn_own, own_down))
    down_blocks = bits_gather(own_down, w_bits)
    hidden_mid = own_input + attn_own
    inverse_two = lax.rsqrt(jnp.mean(hidden_mid * hidden_mid, axis=1, keepdims=True) + EPSILON)
    hat_two = hidden_mid * inverse_two
    normed_two = (hat_two * mlp_gain).astype(narrow)

    weights = [both_cores(blocks) for blocks in (gate_blocks, up_blocks, down_blocks)]
    n_blocks, n_hidden = len(weights[0]), len(weights[0]) // 2
    places = weight_places(f_expert + f_shared, n_blocks, f_expert)

    router_row = shared_router.astype(wide)[None]
    x_chain = chain_gather(normed_two)
    chips = len(x_chain)
    x_steps = [bits_gather(block, r_bits) for block in x_chain]
    forward, out_sums, total = {}, {}, None
    order = list(range(1, chips)) + [0]
    for place, step in enumerate(order):
        x, ready = x_steps[step], []
        if place == 0:
            ready = [x_chain[order[1]], *x_steps[0]]
        if place >= 1:
            ready = list(forward[order[place - 1]][0])
            ready += x_steps[order[min(place + 1, chips - 1)]]
        if place >= 2:
            done = order[place - 2]
            out_sums[done] = bits_scatter(forward[done][0], r_bits)
            ready.append(out_sums[done])
            if total is not None:
                ready.append(total)
        x = list(lax.optimization_barrier((*x, *ready)))
        if place >= 2:
            kept = x[len(x) - (2 if total is not None else 1) :]
            here = kept[0].astype(wide)
            if total is not None:
                here = here + kept[1].astype(wide)
            total = ring_next(here.astype(narrow))
        x = x[: len(x_steps[step])]
        forward[step] = forward_step(
            x, weights, mix_one[step], mix_two[step], router_row, f_expert
        )
    for done in order[-2:]:
        out_sums[done] = bits_scatter(forward[done][0], r_bits)
    total = ring_next((out_sums[order[-2]].astype(wide) + total.astype(wide)).astype(narrow))
    branch_own = out_sums[0].astype(wide) + total.astype(wide)
    result = hidden_mid + branch_own

    difference = result - teacher.astype(wide)
    squared_own = jnp.sum(jnp.where(valid_own[:, None], difference * difference, 0.0))
    result_grad = cotangent.astype(wide) + jnp.where(
        valid_own[:, None], difference * (2.0 / (valid_count * D)), 0.0
    )
    grad_own = result_grad.astype(narrow)

    g_chain = chain_gather(grad_own)
    g_steps = [bits_gather(block, r_bits) for block in g_chain]
    backward, dx_sums, total = [], {}, None
    for step in range(chips):
        g, ready = g_steps[step], []
        if step + 1 < chips:
            ready.append(g_chain[step + 1])
        if step >= 1:
            ready += list(backward[step - 1][0])
        if step >= 2:
            dx_sums[step - 2] = bits_scatter(backward[step - 2][0], r_bits)
            ready.append(dx_sums[step - 2])
        flat = list(lax.optimization_barrier((*g, *ready)))
        if step >= 2:
            dx_sums[step - 2] = flat[-1]
        backward.append(
            backward_step(
                flat[: len(g)],
                weights,
                forward[step][1],
                forward[step][2],
                mix_one[step],
                mix_two[step],
                forward[step][4],
                router_row,
                f_expert,
            )
        )
    gate_grads = [item[1] for item in backward]
    up_grads = [item[2] for item in backward]
    hidden_steps = [forward[step][3] for step in range(chips)]

    def core_sum(mine, other):
        return (mine.astype(wide) + swap_core(other).astype(wide)).astype(narrow)

    def shared_part(both):
        size = f_expert + f_pad
        own = bits_scatter(
            [both[j * size + f_expert : (j + 1) * size] for j in range(n_hidden)], w_bits
        )
        return own[:f_shared].astype(narrow)

    def expert_part(both):
        size = f_expert + f_pad
        return bits_scatter([both[j * size : j * size + f_expert] for j in range(n_hidden)], w_bits)

    def held_until(steps, *others):
        count = len(steps[0])
        flat = lax.optimization_barrier((*[b for blocks in steps for b in blocks], *others))
        blocks = flat[: count * len(steps)]
        held = [list(blocks[i * count : (i + 1) * count]) for i in range(len(steps))]
        return held, flat[count * len(steps) :]

    total = None
    for step in range(1, chips - 2):
        here = dx_sums[step].astype(wide)
        total = ring_next((here if total is None else here + total.astype(wide)).astype(narrow))
    dx_sums[chips - 2] = bits_scatter(backward[chips - 2][0], r_bits)
    held, (dx_sums[chips - 2], total, *_) = held_until(
        g_steps, dx_sums[chips - 2], total, *backward[-1][0]
    )
    down_full = weight_grads(held, hidden_steps, f_expert + f_pad, f_expert, n_blocks)
    total = ring_next((dx_sums[chips - 2].astype(wide) + total.astype(wide)).astype(narrow))
    dx_sums[chips - 1] = bits_scatter(backward[chips - 1][0], r_bits)
    held, (dx_sums[chips - 1], total, *down_full) = held_until(
        x_steps, dx_sums[chips - 1], total, *down_full
    )
    gate_full = weight_grads(held, gate_grads, f_expert + f_pad, f_expert, n_blocks)
    total = ring_next((dx_sums[chips - 1].astype(wide) + total.astype(wide)).astype(narrow))
    normed_two_grad = dx_sums[0].astype(wide) + total.astype(wide)
    down_both = core_sum(*down_full)
    held, (normed_two_grad, down_both, *gate_full) = held_until(
        x_steps, normed_two_grad, down_both, *gate_full
    )
    up_full = weight_grads(held, up_grads, f_expert + f_pad, f_expert, n_blocks)

    grad_wide = grad_own.astype(wide)
    mlp_gain_part = jnp.sum(normed_two_grad * hat_two, axis=0)
    scaled_two = normed_two_grad * mlp_gain
    hidden_grad = grad_wide + inverse_two * (
        scaled_two - hat_two * jnp.mean(scaled_two * hat_two, axis=1, keepdims=True)
    )
    router_grad_part = sum(
        jnp.sum(backward[step][3][i * rows : (i + 1) * rows] * block.astype(wide), axis=0)
        for step in range(chips)
        for i, block in enumerate(x_steps[step])
    )
    own_low = hidden_grad.astype(narrow)
    if n_tensor == 4:
        cut = split_at(rows)
        one, two = flip(own_low, 1), flip(own_low, 2)
        one, two, down_both, *up_full = lax.optimization_barrier((one, two, down_both, *up_full))
        low, high = flip(two[:cut], 1), flip(one[cut:], 2)
        shared_down_own = shared_part(down_both)
        grad_blocks = [own_low, one, two, low, high]
    else:
        shared_down_own = shared_part(down_both)
        grad_blocks = plane_gather(own_low)
    hidden_grad_low = jnp.concatenate(grad_blocks, axis=0)
    gate_both = core_sum(*gate_full)
    hidden_grad_low, shared_down_own, gate_both = lax.optimization_barrier(
        (hidden_grad_low, shared_down_own, gate_both)
    )
    shared_down_all = lax.all_gather(shared_down_own, "dp", axis=0, tiled=True)
    shared_gate_own = shared_part(gate_both)
    up_both = core_sum(*up_full)

    o_grad = dot_tn(mixed_low, hidden_grad_low)
    o_grad, shared_gate_own, up_both = lax.optimization_barrier((o_grad, shared_gate_own, up_both))
    shared_gate_all = lax.all_gather(shared_gate_own, "dp", axis=0, tiled=True)
    shared_up_own = shared_part(up_both)
    mixed_grad = dot_nt(hidden_grad_low, o_weight).astype(narrow).reshape(GROUP, heads, HD)
    scores_again = attention_scores(query_low, key_low, visible, scale)
    probs = jnp.exp(scores_again - log_total)
    probs_grad = jnp.einsum("thd,shd->hts", mixed_grad, value_low, preferred_element_type=wide)
    value_grad = jnp.einsum(
        "hts,thd->shd", probs.astype(narrow), mixed_grad, preferred_element_type=wide
    )
    inner = jnp.sum(probs * probs_grad, axis=2, keepdims=True)
    scores_grad = (probs * (probs_grad - inner)).astype(narrow)
    query_grad = (
        jnp.einsum("hts,shd->thd", scores_grad, key_low, preferred_element_type=wide) * scale
    )
    key_grad = (
        jnp.einsum("hts,thd->shd", scores_grad, query_low, preferred_element_type=wide) * scale
    )
    query_lin_grad = rotate_back(query_grad, cosine, sine).reshape(GROUP, heads * HD).astype(narrow)
    key_lin_grad = rotate_back(key_grad, cosine, sine).reshape(GROUP, heads * HD).astype(narrow)
    value_lin_grad = value_grad.reshape(GROUP, heads * HD).astype(narrow)
    expert_gate_own, expert_up_own, expert_down_own = (
        expert_part(both) for both in (gate_both, up_both, down_both)
    )
    expert_down_grad = expert_down_own[None]
    expert_gate_grad = expert_gate_own.T[None]
    expert_up_grad = expert_up_own.T[None]
    query_lin_grad, shared_up_own, _ = lax.optimization_barrier(
        (query_lin_grad, shared_up_own, expert_down_own)
    )
    shared_up_all = lax.all_gather(shared_up_own, "dp", axis=0, tiled=True)
    norm_one_part = (
        dot_nt(query_lin_grad, q_weight)
        + dot_nt(key_lin_grad, k_weight)
        + dot_nt(value_lin_grad, v_weight)
    ).astype(narrow)
    normed_one_grad = plane_scatter(
        [norm_one_part[j * rows : (j + 1) * rows] for j in range(n_tensor)]
    )
    attn_gain_part = jnp.sum(normed_one_grad * hat_one, axis=0)
    scaled_one = normed_one_grad * attn_gain
    input_grad = hidden_grad + inverse_one * (
        scaled_one - hat_one * jnp.mean(scaled_one * hat_one, axis=1, keepdims=True)
    )

    width = heads * HD

    sources = ring_sources()
    ring_places = ring_chips()

    def dp_sum(full, scatter_ties=(), gather_ties=()):
        piece = full.shape[0] // n_dp
        core = data_index % 2
        by_core = full.reshape(chips, 2, piece, full.shape[1])
        mine = lax.dynamic_index_in_dim(by_core, core, 1, keepdims=False)
        other = lax.dynamic_index_in_dim(by_core, 1 - core, 1, keepdims=False)
        both = (mine.astype(wide) + swap_core(other).astype(wide)).astype(narrow)
        parts = [lax.dynamic_index_in_dim(both, at, 0, keepdims=False) for at in ring_places]

        def tie(value, ties, step):
            return after(value, *ties[step]) if step < len(ties) else value

        total = tie(ring_next(parts[1]), scatter_ties, 0)
        for step in range(2, chips):
            total = ring_next((parts[step].astype(wide) + total.astype(wide)).astype(narrow))
            total = tie(total, scatter_ties, step - 1)
        held = [(parts[0].astype(wide) + total.astype(wide)).astype(narrow)]
        for step in range(chips - 1):
            held.append(tie(ring_next(held[-1]), gather_ties, step))
        blocks, places = [], []
        for block, at in zip(held, sources):
            blocks += [block, swap_core(block)]
            places += [source * piece for source in at]
        return blocks, jnp.stack(places)

    o_blocks, o_places = dp_sum(o_grad.astype(narrow))
    (o_sum,) = assemble(o_blocks, o_places, 1)
    qkv_grad = dot_tn(
        normed_one, jnp.concatenate([query_lin_grad, key_lin_grad, value_lin_grad], axis=1)
    ).astype(narrow)
    shared_down_grad = shared_down_all.astype(wide)
    shared_gate_grad = turn(shared_gate_all)
    shared_up_grad = turn(shared_up_all)
    qkv_blocks, qkv_places = dp_sum(
        qkv_grad,
        ((shared_down_grad, expert_gate_grad), (shared_gate_grad,), (expert_up_grad, input_grad)),
        ((shared_up_grad,), (o_sum,)),
    )
    q_sum, k_sum, v_sum = assemble(qkv_blocks, qkv_places, 3)

    gains = sum_over_plane(
        jnp.concatenate(
            [
                attn_gain_part,
                mlp_gain_part,
                router_grad_part,
                jnp.broadcast_to(squared_own, (128,)),
            ]
        )
    )
    small = sum_over_dp(
        jnp.concatenate(
            [
                gains,
                jnp.sum(query_lin_grad.astype(wide), axis=0),
                jnp.sum(key_lin_grad.astype(wide), axis=0),
                jnp.sum(value_lin_grad.astype(wide), axis=0),
            ]
        )
    )
    attn_gain_grad, mlp_gain_grad, shared_router_grad = (small[i * D : (i + 1) * D] for i in range(3))
    teacher_loss = small[3 * D] / (valid_count * D)
    biases = small[3 * D + 128 :]
    return (
        result.astype(narrow),
        teacher_loss,
        input_grad,
        attn_gain_grad,
        q_sum,
        biases[:width],
        k_sum,
        biases[width : 2 * width],
        v_sum,
        biases[2 * width :],
        o_sum,
        mlp_gain_grad,
        expert_gate_grad,
        expert_up_grad,
        expert_down_grad,
        shared_gate_grad,
        shared_up_grad,
        shared_down_grad,
        shared_router_grad,
    )


def solution(mesh):
    return jax.shard_map(
        shards,
        mesh=mesh,
        in_specs=(
            P(("dp", "tensor"), None),
            P(),
            P(None, "tensor"),
            P("tensor"),
            P(None, "tensor"),
            P("tensor"),
            P(None, "tensor"),
            P("tensor"),
            P("tensor", None),
            P(),
            P("dp", None, "tensor"),
            P("dp", None, "tensor"),
            P("dp", "tensor", None),
            P(None, "tensor"),
            P(None, "tensor"),
            P("tensor", None),
            P(),
            P("dp", None),
            P("dp", None),
            P(),
            P(),
            P(("dp", "tensor"), None),
            P(("dp", "tensor"), None),
        ),
        out_specs=(
            P(("dp", "tensor"), None),
            P(),
            P(("dp", "tensor"), None),
            P(),
            P(None, "tensor"),
            P("tensor"),
            P(None, "tensor"),
            P("tensor"),
            P(None, "tensor"),
            P("tensor"),
            P("tensor", None),
            P(),
            P("dp", None, "tensor"),
            P("dp", None, "tensor"),
            P("dp", "tensor", None),
            P(None, "tensor"),
            P(None, "tensor"),
            P("tensor", None),
            P(),
        ),
        check_vma=False,
    )
```

```python
import functools
import math

import jax
import jax.numpy as jnp
from jax import lax
from jax.experimental import pallas as pl
from jax.experimental.pallas import tpu as pltpu
from jax.sharding import PartitionSpec as P

D = 2048
HD = 128
PROMPT = 512
SLOT = 128
CONTS = 2
GROUP = 768


EPSILON = 1e-06
ROTARY_BASE = 1000000.0
WIDE = jnp.float32
NARROW = jnp.bfloat16
VMEM_BYTES = 60 * 1024 * 1024


def slot_layout(lengths_row, position):
    offset = jnp.maximum(position - PROMPT, 0)
    in_prompt = position < PROMPT
    segment = jnp.where(in_prompt, 0, 1 + offset // SLOT)
    rotary_place = jnp.where(in_prompt, position, PROMPT + offset % SLOT)
    matches = segment[:, None] - 1 == jnp.arange(CONTS, dtype=jnp.int32)[None, :]
    length_here = jnp.sum(jnp.where(matches, lengths_row[None, :], 0), axis=1)
    living = in_prompt | (offset % SLOT < length_here)
    return (segment, rotary_place, living)


def visible_keys(position, segment, living):
    causal = position[None, :] <= position[:, None]
    same_part = (segment[None, :] == segment[:, None]) | (segment[None, :] == 0)
    return causal & same_part & living[None, :]


def rotary_tables(rotary_place):
    freqs = jnp.exp(jnp.arange(HD // 2, dtype=jnp.float32) * (-2.0 * math.log(ROTARY_BASE) / HD))
    angles = rotary_place.astype(jnp.float32)[:, None] * freqs[None, :]
    angles = jnp.concatenate([angles, angles], axis=1)
    return (jnp.cos(angles), jnp.sin(angles))


def rotate(values, cosine, sine):
    half = values.shape[-1] // 2
    flipped = jnp.concatenate([-values[..., half:], values[..., :half]], axis=-1)
    return values * cosine[:, None, :] + flipped * sine[:, None, :]


def rotate_back(grads, cosine, sine):
    half = grads.shape[-1] // 2
    turned = grads * sine[:, None, :]
    flipped = jnp.concatenate([turned[..., half:], -turned[..., :half]], axis=-1)
    return grads * cosine[:, None, :] + flipped


def attention_scores(query_low, key_low, visible, scale):
    scores = (
        jnp.einsum("thd,shd->hts", query_low, key_low, preferred_element_type=jnp.float32) * scale
    )
    return jnp.where(visible[None], scores, -1e30)


def dot_nt(left, right):
    return lax.dot_general(left, right, (((1,), (1,)), ((), ())), preferred_element_type=WIDE)


def dot_nn(left, right):
    return lax.dot_general(left, right, (((1,), (0,)), ((), ())), preferred_element_type=WIDE)


def dot_tn(left, right):
    return lax.dot_general(left, right, (((0,), (0,)), ((), ())), preferred_element_type=WIDE)


def pin(values):
    return lax.optimization_barrier(values)


def after(value, *others):
    return pin((value,) + others)[0]


def flip(value, bit):
    size = lax.axis_size("tensor")
    return lax.ppermute(value, "tensor", [(i, i ^ bit) for i in range(size)])


def split_at(rows):
    return rows // 32 * 16


def plane_gather(value):
    size = lax.axis_size("tensor")
    if size == 4:
        cut = split_at(value.shape[0])
        one, two = flip(value, 1), flip(value, 2)
        low, high = flip(two[:cut], 1), flip(one[cut:], 2)
        return [value, one, two, jnp.concatenate([low, high], axis=0)]
    blocks, bit = [value], 1
    while bit < size:
        blocks = blocks + [flip(block, bit) for block in blocks]
        bit *= 2
    return blocks


def plane_scatter(parts):
    size = lax.axis_size("tensor")
    if size == 4:
        cut = split_at(parts[3].shape[0])
        far = parts[3].astype(NARROW)
        low, high = flip(far[:cut], 1), flip(far[cut:], 2)
        two = jnp.concatenate(
            [(parts[2][:cut].astype(WIDE) + low.astype(WIDE)).astype(NARROW), parts[2][cut:].astype(NARROW)], axis=0
        )
        one = jnp.concatenate(
            [parts[1][:cut].astype(NARROW), (parts[1][cut:].astype(WIDE) + high.astype(WIDE)).astype(NARROW)], axis=0
        )
        return parts[0].astype(WIDE) + flip(one, 1).astype(WIDE) + flip(two, 2).astype(WIDE)
    parts = [part.astype(WIDE) for part in parts]
    bit = size // 2
    while bit >= 1:
        parts = [parts[j] + flip(parts[bit + j].astype(NARROW), bit).astype(WIDE) for j in range(bit)]
        bit //= 2
    return parts[0]


def plane_gather_spare(value):
    if lax.axis_size("tensor") != 4:
        return plane_gather(value)
    one, two = flip(value, 1), flip(value, 2)
    return [value, one, two, flip(one, 2)]


def ring_order(chips):
    odd = list(range(1, chips, 2))
    even = list(range(2, chips, 2))
    return [0] + odd + even[::-1]


def ring_next(value):
    chips = lax.axis_size("dp") // 2
    order = ring_order(chips)
    pairs = [
        (2 * order[i] + c, 2 * order[(i + 1) % chips] + c) for i in range(chips) for c in range(2)
    ]
    return lax.ppermute(value, "dp", pairs)


def swap_core(value):
    size = lax.axis_size("dp")
    return lax.ppermute(value, "dp", [(i, i ^ 1) for i in range(size)])


def ring_chips():
    chips = lax.axis_size("dp") // 2
    order = ring_order(chips)
    chip = lax.axis_index("dp") // 2
    sources = []
    for step in range(chips):
        table = [0] * chips
        for place, here in enumerate(order):
            table[here] = order[(place - step) % chips]
        sources.append(jnp.asarray(table, jnp.int32)[chip])
    return sources


def ring_sources():
    core = lax.axis_index("dp") % 2
    return [(2 * chip + core, 2 * chip + 1 - core) for chip in ring_chips()]


def ring_gather(value):
    chips = lax.axis_size("dp") // 2
    held = [value]
    for _ in range(chips - 1):
        held.append(ring_next(held[-1]))
    return [(block, swap_core(block)) for block in held]


def ring_scatter(parts):
    chips = len(parts)
    total = None
    for step in list(range(1, chips)) + [0]:
        mine, other = parts[step]
        here = mine.astype(WIDE) + swap_core(other.astype(NARROW)).astype(WIDE)
        if total is not None:
            here = here + total.astype(WIDE)
        if step == 0:
            return here
        total = ring_next(here.astype(NARROW))


def plane_bits():
    size = lax.axis_size("tensor")
    bits = [1 << i for i in range(size.bit_length() - 1)]
    return bits[:1] + bits[2:], bits[1:2]


def bits_gather(value, bits):
    blocks = [value]
    for bit in bits:
        blocks = blocks + [flip(block, bit) for block in blocks]
    return blocks


def bits_scatter(parts, bits):
    for bit in bits[::-1]:
        half = len(parts) // 2
        parts = [
            parts[j].astype(WIDE) + flip(parts[half + j].astype(NARROW), bit).astype(WIDE)
            for j in range(half)
        ]
    return parts[0]


def bits_offsets(bits):
    offsets = [0]
    for bit in bits:
        offsets = offsets + [offset ^ bit for offset in offsets]
    return offsets


def chain_gather(value):
    held = [value]
    for _ in range(lax.axis_size("dp") // 2 - 1):
        held.append(ring_next(held[-1]))
    return held


def chain_scatter(parts):
    total = None
    for step in list(range(1, len(parts))) + [0]:
        here = parts[step].astype(WIDE)
        if total is not None:
            here = here + total.astype(WIDE)
        if step == 0:
            return here
        total = ring_next(here.astype(NARROW))


def sum_over_plane(vector):
    bit = 1
    while bit < lax.axis_size("tensor"):
        vector = vector + flip(vector, bit)
        bit *= 2
    return vector


class Copies:
    def __init__(self, sems):
        self.sems, self.used = sems, 0

    def start(self, source, target):
        copy = pltpu.make_async_copy(source, target, self.sems.at[self.used])
        self.used += 1
        copy.start()
        return copy


def weight_places(parts, count, cut):
    half = count // 2
    left = parts - cut
    chunks = [
        [(b, 0, cut, b * cut) for b in range(half)],
        [(b, 0, cut, (b - half) * cut) for b in range(half, count)],
        [(b, cut, left, b * left) for b in range(count)],
    ]
    sizes = [half * cut, half * cut, count * left]
    starts = [0, half * cut, count * cut]
    return [
        (start, size, [(b, at, n, start + place) for b, at, n, place in chunk])
        for start, size, chunk in zip(starts, sizes, chunks)
    ]


def piece_moves(moves, piece_rows):
    found = []
    for block, at, size, place in moves:
        first = 0
        for piece, (owner, rows) in enumerate(piece_rows):
            if owner != block:
                continue
            low, high = max(at, first), min(at + size, first + rows)
            if low < high:
                found.append((piece, low - first, high - low, place + low - at))
            first += rows
    return found


def flat_pieces(weights):
    pieces = [piece for blocks in weights for block in blocks for piece in block]
    rows = [
        [(b, piece.shape[0]) for b, block in enumerate(blocks) for piece in block]
        for blocks in weights
    ]
    return pieces, rows


def column(mix):
    return mix[...].T[:, :1]


def forward_body(rows, count, places, piece_rows, *refs):
    x_refs, refs = refs[:count], refs[count:]
    weights = []
    for held in piece_rows:
        weights.append(refs[: len(held)])
        refs = refs[len(held) :]
    mix_one, mix_two, router = refs[:3]
    out_refs, refs = refs[3 : 3 + count], refs[3 + count :]
    kept_refs, factor_ref, refs = refs[:9], refs[9], refs[10:]
    xs, gate_s, up_s, down_s, ys = refs[:5]
    kept, sems = refs[5:14], refs[14]
    copies = Copies(sems)
    x_in = [copies.start(x_refs[i], xs.at[pl.ds(i * rows, rows)]) for i in range(count)]
    w_in = [
        [
            [
                copies.start(weights[n][b].at[pl.ds(at, size)], held.at[pl.ds(place, size)])
                for b, at, size, place in piece_moves(moves, piece_rows[n])
            ]
            for n, held in enumerate((gate_s, up_s, down_s))
        ]
        for _, _, moves in places
    ]
    for copy in x_in:
        copy.wait()
    x = xs[...]
    router_gate = jax.nn.sigmoid(jnp.sum(x.astype(WIDE) * router[...], axis=1, keepdims=True))
    factor_ref[...] = router_gate
    factors = (column(mix_one), column(mix_two), router_gate)
    total, away = None, []
    for at, ((start, size, _), arriving) in enumerate(zip(places, w_in)):
        span = pl.ds(start, size)
        for copy in arriving[0]:
            copy.wait()
        gate_in = dot_nt(x, gate_s[span])
        for copy in arriving[1]:
            copy.wait()
        up_in = dot_nt(x, up_s[span])
        hidden = (gate_in * jax.nn.sigmoid(gate_in) * up_in * factors[at]).astype(NARROW)
        for n, value in enumerate((gate_in, up_in, hidden)):
            kept[3 * n + at][...] = value.astype(NARROW)
            away.append(copies.start(kept[3 * n + at], kept_refs[3 * n + at]))
        for copy in arriving[2]:
            copy.wait()
        part = dot_nn(hidden, down_s[span])
        total = part if total is None else total + part
    ys[...] = total.astype(NARROW)
    away += [copies.start(ys.at[pl.ds(i * rows, rows)], out_refs[i]) for i in range(count)]
    for copy in away:
        copy.wait()


def forward_step(x_blocks, weights, mix_one, mix_two, router, cut):
    count, (rows, width) = len(x_blocks), x_blocks[0].shape
    pieces, piece_rows = flat_pieces(weights)
    blocks, parts = len(weights[0]), sum(piece.shape[0] for piece in weights[0][0])
    places = weight_places(parts, blocks, cut)
    total, hidden = count * rows, blocks * parts
    anywhere, local = pl.BlockSpec(memory_space=pl.ANY), pl.BlockSpec(memory_space=pltpu.VMEM)
    shape = jax.ShapeDtypeStruct
    outs = pl.pallas_call(
        functools.partial(forward_body, rows, count, places, piece_rows),
        out_shape=[shape((rows, width), NARROW)] * count
        + [shape((total, size), NARROW) for _ in range(3) for _, size, _ in places]
        + [shape((total, 1), WIDE)],
        in_specs=[anywhere] * (count + len(pieces)) + [local] * 3,
        out_specs=[anywhere] * (count + 9) + [local],
        scratch_shapes=[pltpu.VMEM((total, width), NARROW)]
        + [pltpu.VMEM((hidden, width), NARROW)] * 3
        + [pltpu.VMEM((total, width), NARROW)]
        + [pltpu.VMEM((total, size), NARROW) for _ in range(3) for _, size, _ in places]
        + [pltpu.SemaphoreType.DMA((2 * count + 3 * len(pieces) + 9,))],
        compiler_params=pltpu.CompilerParams(vmem_limit_bytes=VMEM_BYTES),
        cost_estimate=pl.CostEstimate(
            flops=6 * total * hidden * width,
            bytes_accessed=6 * hidden * width + 4 * total * width + 6 * total * hidden,
            transcendentals=total * hidden,
        ),
        name="ffn_forward",
    )(*x_blocks, *pieces, mix_one, mix_two, router)
    outs, kept = outs[:count], outs[count:]
    return outs, kept[:3], kept[3:6], kept[6:9], kept[9]


def backward_body(rows, count, places, piece_rows, *refs):
    g_refs, refs = refs[:count], refs[count:]
    weights = []
    for held in piece_rows:
        weights.append(refs[: len(held)])
        refs = refs[len(held) :]
    kept_refs, refs = refs[:6], refs[6:]
    mix_one, mix_two, rg, router = refs[:4]
    out_refs, refs = refs[4 : 4 + count], refs[4 + count :]
    grad_refs, logit_ref, refs = refs[:6], refs[6], refs[7:]
    xs, gate_s, up_s, down_s, ys = refs[:5]
    kept, sems = refs[5:11], refs[11]
    copies = Copies(sems)
    g_in = [copies.start(g_refs[i], xs.at[pl.ds(i * rows, rows)]) for i in range(count)]
    w_in, kept_in = [], []
    for at, (start, size, moves) in enumerate(places):
        arriving = []
        for n, held in ((2, down_s), (0, gate_s), (1, up_s)):
            arriving.append(
                [
                    copies.start(weights[n][b].at[pl.ds(first, n_rows)], held.at[pl.ds(place, n_rows)])
                    for b, first, n_rows, place in piece_moves(moves, piece_rows[n])
                ]
            )
            if n == 2:
                kept_in.append([copies.start(kept_refs[3 * i + at], kept[3 * i + at]) for i in range(2)])
        w_in.append(arriving)
    for copy in g_in:
        copy.wait()
    grad = xs[...]
    factors = (column(mix_one), column(mix_two), rg[...])
    total, away = None, []
    for at, ((start, size, _), arriving) in enumerate(zip(places, w_in)):
        span = pl.ds(start, size)
        for copy in arriving[0]:
            copy.wait()
        grad_hidden = dot_nt(grad, down_s[span]) * factors[at]
        for copy in kept_in[at]:
            copy.wait()
        gate_in, up_in = kept[at][...].astype(WIDE), kept[3 + at][...].astype(WIDE)
        squash = jax.nn.sigmoid(gate_in)
        up_grad = grad_hidden * gate_in * squash
        gate_grad = grad_hidden * up_in * squash * (1.0 + gate_in * (1.0 - squash))
        logit = jnp.sum(up_grad * up_in, axis=1, keepdims=True)
        gate_grad, up_grad = gate_grad.astype(NARROW), up_grad.astype(NARROW)
        for n, value in enumerate((gate_grad, up_grad)):
            kept[3 * n + at][...] = value
            away.append(copies.start(kept[3 * n + at], grad_refs[3 * n + at]))
        for copy in arriving[1] + arriving[2]:
            copy.wait()
        part = dot_nn(gate_grad, gate_s[span]) + dot_nn(up_grad, up_s[span])
        total = part if total is None else total + part
    logit = logit * (1.0 - rg[...])
    logit_ref[...] = logit
    ys[...] = (total + logit * router[...]).astype(NARROW)
    away += [copies.start(ys.at[pl.ds(i * rows, rows)], out_refs[i]) for i in range(count)]
    for copy in away:
        copy.wait()


def backward_step(g_blocks, weights, gate_in, up_in, mix_one, mix_two, rg, router, cut):
    count, (rows, width) = len(g_blocks), g_blocks[0].shape
    pieces, piece_rows = flat_pieces(weights)
    blocks, parts = len(weights[0]), sum(piece.shape[0] for piece in weights[0][0])
    places = weight_places(parts, blocks, cut)
    total, hidden = count * rows, blocks * parts
    anywhere, local = pl.BlockSpec(memory_space=pl.ANY), pl.BlockSpec(memory_space=pltpu.VMEM)
    shape = jax.ShapeDtypeStruct
    outs = pl.pallas_call(
        functools.partial(backward_body, rows, count, places, piece_rows),
        out_shape=[shape((rows, width), NARROW)] * count
        + [shape((total, size), NARROW) for _ in range(2) for _, size, _ in places]
        + [shape((total, 1), WIDE)],
        in_specs=[anywhere] * (count + len(pieces) + 6) + [local] * 4,
        out_specs=[anywhere] * (count + 6) + [local],
        scratch_shapes=[pltpu.VMEM((total, width), NARROW)]
        + [pltpu.VMEM((hidden, width), NARROW)] * 3
        + [pltpu.VMEM((total, width), NARROW)]
        + [pltpu.VMEM((total, size), NARROW) for _ in range(2) for _, size, _ in places]
        + [pltpu.SemaphoreType.DMA((2 * count + 3 * len(pieces) + 12,))],
        compiler_params=pltpu.CompilerParams(vmem_limit_bytes=VMEM_BYTES),
        cost_estimate=pl.CostEstimate(
            flops=6 * total * hidden * width,
            bytes_accessed=6 * hidden * width + 4 * total * width + 8 * total * hidden,
            transcendentals=total * hidden,
        ),
        name="ffn_backward",
    )(
        *g_blocks,
        *pieces,
        *gate_in,
        *up_in,
        mix_one,
        mix_two,
        rg,
        router,
    )
    outs, kept = outs[:count], outs[count:]
    return outs, kept[:3], kept[3:6], kept[6]


def weight_body(rows, steps, blocks, shape, splits, apart, *refs):
    groups, names = len(shape), sum(shape)
    x_refs, refs = refs[: groups * steps * blocks], refs[groups * steps * blocks :]
    left_refs, refs = refs[: names * steps], refs[names * steps :]
    out_refs, refs = refs[:splits], refs[splits:]
    xs, ls, os, sems = refs
    copies = Copies(sems)
    part, hidden = blocks * rows, os.shape[1]
    x_in, left_in, n = [], [], 0
    for group, amount in enumerate(shape):
        arriving = []
        for i in range(steps * blocks):
            source = x_refs[group * steps * blocks + i]
            arriving.append(copies.start(source, xs.at[group, pl.ds(i * rows, rows)]))
        x_in.append(arriving)
        for _ in range(amount):
            left_in.append(
                [
                    copies.start(left_refs[n * steps + s], ls.at[n, pl.ds(s * part, part)])
                    for s in range(steps)
                ]
            )
            n += 1
    away, n = [], 0
    size = hidden // splits
    for group, amount in enumerate(shape):
        for copy in x_in[group]:
            copy.wait()
        for _ in range(amount):
            for copy in left_in[n]:
                copy.wait()
            os[n] = dot_tn(ls[n], xs[group]).astype(NARROW)
            if apart:
                away.append(copies.start(os.at[n], out_refs[n]))
            else:
                for j in range(splits):
                    target = out_refs[j].at[pl.ds(n * size, size)]
                    away.append(copies.start(os.at[n, pl.ds(j * size, size)], target))
            n += 1
    for copy in away:
        copy.wait()


def weight_grads(groups, splits, apart=False, light=False):
    steps, blocks = len(groups[0][0]), len(groups[0][0][0])
    shape = [len(lefts) for _, lefts in groups]
    names = sum(shape)
    rows, width = groups[0][0][0][0].shape
    total, hidden = steps * blocks * rows, groups[0][1][0][0].shape[1]
    anywhere = pl.BlockSpec(memory_space=pl.ANY)
    outs = pl.pallas_call(
        functools.partial(weight_body, rows, steps, blocks, shape, splits, apart),
        out_shape=[jax.ShapeDtypeStruct((names * hidden // splits, width), NARROW)] * splits,
        in_specs=[anywhere] * (steps * (len(groups) * blocks + names)),
        out_specs=[anywhere] * splits,
        scratch_shapes=[
            pltpu.VMEM((len(groups), total, width), NARROW),
            pltpu.VMEM((names, total, hidden), NARROW),
            pltpu.VMEM((names, hidden, width), NARROW),
            pltpu.SemaphoreType.DMA((steps * (len(groups) * blocks + names) + names * splits,)),
        ],
        compiler_params=pltpu.CompilerParams(vmem_limit_bytes=VMEM_BYTES),
        cost_estimate=pl.CostEstimate(
            flops=0 if light else 2 * names * total * hidden * width,
            bytes_accessed=0 if light else 2 * total * width + 2 * names * (total + width) * hidden,
            transcendentals=0,
        ),
        name="weight_grads",
    )(
        *[b for x_blocks, _ in groups for step in x_blocks for b in step],
        *[a for _, lefts in groups for left in lefts for a in left],
    )
    return list(outs)


def attention_body(piece, order, normed, grads, hidden, mixed, mine_ref, other_ref):
    width = mixed.shape[1]
    half = mine_ref.shape[0]
    for i in range(2 * half):
        target = mine_ref if i < half else other_ref
        span = pl.ds(pl.multiple_of(order[i] * piece, 128), piece)
        target[i % half, :, : 3 * width] = dot_tn(normed[:, span], grads[...]).astype(NARROW)
        target[i % half, :, 3 * width :] = dot_tn(hidden[:, span], mixed[...]).astype(NARROW)


def attention_grads(order, normed, grads, hidden, mixed):
    count = order.shape[0]
    group, depth = normed.shape
    width = mixed.shape[1]
    piece = depth // count
    local = pl.BlockSpec(memory_space=pltpu.VMEM)
    return pl.pallas_call(
        functools.partial(attention_body, piece),
        out_shape=[jax.ShapeDtypeStruct((count // 2, piece, 4 * width), NARROW)] * 2,
        in_specs=[pl.BlockSpec(memory_space=pltpu.SMEM)] + [local] * 4,
        out_specs=[local] * 2,
        compiler_params=pltpu.CompilerParams(vmem_limit_bytes=VMEM_BYTES),
        cost_estimate=pl.CostEstimate(
            flops=8 * group * depth * width,
            bytes_accessed=4 * group * depth + 8 * group * width + 8 * depth * width,
            transcendentals=0,
        ),
        name="attention_grads",
    )(order, normed, grads, hidden, mixed)


def assemble_body(count, rows, *refs):
    places, blocks, refs = refs[0], refs[1 : 1 + count], refs[1 + count :]
    outs, (held, straight, turned, sems) = refs[-8:-4], refs[-4:]
    copies = Copies(sems)
    width = straight.shape[3]
    moved = []
    for i in range(count):
        moved.append(copies.start(blocks[i].at[pl.ds(0, rows)], held.at[i]))
    away = []
    for i in range(count):
        moved[i].wait()
        place = pl.multiple_of(places[i], 128)
        for j in range(3):
            straight[i, j] = held[i, :, j * width : (j + 1) * width].astype(WIDE)
            away.append(copies.start(straight.at[i, j], outs[j].at[pl.ds(place, rows)]))
        turned[i] = held[i, :, 3 * width :].astype(WIDE).T
        away.append(copies.start(turned.at[i], outs[3].at[:, pl.ds(place, rows)]))
    for copy in away:
        copy.wait()


def assemble(blocks, places, rows, before):
    count, wide = len(blocks), blocks[0].shape[1]
    width = wide // 4
    depth = D
    shapes = [jax.ShapeDtypeStruct((depth, width), WIDE)] * 3
    anywhere = pl.BlockSpec(memory_space=pl.ANY)
    before = [] if before is None else list(before)
    return pl.pallas_call(
        functools.partial(assemble_body, count, rows),
        out_shape=shapes + [jax.ShapeDtypeStruct((width, depth), WIDE)],
        in_specs=[pl.BlockSpec(memory_space=pltpu.SMEM)] + [anywhere] * (count + len(before)),
        out_specs=[anywhere] * 4,
        scratch_shapes=[
            pltpu.VMEM((count, rows, wide), NARROW),
            pltpu.VMEM((count, 3, rows, width), WIDE),
            pltpu.VMEM((count, width, rows), WIDE),
            pltpu.SemaphoreType.DMA((5 * count,)),
        ],
        input_output_aliases={1 + count + i: i for i in range(len(before))},
        compiler_params=pltpu.CompilerParams(vmem_limit_bytes=VMEM_BYTES),
        name="assemble",
    )(places, *blocks, *before)


def turn_body(x_ref, out_ref):
    out_ref[...] = x_ref[...].astype(WIDE).T


def turn(value):
    rows, width = value.shape
    if rows % 128:
        return value.T.astype(WIDE)
    return pl.pallas_call(
        turn_body,
        grid=(width // 256,),
        out_shape=jax.ShapeDtypeStruct((width, rows), WIDE),
        in_specs=[pl.BlockSpec((rows, 256), lambda i: (0, i))],
        out_specs=pl.BlockSpec((256, rows), lambda i: (i, 0)),
        compiler_params=pltpu.CompilerParams(vmem_limit_bytes=VMEM_BYTES),
        name="turn",
    )(value)


def shards(
    hidden_in,
    attn_gain,
    q_weight,
    q_bias,
    k_weight,
    k_bias,
    v_weight,
    v_bias,
    o_weight,
    mlp_gain,
    expert_gate,
    expert_up,
    expert_down,
    shared_gate,
    shared_up,
    shared_down,
    shared_router,
    routes,
    gate_weights,
    lengths,
    loss_mask,
    teacher,
    cotangent,
):
    wide = WIDE
    narrow = NARROW
    data_index = lax.axis_index("dp")
    slice_index = lax.axis_index("tensor")
    n_dp = lax.axis_size("dp")
    n_tensor = lax.axis_size("tensor")
    rows = hidden_in.shape[0]
    heads = q_weight.shape[1] // HD
    f_expert = expert_gate.shape[2]
    f_shared = shared_gate.shape[1] // n_dp
    f_pad = -(-f_shared // 16) * 16
    scale = 1.0 / math.sqrt(HD)

    position = jnp.concatenate(
        [(slice_index ^ j) * rows + jnp.arange(rows, dtype=jnp.int32) for j in range(n_tensor)]
    )
    own_lengths = lax.dynamic_index_in_dim(lengths, data_index, 0, keepdims=False)
    segment, rotary_place, living = slot_layout(own_lengths, position)
    visible = visible_keys(position, segment, living)
    cosine, sine = rotary_tables(rotary_place)
    every = jnp.arange(GROUP, dtype=jnp.int32)
    living_all = jax.vmap(lambda row: slot_layout(row, every)[2])(lengths)
    valid_count = jnp.sum((living_all.reshape(-1) & (loss_mask == 1)).astype(wide))
    own_mask = lax.dynamic_slice_in_dim(loss_mask, data_index * GROUP + slice_index * rows, rows, 0)
    valid_own = living[:rows] & (own_mask == 1)

    own_input = hidden_in.astype(wide)
    inverse_one = lax.rsqrt(jnp.mean(own_input * own_input, axis=1, keepdims=True) + EPSILON)
    hat_one = own_input * inverse_one
    normed_own = (hat_one * attn_gain).astype(narrow)

    def pack(expert_rows, shared_rows):
        if f_pad != f_shared:
            shared_rows = jnp.pad(shared_rows, ((0, f_pad - f_shared), (0, 0)))
        return jnp.concatenate([expert_rows, shared_rows], axis=0)

    shared_at = data_index * f_shared
    own_gate = pack(
        expert_gate[0].T, lax.dynamic_slice_in_dim(shared_gate, shared_at, f_shared, 1).T
    )
    own_up = pack(expert_up[0].T, lax.dynamic_slice_in_dim(shared_up, shared_at, f_shared, 1).T)
    own_down = pack(expert_down[0], lax.dynamic_slice_in_dim(shared_down, shared_at, f_shared, 0))

    w_bits, r_bits = plane_bits()

    def both_cores(blocks):
        return blocks + [swap_core(block) for block in blocks]

    staged = n_tensor == 4 and n_dp == 8
    if staged:
        cut = split_at(own_down.shape[0])
        low = flip((expert_down[0] if cut <= f_expert else own_down)[:cut], w_bits[0])
        one, two = flip(normed_own, 1), flip(normed_own, 2)
        one, two, low, own_gate, own_down = pin((one, two, low, own_gate, own_down))
        normed_one_blocks = [normed_own, one, two, flip(one, 2)]
        high = flip(own_down[cut:], w_bits[0])
    else:
        normed_one_blocks = plane_gather(normed_own)
        high = own_down
    gate_blocks = bits_gather(own_gate, w_bits)
    normed_one = jnp.concatenate(normed_one_blocks, axis=0)

    row_slices = [slice_index ^ offset for offset in bits_offsets(r_bits)]
    mixing = jnp.sum(
        jnp.where(
            routes[None, :, :] == jnp.arange(n_dp, dtype=jnp.int32)[:, None, None],
            gate_weights[None, :, :],
            0.0,
        ),
        axis=2,
    )
    mixing = after(mixing, normed_one_blocks[-1])
    mixing_all = jnp.stack(chain_gather(mixing))
    experts = jnp.arange(n_dp, dtype=jnp.int32)
    slices = jnp.arange(n_tensor, dtype=jnp.int32)

    def mixing_of(expert):
        chosen = jnp.sum(
            jnp.where((experts == expert)[None, :, None], mixing_all, 0.0), axis=1
        ).reshape(-1, n_tensor, rows)
        chosen = jnp.stack(
            [jnp.sum(jnp.where((slices == at)[None, :, None], chosen, 0.0), axis=1) for at in row_slices],
            axis=1,
        )
        chosen = chosen.reshape(-1, 1, len(row_slices) * rows)
        return jnp.broadcast_to(chosen, (chosen.shape[0], 8, chosen.shape[2]))

    mix_one, mix_two = mixing_of(data_index), mixing_of(data_index ^ 1)

    query_lin = dot_nn(normed_one, q_weight) + q_bias
    key_lin = dot_nn(normed_one, k_weight) + k_bias
    value_low = (dot_nn(normed_one, v_weight) + v_bias).astype(narrow).reshape(GROUP, heads, HD)
    query_low = rotate(query_lin.reshape(GROUP, heads, HD), cosine, sine).astype(narrow)
    key_low = rotate(key_lin.reshape(GROUP, heads, HD), cosine, sine).astype(narrow)
    scores = attention_scores(query_low, key_low, visible, scale)
    top_score = jnp.max(scores, axis=2, keepdims=True)
    expo = jnp.exp(scores - top_score)
    total_expo = jnp.sum(expo, axis=2, keepdims=True)
    log_total = top_score + jnp.log(total_expo)
    probs_low = (expo / total_expo).astype(narrow)
    mixed = jnp.einsum("hts,shd->thd", probs_low, value_low, preferred_element_type=wide)
    mixed_low = mixed.reshape(GROUP, heads * HD).astype(narrow)
    own_swaps = [swap_core(own) for own in (own_gate, own_up, own_down)]
    mix_one, mix_two = ([mix[i] for i in range(n_dp // 2)] for mix in (mix_one, mix_two))
    mixed_low, mix_one, mix_two, own_swaps = pin((mixed_low, mix_one, mix_two, own_swaps))
    head_part = dot_nn(mixed_low, o_weight).astype(narrow)
    parts = [head_part[j * rows : (j + 1) * rows] for j in range(n_tensor)]
    if n_tensor == 4:
        far = [flip(part, 2) for part in parts[2:]]
        near = (parts[1].astype(wide) + far[1].astype(wide)).astype(narrow)
        near, gate_blocks, own_up, high = pin((near, gate_blocks, own_up, high))
        attn_own = parts[0].astype(wide) + far[0].astype(wide) + flip(near, 1).astype(wide)
    else:
        attn_own = plane_scatter(parts)

    hidden_mid = own_input + attn_own
    inverse_two = lax.rsqrt(jnp.mean(hidden_mid * hidden_mid, axis=1, keepdims=True) + EPSILON)
    hat_two = hidden_mid * inverse_two
    normed_two = (hat_two * mlp_gain).astype(narrow)
    chips = n_dp // 2
    x_chain = [normed_two, ring_next(normed_two)]
    x_steps = [bits_gather(normed_two, r_bits)]
    if staged:
        up_low = flip(own_up[:cut], w_bits[0])
        x_chain[1], x_steps, own_up = pin((x_chain[1], x_steps, own_up))
        x_chain.append(ring_next(x_chain[1]))
        x_steps.append(bits_gather(x_chain[1], r_bits))
        up_high = flip(own_up[cut:], w_bits[0])
        x_chain[2], x_steps = pin((x_chain[2], x_steps))
        x_chain.append(ring_next(x_chain[2]))
        x_steps.append(bits_gather(x_chain[2], r_bits))
        x_steps.append(bits_gather(x_chain[3], r_bits))
        arrived = ([gate_blocks[1]], [up_low, up_high], [low, high])
        weights = [
            [[own], pieces, [swapped], [swap_core(piece) for piece in pieces]]
            for own, pieces, swapped in zip((own_gate, own_up, own_down), arrived, own_swaps)
        ]
    else:
        while len(x_chain) < chips:
            x_chain.append(ring_next(x_chain[-1]))
        x_steps += [bits_gather(block, r_bits) for block in x_chain[1:]]
        up_blocks, down_blocks = bits_gather(own_up, w_bits), bits_gather(own_down, w_bits)
        weights = [
            [[block] for block in blocks + [swapped] + [swap_core(block) for block in blocks[1:]]]
            for blocks, swapped in zip((gate_blocks, up_blocks, down_blocks), own_swaps)
        ]
    n_blocks, n_hidden = len(weights[0]), len(weights[0]) // 2
    places = weight_places(f_expert + f_shared, n_blocks, f_expert)

    router_row = shared_router.astype(wide)[None]
    forward, out_sums, total = {}, {}, None
    order = list(range(1, chips)) + [0]
    for place, step in enumerate(order):
        x, ready = x_steps[step], []
        if place == 0:
            ready = [x_chain[order[1]], *x_steps[0]]
        if place >= 1:
            ready = list(forward[order[place - 1]][0])
            ready += x_steps[order[min(place + 1, chips - 1)]]
        if place >= 2:
            done = order[place - 2]
            out_sums[done] = bits_scatter(forward[done][0], r_bits)
            ready.append(out_sums[done])
            if total is not None:
                ready.append(total)
        x = list(lax.optimization_barrier((*x, *ready)))
        if place >= 2:
            kept = x[len(x) - (2 if total is not None else 1) :]
            here = kept[0].astype(wide)
            if total is not None:
                here = here + kept[1].astype(wide)
            total = ring_next(here.astype(narrow))
        x = x[: len(x_steps[step])]
        forward[step] = forward_step(
            x, weights, mix_one[step], mix_two[step], router_row, f_expert
        )
    for done in order[-2:]:
        out_sums[done] = bits_scatter(forward[done][0], r_bits)
    total = ring_next((out_sums[order[-2]].astype(wide) + total.astype(wide)).astype(narrow))
    branch_own = out_sums[0].astype(wide) + total.astype(wide)
    result = hidden_mid + branch_own

    difference = result - teacher.astype(wide)
    squared_own = jnp.sum(jnp.where(valid_own[:, None], difference * difference, 0.0))
    result_grad = cotangent.astype(wide) + jnp.where(
        valid_own[:, None], difference * (2.0 / (valid_count * D)), 0.0
    )
    grad_own = result_grad.astype(narrow)

    def core_parts(mine, other, first, size):
        return [
            mine[first + j * size : first + (j + 1) * size].astype(wide)
            + other[first + j * size : first + (j + 1) * size].astype(wide)
            for j in range(n_hidden)
        ]

    def shared_parts(mine, other, which):
        both = core_parts(mine, other, which * n_hidden * f_pad, f_pad)
        return [both[0]] + [part.astype(narrow) for part in both[1:]]

    def shared_sum(parts):
        return bits_scatter(parts, w_bits)[:f_shared].astype(narrow)

    def expert_sum(mine, other):
        return bits_scatter(core_parts(mine, other, 0, f_expert), w_bits)

    hidden_of = [[forward[step][3][part] for step in range(chips)] for part in range(3)]
    g_chain = chain_gather(grad_own)
    g_steps = [bits_gather(block, r_bits) for block in g_chain]
    backward, dx_sums, total = [], {}, None
    for step in range(chips):
        ready = []
        if step + 1 < chips:
            ready.append(g_chain[step + 1])
        if step >= 1:
            ready.append(backward[step - 1][0])
        if step >= 2:
            dx_sums[step - 2] = bits_scatter(backward[step - 2][0], r_bits)
            ready.append(dx_sums[step - 2])
        g, ready = pin((g_steps[step], ready))
        if step >= 2:
            dx_sums[step - 2] = ready[2 if step + 1 < chips else 1]
        backward.append(
            backward_step(
                g,
                weights,
                forward[step][1],
                forward[step][2],
                mix_one[step],
                mix_two[step],
                forward[step][4],
                router_row,
                f_expert,
            )
        )
    gate_of, up_of = (
        [[backward[step][n][part] for step in range(chips)] for part in range(3)] for n in (1, 2)
    )
    for step in range(1, chips - 2):
        here = dx_sums[step].astype(wide)
        total = ring_next((here if total is None else here + total.astype(wide)).astype(narrow))
    dx_sums[chips - 2] = bits_scatter(backward[chips - 2][0], r_bits)
    x_steps, g_steps, dx_sums[chips - 2], total, _ = pin(
        (x_steps, g_steps, dx_sums[chips - 2], total, backward[-1][0])
    )
    shared_mine, shared_other = weight_grads(
        [(g_steps, [hidden_of[2]]), (x_steps, [gate_of[2], up_of[2]])], 2
    )
    total = ring_next((dx_sums[chips - 2].astype(wide) + total.astype(wide)).astype(narrow))
    dx_sums[chips - 1] = bits_scatter(backward[chips - 1][0], r_bits)
    g_steps, dx_sums[chips - 1], total, shared_mine, shared_other = pin(
        (g_steps, dx_sums[chips - 1], total, shared_mine, shared_other)
    )
    here = (dx_sums[chips - 1].astype(wide) + total.astype(wide)).astype(narrow)
    here, g_steps = pin((here, g_steps))
    total = ring_next(here)
    (down_other,) = weight_grads([(g_steps, hidden_of[1:2])], 1, light=True)
    g_steps, down_other, shared_other = pin((g_steps, down_other, shared_other))
    shared_other = swap_core(shared_other)
    (down_mine,) = weight_grads([(g_steps, hidden_of[:1])], 1, light=True)
    shared_mine, shared_other, down_mine, down_other = pin(
        (shared_mine, shared_other, down_mine, down_other)
    )
    shared_down_own = shared_sum(shared_parts(shared_mine, shared_other, 0))
    normed_two_grad = dx_sums[0].astype(wide) + total.astype(wide)

    grad_wide = grad_own.astype(wide)
    mlp_gain_part = jnp.sum(normed_two_grad * hat_two, axis=0)
    scaled_two = normed_two_grad * mlp_gain
    hidden_grad = grad_wide + inverse_two * (
        scaled_two - hat_two * jnp.mean(scaled_two * hat_two, axis=1, keepdims=True)
    )
    router_grad_part = sum(
        jnp.sum(backward[step][3][i * rows : (i + 1) * rows] * block.astype(wide), axis=0)
        for step in range(chips)
        for i, block in enumerate(x_steps[step])
    )
    own_low = hidden_grad.astype(narrow)
    if n_tensor == 4:
        own_low, x_steps, shared_down_own = pin((own_low, x_steps, shared_down_own))
        one, two = flip(own_low, 1), flip(own_low, 2)
        gate_experts = weight_grads([(x_steps, gate_of[:2])], 2, True)
        one, two, gate_experts, shared_mine, shared_other = pin(
            (one, two, gate_experts, shared_mine, shared_other)
        )
        grad_blocks = [own_low, one, two, flip(one, 2)]
    else:
        gate_experts = weight_grads([(x_steps, gate_of[:2])], 2, True)
        grad_blocks = plane_gather(own_low)
    down_experts = [down_mine, down_other]
    shared_down_all = lax.all_gather(shared_down_own, "dp", axis=0, tiled=True)
    shared_gate_own = shared_sum(shared_parts(shared_mine, shared_other, 1))
    grad_blocks, gate_experts, shared_gate_own, shared_mine, shared_other = pin(
        (grad_blocks, gate_experts, shared_gate_own, shared_mine, shared_other)
    )
    shared_gate_all = lax.all_gather(shared_gate_own, "dp", axis=0, tiled=True)
    shared_up_own = shared_sum(shared_parts(shared_mine, shared_other, 2))
    hidden_grad_low = jnp.concatenate(grad_blocks, axis=0)

    mixed_grad = dot_nt(hidden_grad_low, o_weight).astype(narrow).reshape(GROUP, heads, HD)
    scores_again = attention_scores(query_low, key_low, visible, scale)
    probs = jnp.exp(scores_again - log_total)
    probs_grad = jnp.einsum("thd,shd->hts", mixed_grad, value_low, preferred_element_type=wide)
    value_grad = jnp.einsum(
        "hts,thd->shd", probs.astype(narrow), mixed_grad, preferred_element_type=wide
    )
    inner = jnp.sum(probs * probs_grad, axis=2, keepdims=True)
    scores_grad = (probs * (probs_grad - inner)).astype(narrow)
    query_grad = (
        jnp.einsum("hts,shd->thd", scores_grad, key_low, preferred_element_type=wide) * scale
    )
    key_grad = (
        jnp.einsum("hts,thd->shd", scores_grad, query_low, preferred_element_type=wide) * scale
    )
    query_grad, shared_up_own, down_experts, gate_experts = pin(
        (query_grad, shared_up_own, down_experts, gate_experts)
    )
    shared_up_all = lax.all_gather(shared_up_own, "dp", axis=0, tiled=True)
    for experts_of in (down_experts, gate_experts):
        experts_of[1] = swap_core(experts_of[1])
    query_lin_grad = rotate_back(query_grad, cosine, sine).reshape(GROUP, heads * HD).astype(narrow)
    key_lin_grad = rotate_back(key_grad, cosine, sine).reshape(GROUP, heads * HD).astype(narrow)
    value_lin_grad = value_grad.reshape(GROUP, heads * HD).astype(narrow)
    width = heads * HD
    piece = D // n_dp
    sources = ring_sources()
    ring_places = ring_chips()
    lin_grads = jnp.concatenate([query_lin_grad, key_lin_grad, value_lin_grad], axis=1)
    attn_mine, attn_other = attention_grads(
        jnp.stack([at[0] for at in sources] + [at[1] for at in sources]).astype(jnp.int32),
        normed_one,
        lin_grads,
        hidden_grad_low,
        mixed_low,
    )
    attn_other = swap_core(attn_other)
    attn_other, lin_grads, x_steps = pin((attn_other, lin_grads, x_steps))

    def attn_part(step):
        return attn_mine[step].astype(wide) + attn_other[step].astype(wide)

    here, x_steps = pin((attn_part(1).astype(narrow), x_steps))
    total = ring_next(here)
    up_experts = weight_grads([(x_steps, up_of[:2])], 2, True)
    up_experts[1] = swap_core(up_experts[1])
    total, up_experts, down_experts, gate_experts = pin(
        (total, up_experts, down_experts, gate_experts)
    )
    norm_one_part = sum(
        dot_nt(lin_grads[:, i * width : (i + 1) * width], weight)
        for i, weight in enumerate((q_weight, k_weight, v_weight))
    ).astype(narrow)
    normed_one_grad = plane_scatter(
        [norm_one_part[j * rows : (j + 1) * rows] for j in range(n_tensor)]
    )
    attn_gain_part = jnp.sum(normed_one_grad * hat_one, axis=0)
    scaled_one = normed_one_grad * attn_gain
    input_grad = hidden_grad + inverse_one * (
        scaled_one - hat_one * jnp.mean(scaled_one * hat_one, axis=1, keepdims=True)
    )

    def small_rows():
        gains = jnp.concatenate(
            [
                attn_gain_part,
                mlp_gain_part,
                router_grad_part,
                jnp.broadcast_to(squared_own, (128,)),
            ]
        )
        biases = [
            jnp.sum(grad.astype(wide), axis=0)
            for grad in (query_lin_grad, key_lin_grad, value_lin_grad)
        ]
        small = jnp.concatenate([sum_over_plane(gains), *biases])
        small = small + swap_core(small)
        lanes = 4 * width
        count = -(-small.shape[0] // (8 * lanes)) * 8
        small = jnp.pad(small, (0, count * lanes - small.shape[0])).reshape(count, lanes)
        high = small.astype(narrow)
        return jnp.concatenate([high, (small - high.astype(wide)).astype(narrow)], axis=0)

    expert_down_grad = expert_sum(*down_experts)[None]
    expert_gate_grad = expert_sum(*gate_experts).T[None]
    expert_up_grad = expert_sum(*up_experts).T[None]
    shared_down_grad = shared_down_all.astype(wide)
    shared_gate_grad = turn(shared_gate_all)
    shared_up_grad = turn(shared_up_all)
    ties = [(), (shared_down_grad, shared_gate_grad)]
    for step in range(2, chips):
        if step - 2 < len(ties):
            total = after(total, *ties[step - 2])
        total = ring_next((attn_part(step) + total.astype(wide)).astype(narrow))
    total = after(total, input_grad, expert_down_grad)
    attn_own = (attn_part(0) + total.astype(wide)).astype(narrow)
    attn_held = [jnp.concatenate([attn_own, small_rows()], axis=0)]
    ties = [(shared_up_grad, expert_gate_grad), (expert_up_grad,)]
    for step in range(chips - 1):
        block = ring_next(attn_held[-1])
        attn_held.append(after(block, *ties[step]) if step < len(ties) else block)
    attn_blocks, attn_places, sums = [], [], None
    for step, (block, at) in enumerate(zip(attn_held, sources)):
        if step == chips - 1:
            sums = assemble(attn_blocks, jnp.stack(attn_places), piece, None)
            block, sums = pin((block, sums))
            attn_blocks, attn_places = [], []
        attn_blocks += [block, swap_core(block)]
        attn_places += [source * piece for source in at]
    q_sum, k_sum, v_sum, o_sum = assemble(attn_blocks, jnp.stack(attn_places), piece, sums)
    small = 0.0
    for chip in range(chips):
        rows_of = sum(
            jnp.where(at == chip, block[piece:].astype(wide), 0.0)
            for block, at in zip(attn_held, ring_places)
        )
        small = small + rows_of
    half = small.shape[0] // 2
    small = (small[:half] + small[half:]).reshape(-1)

    attn_gain_grad, mlp_gain_grad, shared_router_grad = (small[i * D : (i + 1) * D] for i in range(3))
    teacher_loss = small[3 * D] / (valid_count * D)
    biases = small[3 * D + 128 :]
    return (
        result.astype(narrow),
        teacher_loss,
        input_grad,
        attn_gain_grad,
        q_sum,
        biases[:width],
        k_sum,
        biases[width : 2 * width],
        v_sum,
        biases[2 * width : 3 * width],
        o_sum,
        mlp_gain_grad,
        expert_gate_grad,
        expert_up_grad,
        expert_down_grad,
        shared_gate_grad,
        shared_up_grad,
        shared_down_grad,
        shared_router_grad,
    )


def solution(mesh):
    return jax.shard_map(
        shards,
        mesh=mesh,
        in_specs=(
            P(("dp", "tensor"), None),
            P(),
            P(None, "tensor"),
            P("tensor"),
            P(None, "tensor"),
            P("tensor"),
            P(None, "tensor"),
            P("tensor"),
            P("tensor", None),
            P(),
            P("dp", None, "tensor"),
            P("dp", None, "tensor"),
            P("dp", "tensor", None),
            P(None, "tensor"),
            P(None, "tensor"),
            P("tensor", None),
            P(),
            P("dp", None),
            P("dp", None),
            P(),
            P(),
            P(("dp", "tensor"), None),
            P(("dp", "tensor"), None),
        ),
        out_specs=(
            P(("dp", "tensor"), None),
            P(),
            P(("dp", "tensor"), None),
            P(),
            P(None, "tensor"),
            P("tensor"),
            P(None, "tensor"),
            P("tensor"),
            P(None, "tensor"),
            P("tensor"),
            P("tensor", None),
            P(),
            P("dp", None, "tensor"),
            P("dp", None, "tensor"),
            P("dp", "tensor", None),
            P(None, "tensor"),
            P(None, "tensor"),
            P("tensor", None),
            P(),
        ),
        check_vma=False,
    )
```

```python
import functools
import math

import jax
import jax.numpy as jnp
from jax import lax
from jax.experimental import pallas as pl
from jax.experimental.pallas import tpu as pltpu
from jax.sharding import PartitionSpec as P

D = 2048
HD = 128
PROMPT = 512
SLOT = 128
CONTS = 2
GROUP = 768


EPSILON = 1e-06
ROTARY_BASE = 1000000.0
WIDE = jnp.float32
NARROW = jnp.bfloat16
VMEM_BYTES = 60 * 1024 * 1024


def slot_layout(lengths_row, position):
    offset = jnp.maximum(position - PROMPT, 0)
    in_prompt = position < PROMPT
    segment = jnp.where(in_prompt, 0, 1 + offset // SLOT)
    rotary_place = jnp.where(in_prompt, position, PROMPT + offset % SLOT)
    matches = segment[:, None] - 1 == jnp.arange(CONTS, dtype=jnp.int32)[None, :]
    length_here = jnp.sum(jnp.where(matches, lengths_row[None, :], 0), axis=1)
    living = in_prompt | (offset % SLOT < length_here)
    return (segment, rotary_place, living)


def visible_keys(position, segment, living):
    causal = position[None, :] <= position[:, None]
    same_part = (segment[None, :] == segment[:, None]) | (segment[None, :] == 0)
    return causal & same_part & living[None, :]


def rotary_tables(rotary_place):
    freqs = jnp.exp(jnp.arange(HD // 2, dtype=jnp.float32) * (-2.0 * math.log(ROTARY_BASE) / HD))
    angles = rotary_place.astype(jnp.float32)[:, None] * freqs[None, :]
    angles = jnp.concatenate([angles, angles], axis=1)
    return (jnp.cos(angles), jnp.sin(angles))


def rotate(values, cosine, sine):
    half = values.shape[-1] // 2
    flipped = jnp.concatenate([-values[..., half:], values[..., :half]], axis=-1)
    return values * cosine[:, None, :] + flipped * sine[:, None, :]


def rotate_back(grads, cosine, sine):
    half = grads.shape[-1] // 2
    turned = grads * sine[:, None, :]
    flipped = jnp.concatenate([turned[..., half:], -turned[..., :half]], axis=-1)
    return grads * cosine[:, None, :] + flipped


def attention_scores(query_low, key_low, visible, scale):
    scores = (
        jnp.einsum("thd,shd->hts", query_low, key_low, preferred_element_type=jnp.float32) * scale
    )
    return jnp.where(visible[None], scores, -1e30)


def dot_nt(left, right):
    return lax.dot_general(left, right, (((1,), (1,)), ((), ())), preferred_element_type=WIDE)


def dot_nn(left, right):
    return lax.dot_general(left, right, (((1,), (0,)), ((), ())), preferred_element_type=WIDE)


def dot_tn(left, right):
    return lax.dot_general(left, right, (((0,), (0,)), ((), ())), preferred_element_type=WIDE)


def pin(values):
    return lax.optimization_barrier(values)


def after(value, *others):
    return pin((value,) + others)[0]


def flip(value, bit):
    size = lax.axis_size("tensor")
    return lax.ppermute(value, "tensor", [(i, i ^ bit) for i in range(size)])


def split_at(rows):
    return rows // 32 * 16


def plane_gather(value):
    size = lax.axis_size("tensor")
    if size == 4:
        cut = split_at(value.shape[0])
        one, two = flip(value, 1), flip(value, 2)
        low, high = flip(two[:cut], 1), flip(one[cut:], 2)
        return [value, one, two, jnp.concatenate([low, high], axis=0)]
    blocks, bit = [value], 1
    while bit < size:
        blocks = blocks + [flip(block, bit) for block in blocks]
        bit *= 2
    return blocks


def plane_scatter(parts):
    size = lax.axis_size("tensor")
    if size == 4:
        cut = split_at(parts[3].shape[0])
        far = parts[3].astype(NARROW)
        low, high = flip(far[:cut], 1), flip(far[cut:], 2)
        two = jnp.concatenate(
            [(parts[2][:cut].astype(WIDE) + low.astype(WIDE)).astype(NARROW), parts[2][cut:].astype(NARROW)], axis=0
        )
        one = jnp.concatenate(
            [parts[1][:cut].astype(NARROW), (parts[1][cut:].astype(WIDE) + high.astype(WIDE)).astype(NARROW)], axis=0
        )
        return parts[0].astype(WIDE) + flip(one, 1).astype(WIDE) + flip(two, 2).astype(WIDE)
    parts = [part.astype(WIDE) for part in parts]
    bit = size // 2
    while bit >= 1:
        parts = [parts[j] + flip(parts[bit + j].astype(NARROW), bit).astype(WIDE) for j in range(bit)]
        bit //= 2
    return parts[0]


def plane_gather_spare(value):
    if lax.axis_size("tensor") != 4:
        return plane_gather(value)
    one, two = flip(value, 1), flip(value, 2)
    return [value, one, two, flip(one, 2)]


def ring_order(chips):
    odd = list(range(1, chips, 2))
    even = list(range(2, chips, 2))
    return [0] + odd + even[::-1]


def ring_next(value):
    chips = lax.axis_size("dp") // 2
    order = ring_order(chips)
    pairs = [
        (2 * order[i] + c, 2 * order[(i + 1) % chips] + c) for i in range(chips) for c in range(2)
    ]
    return lax.ppermute(value, "dp", pairs)


def swap_core(value):
    size = lax.axis_size("dp")
    return lax.ppermute(value, "dp", [(i, i ^ 1) for i in range(size)])


def both_ways(value, bit):
    n_dp, size = lax.axis_size("dp"), lax.axis_size("tensor")
    pairs = [(d * size + t, (d ^ 1) * size + (t ^ bit)) for d in range(n_dp) for t in range(size)]
    return lax.ppermute(value, ("dp", "tensor"), pairs)


def ring_chips():
    chips = lax.axis_size("dp") // 2
    order = ring_order(chips)
    chip = lax.axis_index("dp") // 2
    sources = []
    for step in range(chips):
        table = [0] * chips
        for place, here in enumerate(order):
            table[here] = order[(place - step) % chips]
        sources.append(jnp.asarray(table, jnp.int32)[chip])
    return sources


def ring_sources():
    core = lax.axis_index("dp") % 2
    return [(2 * chip + core, 2 * chip + 1 - core) for chip in ring_chips()]


def ring_gather(value):
    chips = lax.axis_size("dp") // 2
    held = [value]
    for _ in range(chips - 1):
        held.append(ring_next(held[-1]))
    return [(block, swap_core(block)) for block in held]


def ring_scatter(parts):
    chips = len(parts)
    total = None
    for step in list(range(1, chips)) + [0]:
        mine, other = parts[step]
        here = mine.astype(WIDE) + swap_core(other.astype(NARROW)).astype(WIDE)
        if total is not None:
            here = here + total.astype(WIDE)
        if step == 0:
            return here
        total = ring_next(here.astype(NARROW))


def plane_bits():
    size = lax.axis_size("tensor")
    bits = [1 << i for i in range(size.bit_length() - 1)]
    return bits[:1] + bits[2:], bits[1:2]


def bits_gather(value, bits):
    blocks = [value]
    for bit in bits:
        blocks = blocks + [flip(block, bit) for block in blocks]
    return blocks


def bits_scatter(parts, bits):
    for bit in bits[::-1]:
        half = len(parts) // 2
        parts = [
            parts[j].astype(WIDE) + flip(parts[half + j].astype(NARROW), bit).astype(WIDE)
            for j in range(half)
        ]
    return parts[0]


def bits_offsets(bits):
    offsets = [0]
    for bit in bits:
        offsets = offsets + [offset ^ bit for offset in offsets]
    return offsets


def chain_gather(value):
    held = [value]
    for _ in range(lax.axis_size("dp") // 2 - 1):
        held.append(ring_next(held[-1]))
    return held


def chain_scatter(parts):
    total = None
    for step in list(range(1, len(parts))) + [0]:
        here = parts[step].astype(WIDE)
        if total is not None:
            here = here + total.astype(WIDE)
        if step == 0:
            return here
        total = ring_next(here.astype(NARROW))


def sum_over_plane(vector):
    bit = 1
    while bit < lax.axis_size("tensor"):
        vector = vector + flip(vector, bit)
        bit *= 2
    return vector


class Copies:
    def __init__(self, sems):
        self.sems, self.used = sems, 0

    def start(self, source, target):
        copy = pltpu.make_async_copy(source, target, self.sems.at[self.used])
        self.used += 1
        copy.start()
        return copy


def weight_places(parts, count, cut):
    half = count // 2
    left = parts - cut
    chunks = [
        [(b, 0, cut, b * cut) for b in range(half)],
        [(b, 0, cut, (b - half) * cut) for b in range(half, count)],
        [(b, cut, left, b * left) for b in range(count)],
    ]
    sizes = [half * cut, half * cut, count * left]
    starts = [0, half * cut, count * cut]
    return [
        (start, size, [(b, at, n, start + place) for b, at, n, place in chunk])
        for start, size, chunk in zip(starts, sizes, chunks)
    ]


def piece_moves(moves, piece_rows):
    found = []
    for block, at, size, place in moves:
        first = 0
        for piece, (owner, rows) in enumerate(piece_rows):
            if owner != block:
                continue
            low, high = max(at, first), min(at + size, first + rows)
            if low < high:
                found.append((piece, low - first, high - low, place + low - at))
            first += rows
    return found


def flat_pieces(weights):
    pieces = [piece for blocks in weights for block in blocks for piece in block]
    rows = [
        [(b, piece.shape[0]) for b, block in enumerate(blocks) for piece in block]
        for blocks in weights
    ]
    return pieces, rows


def column(mix):
    return mix[...].T[:, :1]


def forward_body(rows, count, places, piece_rows, *refs):
    x_refs, refs = refs[:count], refs[count:]
    weights = []
    for held in piece_rows:
        weights.append(refs[: len(held)])
        refs = refs[len(held) :]
    mix_one, mix_two, router = refs[:3]
    out_refs, refs = refs[3 : 3 + count], refs[3 + count :]
    kept_refs, factor_ref, refs = refs[:9], refs[9], refs[10:]
    xs, gate_s, up_s, down_s, ys = refs[:5]
    kept, sems = refs[5:14], refs[14]
    copies = Copies(sems)
    x_in = [copies.start(x_refs[i], xs.at[pl.ds(i * rows, rows)]) for i in range(count)]
    w_in = [
        [
            [
                copies.start(weights[n][b].at[pl.ds(at, size)], held.at[pl.ds(place, size)])
                for b, at, size, place in piece_moves(moves, piece_rows[n])
            ]
            for n, held in enumerate((gate_s, up_s, down_s))
        ]
        for _, _, moves in places
    ]
    for copy in x_in:
        copy.wait()
    x = xs[...]
    router_gate = jax.nn.sigmoid(jnp.sum(x.astype(WIDE) * router[...], axis=1, keepdims=True))
    factor_ref[...] = router_gate
    factors = (column(mix_one), column(mix_two), router_gate)
    away, products, total = [], [], None
    for at in range(len(places) + 1):
        if at < len(places):
            start, size, _ = places[at]
            for copy in w_in[at][0] + w_in[at][1]:
                copy.wait()
        if at > 0:
            for copy in w_in[at - 1][2]:
                copy.wait()
        if at < len(places):
            products.append(
                (dot_nt(x, gate_s[pl.ds(start, size)]), dot_nt(x, up_s[pl.ds(start, size)]))
            )
        if at > 0:
            gate_in, up_in = products[at - 1]
            hidden = (gate_in * jax.nn.sigmoid(gate_in) * up_in * factors[at - 1]).astype(NARROW)
            for n, value in enumerate((gate_in, up_in, hidden)):
                kept[3 * n + at - 1][...] = value.astype(NARROW)
            start, size, _ = places[at - 1]
            part = dot_nn(hidden, down_s[pl.ds(start, size)])
            total = part if total is None else total + part
            for n in range(3):
                away.append(copies.start(kept[3 * n + at - 1], kept_refs[3 * n + at - 1]))
    ys[...] = total.astype(NARROW)
    away += [copies.start(ys.at[pl.ds(i * rows, rows)], out_refs[i]) for i in range(count)]
    for copy in away:
        copy.wait()


def forward_step(x_blocks, weights, mix_one, mix_two, router, cut):
    count, (rows, width) = len(x_blocks), x_blocks[0].shape
    pieces, piece_rows = flat_pieces(weights)
    blocks, parts = len(weights[0]), sum(piece.shape[0] for piece in weights[0][0])
    places = weight_places(parts, blocks, cut)
    total, hidden = count * rows, blocks * parts
    anywhere, local = pl.BlockSpec(memory_space=pl.ANY), pl.BlockSpec(memory_space=pltpu.VMEM)
    shape = jax.ShapeDtypeStruct
    outs = pl.pallas_call(
        functools.partial(forward_body, rows, count, places, piece_rows),
        out_shape=[shape((rows, width), NARROW)] * count
        + [shape((total, size), NARROW) for _ in range(3) for _, size, _ in places]
        + [shape((total, 1), WIDE)],
        in_specs=[anywhere] * (count + len(pieces)) + [local] * 3,
        out_specs=[anywhere] * (count + 9) + [local],
        scratch_shapes=[pltpu.VMEM((total, width), NARROW)]
        + [pltpu.VMEM((hidden, width), NARROW)] * 3
        + [pltpu.VMEM((total, width), NARROW)]
        + [pltpu.VMEM((total, size), NARROW) for _ in range(3) for _, size, _ in places]
        + [pltpu.SemaphoreType.DMA((2 * count + 3 * len(pieces) + 9,))],
        compiler_params=pltpu.CompilerParams(vmem_limit_bytes=VMEM_BYTES),
        cost_estimate=pl.CostEstimate(
            flops=6 * total * hidden * width,
            bytes_accessed=6 * hidden * width + 4 * total * width + 6 * total * hidden,
            transcendentals=total * hidden,
        ),
        name="ffn_forward",
    )(*x_blocks, *pieces, mix_one, mix_two, router)
    outs, kept = outs[:count], outs[count:]
    return outs, kept[:3], kept[3:6], kept[6:9], kept[9]


def backward_body(rows, count, places, piece_rows, *refs):
    g_refs, refs = refs[:count], refs[count:]
    weights = []
    for held in piece_rows:
        weights.append(refs[: len(held)])
        refs = refs[len(held) :]
    kept_refs, refs = refs[:6], refs[6:]
    mix_one, mix_two, rg, router = refs[:4]
    out_refs, refs = refs[4 : 4 + count], refs[4 + count :]
    grad_refs, logit_ref, refs = refs[:6], refs[6], refs[7:]
    xs, gate_s, up_s, down_s, ys = refs[:5]
    kept, sems = refs[5:11], refs[11]
    copies = Copies(sems)
    g_in = [copies.start(g_refs[i], xs.at[pl.ds(i * rows, rows)]) for i in range(count)]
    w_in, kept_in = [], []
    for at, (start, size, moves) in enumerate(places):
        arriving = []
        for n, held in ((2, down_s), (0, gate_s), (1, up_s)):
            arriving.append(
                [
                    copies.start(weights[n][b].at[pl.ds(first, n_rows)], held.at[pl.ds(place, n_rows)])
                    for b, first, n_rows, place in piece_moves(moves, piece_rows[n])
                ]
            )
            if n == 2:
                kept_in.append([copies.start(kept_refs[3 * i + at], kept[3 * i + at]) for i in range(2)])
        w_in.append(arriving)
    for copy in g_in:
        copy.wait()
    grad = xs[...]
    factors = (column(mix_one), column(mix_two), rg[...])
    away, products, total = [], [], None
    for at in range(len(places) + 1):
        if at < len(places):
            start, size, _ = places[at]
            for copy in w_in[at][0] + kept_in[at]:
                copy.wait()
        if at > 0:
            for copy in w_in[at - 1][1] + w_in[at - 1][2]:
                copy.wait()
        if at < len(places):
            products.append(dot_nt(grad, down_s[pl.ds(start, size)]))
        if at > 0:
            grad_hidden = products[at - 1] * factors[at - 1]
            gate_in, up_in = kept[at - 1][...].astype(WIDE), kept[2 + at][...].astype(WIDE)
            squash = jax.nn.sigmoid(gate_in)
            up_grad = grad_hidden * gate_in * squash
            gate_grad = grad_hidden * up_in * squash * (1.0 + gate_in * (1.0 - squash))
            logit = jnp.sum(up_grad * up_in, axis=1, keepdims=True)
            gate_grad, up_grad = gate_grad.astype(NARROW), up_grad.astype(NARROW)
            kept[at - 1][...] = gate_grad
            kept[2 + at][...] = up_grad
            start, size, _ = places[at - 1]
            span = pl.ds(start, size)
            part = dot_nn(gate_grad, gate_s[span]) + dot_nn(up_grad, up_s[span])
            total = part if total is None else total + part
            for n in range(2):
                away.append(copies.start(kept[3 * n + at - 1], grad_refs[3 * n + at - 1]))
    logit = logit * (1.0 - rg[...])
    logit_ref[...] = logit
    ys[...] = (total + logit * router[...]).astype(NARROW)
    away += [copies.start(ys.at[pl.ds(i * rows, rows)], out_refs[i]) for i in range(count)]
    for copy in away:
        copy.wait()


def backward_step(g_blocks, weights, gate_in, up_in, mix_one, mix_two, rg, router, cut):
    count, (rows, width) = len(g_blocks), g_blocks[0].shape
    pieces, piece_rows = flat_pieces(weights)
    blocks, parts = len(weights[0]), sum(piece.shape[0] for piece in weights[0][0])
    places = weight_places(parts, blocks, cut)
    total, hidden = count * rows, blocks * parts
    anywhere, local = pl.BlockSpec(memory_space=pl.ANY), pl.BlockSpec(memory_space=pltpu.VMEM)
    shape = jax.ShapeDtypeStruct
    outs = pl.pallas_call(
        functools.partial(backward_body, rows, count, places, piece_rows),
        out_shape=[shape((rows, width), NARROW)] * count
        + [shape((total, size), NARROW) for _ in range(2) for _, size, _ in places]
        + [shape((total, 1), WIDE)],
        in_specs=[anywhere] * (count + len(pieces) + 6) + [local] * 4,
        out_specs=[anywhere] * (count + 6) + [local],
        scratch_shapes=[pltpu.VMEM((total, width), NARROW)]
        + [pltpu.VMEM((hidden, width), NARROW)] * 3
        + [pltpu.VMEM((total, width), NARROW)]
        + [pltpu.VMEM((total, size), NARROW) for _ in range(2) for _, size, _ in places]
        + [pltpu.SemaphoreType.DMA((2 * count + 3 * len(pieces) + 12,))],
        compiler_params=pltpu.CompilerParams(vmem_limit_bytes=VMEM_BYTES),
        cost_estimate=pl.CostEstimate(
            flops=6 * total * hidden * width,
            bytes_accessed=6 * hidden * width + 4 * total * width + 8 * total * hidden,
            transcendentals=total * hidden,
        ),
        name="ffn_backward",
    )(
        *g_blocks,
        *pieces,
        *gate_in,
        *up_in,
        mix_one,
        mix_two,
        rg,
        router,
    )
    outs, kept = outs[:count], outs[count:]
    return outs, kept[:3], kept[3:6], kept[6]


def weight_body(rows, steps, blocks, shape, plan, *refs):
    groups, names = len(shape), sum(shape)
    x_refs, refs = refs[: groups * steps * blocks], refs[groups * steps * blocks :]
    left_refs, refs = refs[: names * steps], refs[names * steps :]
    out_refs, (xs, ls, os, sems) = refs[:-4], refs[-4:]
    copies = Copies(sems)
    part = blocks * rows
    x_in, left_in, n = [], [], 0
    for group, amount in enumerate(shape):
        arriving = []
        for i in range(steps * blocks):
            source = x_refs[group * steps * blocks + i]
            arriving.append(copies.start(source, xs.at[group, pl.ds(i * rows, rows)]))
        x_in.append(arriving)
        for _ in range(amount):
            left_in.append(
                [
                    copies.start(left_refs[n * steps + s], ls.at[n, pl.ds(s * part, part)])
                    for s in range(steps)
                ]
            )
            n += 1
    away, n = [], 0
    for group, amount in enumerate(shape):
        for copy in x_in[group]:
            copy.wait()
        for _ in range(amount):
            for copy in left_in[n]:
                copy.wait()
            os[n] = dot_tn(ls[n], xs[group]).astype(NARROW)
            for first, size, out, place in plan[n]:
                target = out_refs[out].at[pl.ds(place, size)]
                away.append(copies.start(os.at[n, pl.ds(first, size)], target))
            n += 1
    for copy in away:
        copy.wait()


def weight_grads(groups, plan=None, light=False):
    steps, blocks = len(groups[0][0]), len(groups[0][0][0])
    shape = [len(lefts) for _, lefts in groups]
    names = sum(shape)
    rows, width = groups[0][0][0][0].shape
    total, hidden = steps * blocks * rows, groups[0][1][0][0].shape[1]
    plan = plan or [[(0, hidden, n, 0)] for n in range(names)]
    sizes = {}
    for moves in plan:
        for _, size, out, place in moves:
            sizes[out] = max(sizes.get(out, 0), place + size)
    anywhere = pl.BlockSpec(memory_space=pl.ANY)
    outs = pl.pallas_call(
        functools.partial(weight_body, rows, steps, blocks, shape, plan),
        out_shape=[jax.ShapeDtypeStruct((sizes[out], width), NARROW) for out in range(len(sizes))],
        in_specs=[anywhere] * (steps * (len(groups) * blocks + names)),
        out_specs=[anywhere] * len(sizes),
        scratch_shapes=[
            pltpu.VMEM((len(groups), total, width), NARROW),
            pltpu.VMEM((names, total, hidden), NARROW),
            pltpu.VMEM((names, hidden, width), NARROW),
            pltpu.SemaphoreType.DMA(
                (steps * (len(groups) * blocks + names) + sum(len(moves) for moves in plan),)
            ),
        ],
        compiler_params=pltpu.CompilerParams(vmem_limit_bytes=VMEM_BYTES),
        cost_estimate=pl.CostEstimate(
            flops=0 if light else 2 * names * total * hidden * width,
            bytes_accessed=0 if light else 2 * total * width + 2 * names * (total + width) * hidden,
            transcendentals=0,
        ),
        name="weight_grads",
    )(
        *[b for x_blocks, _ in groups for step in x_blocks for b in step],
        *[a for _, lefts in groups for left in lefts for a in left],
    )
    return list(outs)


def attention_body(piece, order, normed, grads, hidden, mixed, mine_ref, other_ref):
    width = mixed.shape[1]
    half = mine_ref.shape[0]
    for i in range(2 * half):
        target = mine_ref if i < half else other_ref
        span = pl.ds(pl.multiple_of(order[i] * piece, 128), piece)
        target[i % half, :, : 3 * width] = dot_tn(normed[:, span], grads[...]).astype(NARROW)
        target[i % half, :, 3 * width :] = dot_tn(hidden[:, span], mixed[...]).astype(NARROW)


def attention_grads(order, normed, grads, hidden, mixed):
    count = order.shape[0]
    group, depth = normed.shape
    width = mixed.shape[1]
    piece = depth // count
    local = pl.BlockSpec(memory_space=pltpu.VMEM)
    return pl.pallas_call(
        functools.partial(attention_body, piece),
        out_shape=[jax.ShapeDtypeStruct((count // 2, piece, 4 * width), NARROW)] * 2,
        in_specs=[pl.BlockSpec(memory_space=pltpu.SMEM)] + [local] * 4,
        out_specs=[local] * 2,
        compiler_params=pltpu.CompilerParams(vmem_limit_bytes=VMEM_BYTES),
        cost_estimate=pl.CostEstimate(
            flops=8 * group * depth * width,
            bytes_accessed=4 * group * depth + 8 * group * width + 8 * depth * width,
            transcendentals=0,
        ),
        name="attention_grads",
    )(order, normed, grads, hidden, mixed)


def assemble_body(count, rows, *refs):
    places, blocks, refs = refs[0], refs[1 : 1 + count], refs[1 + count :]
    outs, (held, straight, turned, sems) = refs[-8:-4], refs[-4:]
    copies = Copies(sems)
    width = straight.shape[3]
    moved = []
    for i in range(count):
        moved.append(copies.start(blocks[i].at[pl.ds(0, rows)], held.at[i]))
    away = []
    for i in range(count):
        moved[i].wait()
        place = pl.multiple_of(places[i], 128)
        for j in range(3):
            straight[i, j] = held[i, :, j * width : (j + 1) * width].astype(WIDE)
            away.append(copies.start(straight.at[i, j], outs[j].at[pl.ds(place, rows)]))
        turned[i] = held[i, :, 3 * width :].astype(WIDE).T
        away.append(copies.start(turned.at[i], outs[3].at[:, pl.ds(place, rows)]))
    for copy in away:
        copy.wait()


def assemble(blocks, places, rows, before):
    count, wide = len(blocks), blocks[0].shape[1]
    width = wide // 4
    depth = D
    shapes = [jax.ShapeDtypeStruct((depth, width), WIDE)] * 3
    anywhere = pl.BlockSpec(memory_space=pl.ANY)
    before = [] if before is None else list(before)
    return pl.pallas_call(
        functools.partial(assemble_body, count, rows),
        out_shape=shapes + [jax.ShapeDtypeStruct((width, depth), WIDE)],
        in_specs=[pl.BlockSpec(memory_space=pltpu.SMEM)] + [anywhere] * (count + len(before)),
        out_specs=[anywhere] * 4,
        scratch_shapes=[
            pltpu.VMEM((count, rows, wide), NARROW),
            pltpu.VMEM((count, 3, rows, width), WIDE),
            pltpu.VMEM((count, width, rows), WIDE),
            pltpu.SemaphoreType.DMA((5 * count,)),
        ],
        input_output_aliases={1 + count + i: i for i in range(len(before))},
        compiler_params=pltpu.CompilerParams(vmem_limit_bytes=VMEM_BYTES),
        name="assemble",
    )(places, *blocks, *before)


def turn_body(x_ref, out_ref):
    count, _, rows, width = x_ref.shape
    out_ref[...] = x_ref[...].reshape(count * rows, width).astype(WIDE).T


def turn(value, count, which, rows):
    width = value.shape[1]
    value = value.reshape(count, 2, -1, width)
    if value.shape[2] != rows or (count * rows) % 128:
        return value[:, which, :rows].reshape(count * rows, width).T.astype(WIDE)
    return pl.pallas_call(
        turn_body,
        grid=(width // 256,),
        out_shape=jax.ShapeDtypeStruct((width, count * rows), WIDE),
        in_specs=[pl.BlockSpec((count, 1, rows, 256), lambda i: (0, which, 0, i))],
        out_specs=pl.BlockSpec((256, count * rows), lambda i: (i, 0)),
        compiler_params=pltpu.CompilerParams(vmem_limit_bytes=VMEM_BYTES),
        name="turn",
    )(value)


def shards(
    hidden_in,
    attn_gain,
    q_weight,
    q_bias,
    k_weight,
    k_bias,
    v_weight,
    v_bias,
    o_weight,
    mlp_gain,
    expert_gate,
    expert_up,
    expert_down,
    shared_gate,
    shared_up,
    shared_down,
    shared_router,
    routes,
    gate_weights,
    lengths,
    loss_mask,
    teacher,
    cotangent,
):
    wide = WIDE
    narrow = NARROW
    data_index = lax.axis_index("dp")
    slice_index = lax.axis_index("tensor")
    n_dp = lax.axis_size("dp")
    n_tensor = lax.axis_size("tensor")
    rows = hidden_in.shape[0]
    heads = q_weight.shape[1] // HD
    f_expert = expert_gate.shape[2]
    f_shared = shared_gate.shape[1] // n_dp
    f_pad = -(-f_shared // 16) * 16
    scale = 1.0 / math.sqrt(HD)

    position = jnp.concatenate(
        [(slice_index ^ j) * rows + jnp.arange(rows, dtype=jnp.int32) for j in range(n_tensor)]
    )
    own_lengths = lax.dynamic_index_in_dim(lengths, data_index, 0, keepdims=False)
    segment, rotary_place, living = slot_layout(own_lengths, position)
    visible = visible_keys(position, segment, living)
    cosine, sine = rotary_tables(rotary_place)
    every = jnp.arange(GROUP, dtype=jnp.int32)
    living_all = jax.vmap(lambda row: slot_layout(row, every)[2])(lengths)
    valid_count = jnp.sum((living_all.reshape(-1) & (loss_mask == 1)).astype(wide))
    own_mask = lax.dynamic_slice_in_dim(loss_mask, data_index * GROUP + slice_index * rows, rows, 0)
    valid_own = living[:rows] & (own_mask == 1)

    own_input = hidden_in.astype(wide)
    inverse_one = lax.rsqrt(jnp.mean(own_input * own_input, axis=1, keepdims=True) + EPSILON)
    hat_one = own_input * inverse_one
    normed_own = (hat_one * attn_gain).astype(narrow)

    def pack(expert_rows, shared_rows):
        if f_pad != f_shared:
            shared_rows = jnp.pad(shared_rows, ((0, f_pad - f_shared), (0, 0)))
        return jnp.concatenate([expert_rows, shared_rows], axis=0)

    shared_at = data_index * f_shared
    own_gate = pack(
        expert_gate[0].T, lax.dynamic_slice_in_dim(shared_gate, shared_at, f_shared, 1).T
    )
    own_up = pack(expert_up[0].T, lax.dynamic_slice_in_dim(shared_up, shared_at, f_shared, 1).T)
    own_down = pack(expert_down[0], lax.dynamic_slice_in_dim(shared_down, shared_at, f_shared, 0))

    w_bits, r_bits = plane_bits()

    def both_cores(blocks):
        return blocks + [swap_core(block) for block in blocks]

    staged = n_tensor == 4 and n_dp == 8
    if staged:
        cut = split_at(own_down.shape[0])
        low = flip((expert_down[0] if cut <= f_expert else own_down)[:cut], w_bits[0])
        one, two = flip(normed_own, 1), flip(normed_own, 2)
        one, two, low, own_gate, own_down = pin((one, two, low, own_gate, own_down))
        normed_one_blocks = [normed_own, one, two, flip(one, 2)]
        high = flip(own_down[cut:], w_bits[0])
    else:
        normed_one_blocks = plane_gather(normed_own)
        high = own_down
    gate_blocks = bits_gather(own_gate, w_bits)
    normed_one = jnp.concatenate(normed_one_blocks, axis=0)

    row_slices = [slice_index ^ offset for offset in bits_offsets(r_bits)]
    mixing = jnp.sum(
        jnp.where(
            routes[None, :, :] == jnp.arange(n_dp, dtype=jnp.int32)[:, None, None],
            gate_weights[None, :, :],
            0.0,
        ),
        axis=2,
    )
    mixing = after(mixing, normed_one_blocks[-1])
    mixing_all = jnp.stack(chain_gather(mixing))
    experts = jnp.arange(n_dp, dtype=jnp.int32)
    slices = jnp.arange(n_tensor, dtype=jnp.int32)

    def mixing_of(expert):
        chosen = jnp.sum(
            jnp.where((experts == expert)[None, :, None], mixing_all, 0.0), axis=1
        ).reshape(-1, n_tensor, rows)
        chosen = jnp.stack(
            [jnp.sum(jnp.where((slices == at)[None, :, None], chosen, 0.0), axis=1) for at in row_slices],
            axis=1,
        )
        chosen = chosen.reshape(-1, 1, len(row_slices) * rows)
        return jnp.broadcast_to(chosen, (chosen.shape[0], 8, chosen.shape[2]))

    mix_one, mix_two = mixing_of(data_index), mixing_of(data_index ^ 1)

    query_lin = dot_nn(normed_one, q_weight) + q_bias
    key_lin = dot_nn(normed_one, k_weight) + k_bias
    value_low = (dot_nn(normed_one, v_weight) + v_bias).astype(narrow).reshape(GROUP, heads, HD)
    query_low = rotate(query_lin.reshape(GROUP, heads, HD), cosine, sine).astype(narrow)
    key_low = rotate(key_lin.reshape(GROUP, heads, HD), cosine, sine).astype(narrow)
    scores = attention_scores(query_low, key_low, visible, scale)
    top_score = jnp.max(scores, axis=2, keepdims=True)
    expo = jnp.exp(scores - top_score)
    total_expo = jnp.sum(expo, axis=2, keepdims=True)
    log_total = top_score + jnp.log(total_expo)
    probs_low = (expo / total_expo).astype(narrow)
    mixed = jnp.einsum("hts,shd->thd", probs_low, value_low, preferred_element_type=wide)
    mixed_low = mixed.reshape(GROUP, heads * HD).astype(narrow)
    own_swaps = [swap_core(own) for own in (own_gate, own_up, own_down)]
    mix_one, mix_two = ([mix[i] for i in range(n_dp // 2)] for mix in (mix_one, mix_two))
    mixed_low, mix_one, mix_two, own_swaps = pin((mixed_low, mix_one, mix_two, own_swaps))
    head_part = dot_nn(mixed_low, o_weight).astype(narrow)
    parts = [head_part[j * rows : (j + 1) * rows] for j in range(n_tensor)]
    if n_tensor == 4:
        far = [flip(part, 2) for part in parts[2:]]
        near = (parts[1].astype(wide) + far[1].astype(wide)).astype(narrow)
        near, gate_blocks, own_up, high = pin((near, gate_blocks, own_up, high))
        attn_own = parts[0].astype(wide) + far[0].astype(wide) + flip(near, 1).astype(wide)
    else:
        attn_own = plane_scatter(parts)

    hidden_mid = own_input + attn_own
    inverse_two = lax.rsqrt(jnp.mean(hidden_mid * hidden_mid, axis=1, keepdims=True) + EPSILON)
    hat_two = hidden_mid * inverse_two
    normed_two = (hat_two * mlp_gain).astype(narrow)
    chips = n_dp // 2
    x_chain = [normed_two, ring_next(normed_two)]
    x_steps = [bits_gather(normed_two, r_bits)]
    if staged:
        up_low = flip(own_up[:cut], w_bits[0])
        x_chain[1], x_steps, own_up = pin((x_chain[1], x_steps, own_up))
        x_chain.append(ring_next(x_chain[1]))
        x_steps.append(bits_gather(x_chain[1], r_bits))
        up_high = flip(own_up[cut:], w_bits[0])
        x_chain[2], x_steps = pin((x_chain[2], x_steps))
        x_chain.append(ring_next(x_chain[2]))
        x_steps.append(bits_gather(x_chain[2], r_bits))
        x_steps.append(bits_gather(x_chain[3], r_bits))
        arrived = ([gate_blocks[1]], [up_low, up_high], [low, high])
        weights = [
            [[own], pieces, [swapped], [swap_core(piece) for piece in pieces]]
            for own, pieces, swapped in zip((own_gate, own_up, own_down), arrived, own_swaps)
        ]
    else:
        while len(x_chain) < chips:
            x_chain.append(ring_next(x_chain[-1]))
        x_steps += [bits_gather(block, r_bits) for block in x_chain[1:]]
        up_blocks, down_blocks = bits_gather(own_up, w_bits), bits_gather(own_down, w_bits)
        weights = [
            [[block] for block in blocks + [swapped] + [swap_core(block) for block in blocks[1:]]]
            for blocks, swapped in zip((gate_blocks, up_blocks, down_blocks), own_swaps)
        ]
    n_blocks, n_hidden = len(weights[0]), len(weights[0]) // 2
    places = weight_places(f_expert + f_shared, n_blocks, f_expert)

    router_row = shared_router.astype(wide)[None]
    forward, out_sums, total = {}, {}, None
    order = list(range(1, chips)) + [0]
    for place, step in enumerate(order):
        x, ready = x_steps[step], []
        if place == 0:
            ready = [x_chain[order[1]], *x_steps[0]]
        if place >= 1:
            ready = list(forward[order[place - 1]][0])
            ready += x_steps[order[min(place + 1, chips - 1)]]
        if place >= 2:
            done = order[place - 2]
            out_sums[done] = bits_scatter(forward[done][0], r_bits)
            ready.append(out_sums[done])
            if total is not None:
                ready.append(total)
        x = list(lax.optimization_barrier((*x, *ready)))
        if place >= 2:
            kept = x[len(x) - (2 if total is not None else 1) :]
            here = kept[0].astype(wide)
            if total is not None:
                here = here + kept[1].astype(wide)
            total = ring_next(here.astype(narrow))
        x = x[: len(x_steps[step])]
        forward[step] = forward_step(
            x, weights, mix_one[step], mix_two[step], router_row, f_expert
        )
    for done in order[-2:]:
        out_sums[done] = bits_scatter(forward[done][0], r_bits)
    total = ring_next((out_sums[order[-2]].astype(wide) + total.astype(wide)).astype(narrow))
    branch_own = out_sums[0].astype(wide) + total.astype(wide)
    result = hidden_mid + branch_own

    difference = result - teacher.astype(wide)
    squared_own = jnp.sum(jnp.where(valid_own[:, None], difference * difference, 0.0))
    result_grad = cotangent.astype(wide) + jnp.where(
        valid_own[:, None], difference * (2.0 / (valid_count * D)), 0.0
    )
    grad_own = result_grad.astype(narrow)

    def core_parts(mine, other, first, size):
        return [
            mine[first + j * size : first + (j + 1) * size].astype(wide)
            + other[first + j * size : first + (j + 1) * size].astype(wide)
            for j in range(n_hidden)
        ]

    def shared_sum(parts):
        return bits_scatter(parts, w_bits).astype(narrow)

    def expert_sum(mine, other):
        return bits_scatter(core_parts(mine, other, 0, f_expert), w_bits)

    hidden_of = [[forward[step][3][part] for step in range(chips)] for part in range(3)]
    g_chain = chain_gather(grad_own)
    g_steps = [bits_gather(block, r_bits) for block in g_chain]
    backward, dx_sums, total = [], {}, None
    for step in range(chips):
        ready = []
        if step + 1 < chips:
            ready.append(g_chain[step + 1])
        if step >= 1:
            ready.append(backward[step - 1][0])
        if step >= 2:
            dx_sums[step - 2] = bits_scatter(backward[step - 2][0], r_bits)
            ready.append(dx_sums[step - 2])
        g, ready = pin((g_steps[step], ready))
        if step >= 2:
            dx_sums[step - 2] = ready[2 if step + 1 < chips else 1]
        backward.append(
            backward_step(
                g,
                weights,
                forward[step][1],
                forward[step][2],
                mix_one[step],
                mix_two[step],
                forward[step][4],
                router_row,
                f_expert,
            )
        )
    gate_of, up_of = (
        [[backward[step][n][part] for step in range(chips)] for part in range(3)] for n in (1, 2)
    )
    for step in range(1, chips - 2):
        here = dx_sums[step].astype(wide)
        total = ring_next((here if total is None else here + total.astype(wide)).astype(narrow))
    dx_sums[chips - 2] = bits_scatter(backward[chips - 2][0], r_bits)
    x_steps, g_steps, dx_sums[chips - 2], total, _ = pin(
        (x_steps, g_steps, dx_sums[chips - 2], total, backward[-1][0])
    )
    near, far = n_blocks, n_blocks + 1
    plan = [[(b * f_pad, f_pad, b, 0) for b in range(n_blocks)]]
    plan += [
        [
            (b * f_pad, f_pad, near if b < n_hidden else far, (b % n_hidden * 2 + n) * f_pad)
            for b in range(n_blocks)
        ]
        for n in range(2)
    ]
    *down_pieces, shared_mine, shared_other = weight_grads(
        [(g_steps, [hidden_of[2]]), (x_steps, [gate_of[2], up_of[2]])], plan
    )
    total = ring_next((dx_sums[chips - 2].astype(wide) + total.astype(wide)).astype(narrow))
    dx_sums[chips - 1] = bits_scatter(backward[chips - 1][0], r_bits)
    g_steps, dx_sums[chips - 1], total, shared_mine, shared_other, down_pieces = pin(
        (g_steps, dx_sums[chips - 1], total, shared_mine, shared_other, down_pieces)
    )
    here = (dx_sums[chips - 1].astype(wide) + total.astype(wide)).astype(narrow)
    here, g_steps, down_pieces = pin((here, g_steps, down_pieces))
    total = ring_next(here)
    if n_hidden == 2:
        bit = w_bits[0]
        parts = [
            down_pieces[0],
            flip(down_pieces[1], bit),
            swap_core(down_pieces[2]),
            both_ways(down_pieces[3], bit),
        ]
        down_experts = weight_grads([(g_steps, hidden_of[:2])])
        total, parts, down_experts = pin((total, parts, down_experts))
        shared_down_own = sum(part.astype(wide) for part in parts)[:f_shared].astype(narrow)
    else:
        parts = [
            mine.astype(wide) + swap_core(other).astype(wide)
            for mine, other in zip(down_pieces[:n_hidden], down_pieces[n_hidden:])
        ]
        down_experts = weight_grads([(g_steps, hidden_of[:2])])
        shared_down_own = shared_sum(parts)[:f_shared]
    shared_down_all = lax.all_gather(shared_down_own, "dp", axis=0, tiled=True)
    normed_two_grad = dx_sums[0].astype(wide) + total.astype(wide)

    grad_wide = grad_own.astype(wide)
    mlp_gain_part = jnp.sum(normed_two_grad * hat_two, axis=0)
    scaled_two = normed_two_grad * mlp_gain
    hidden_grad = grad_wide + inverse_two * (
        scaled_two - hat_two * jnp.mean(scaled_two * hat_two, axis=1, keepdims=True)
    )
    router_grad_part = sum(
        jnp.sum(backward[step][3][i * rows : (i + 1) * rows] * block.astype(wide), axis=0)
        for step in range(chips)
        for i, block in enumerate(x_steps[step])
    )
    own_low = hidden_grad.astype(narrow)
    if n_tensor == 4:
        own_low, x_steps = pin((own_low, x_steps))
        shared_other = swap_core(shared_other)
        one, two = flip(own_low, 1), flip(own_low, 2)
        gate_experts = weight_grads([(x_steps, gate_of[:2])])
        one, two, gate_experts, shared_mine, shared_other = pin(
            (one, two, gate_experts, shared_mine, shared_other)
        )
        grad_blocks = [own_low, one, two, flip(one, 2)]
    else:
        gate_experts = weight_grads([(x_steps, gate_of[:2])])
        shared_other = swap_core(shared_other)
        grad_blocks = plane_gather(own_low)
    both = core_parts(shared_mine, shared_other, 0, 2 * f_pad)
    shared_two_own = shared_sum([both[0]] + [part.astype(narrow) for part in both[1:]])
    grad_blocks, gate_experts = pin((grad_blocks, gate_experts))
    hidden_grad_low = jnp.concatenate(grad_blocks, axis=0)

    mixed_grad = dot_nt(hidden_grad_low, o_weight).astype(narrow).reshape(GROUP, heads, HD)
    scores_again = attention_scores(query_low, key_low, visible, scale)
    probs = jnp.exp(scores_again - log_total)
    probs_grad = jnp.einsum("thd,shd->hts", mixed_grad, value_low, preferred_element_type=wide)
    value_grad = jnp.einsum(
        "hts,thd->shd", probs.astype(narrow), mixed_grad, preferred_element_type=wide
    )
    inner = jnp.sum(probs * probs_grad, axis=2, keepdims=True)
    inner, shared_two_own = pin((inner, shared_two_own))
    shared_two_all = lax.all_gather(shared_two_own, "dp", axis=0, tiled=True)
    scores_grad = (probs * (probs_grad - inner)).astype(narrow)
    query_grad = (
        jnp.einsum("hts,shd->thd", scores_grad, key_low, preferred_element_type=wide) * scale
    )
    key_grad = (
        jnp.einsum("hts,thd->shd", scores_grad, query_low, preferred_element_type=wide) * scale
    )
    query_grad, down_experts, gate_experts = pin((query_grad, down_experts, gate_experts))
    for experts_of in (down_experts, gate_experts):
        experts_of[1] = swap_core(experts_of[1])
    query_lin_grad = rotate_back(query_grad, cosine, sine).reshape(GROUP, heads * HD).astype(narrow)
    key_lin_grad = rotate_back(key_grad, cosine, sine).reshape(GROUP, heads * HD).astype(narrow)
    value_lin_grad = value_grad.reshape(GROUP, heads * HD).astype(narrow)
    width = heads * HD
    piece = D // n_dp
    sources = ring_sources()
    ring_places = ring_chips()
    lin_grads = jnp.concatenate([query_lin_grad, key_lin_grad, value_lin_grad], axis=1)
    attn_mine, attn_other = attention_grads(
        jnp.stack([at[0] for at in sources] + [at[1] for at in sources]).astype(jnp.int32),
        normed_one,
        lin_grads,
        hidden_grad_low,
        mixed_low,
    )
    attn_other = swap_core(attn_other)
    attn_other, lin_grads, x_steps = pin((attn_other, lin_grads, x_steps))

    def attn_part(step):
        return attn_mine[step].astype(wide) + attn_other[step].astype(wide)

    total = ring_next(attn_part(1).astype(narrow))
    up_experts = weight_grads([(x_steps, up_of[:2])])
    up_experts[1] = swap_core(up_experts[1])
    norm_one_part = sum(
        dot_nt(lin_grads[:, i * width : (i + 1) * width], weight)
        for i, weight in enumerate((q_weight, k_weight, v_weight))
    ).astype(narrow)
    normed_one_grad = plane_scatter(
        [norm_one_part[j * rows : (j + 1) * rows] for j in range(n_tensor)]
    )
    attn_gain_part = jnp.sum(normed_one_grad * hat_one, axis=0)
    scaled_one = normed_one_grad * attn_gain
    input_grad = hidden_grad + inverse_one * (
        scaled_one - hat_one * jnp.mean(scaled_one * hat_one, axis=1, keepdims=True)
    )

    gains = sum_over_plane(
        jnp.concatenate(
            [
                attn_gain_part,
                mlp_gain_part,
                router_grad_part,
                jnp.broadcast_to(squared_own, (128,)),
            ]
        )
    )
    gains, down_experts, gate_experts, up_experts = pin(
        (gains, down_experts, gate_experts, up_experts)
    )

    def small_rows():
        biases = [
            jnp.sum(grad.astype(wide), axis=0)
            for grad in (query_lin_grad, key_lin_grad, value_lin_grad)
        ]
        small = jnp.concatenate([gains, *biases])
        small = small + swap_core(small)
        lanes = 4 * width
        count = -(-small.shape[0] // (8 * lanes)) * 8
        small = jnp.pad(small, (0, count * lanes - small.shape[0])).reshape(count, lanes)
        high = small.astype(narrow)
        return jnp.concatenate([high, (small - high.astype(wide)).astype(narrow)], axis=0)

    expert_down_grad = expert_sum(*down_experts)[None]
    expert_gate_grad = expert_sum(*gate_experts).T[None]
    expert_up_grad = expert_sum(*up_experts).T[None]
    shared_down_grad = shared_down_all.astype(wide)
    shared_gate_grad = turn(shared_two_all, n_dp, 0, f_shared)
    shared_up_grad = turn(shared_two_all, n_dp, 1, f_shared)
    ties = [(), (shared_down_grad,)]
    for step in range(2, chips):
        if step - 2 < len(ties):
            total = after(total, *ties[step - 2])
        total = ring_next((attn_part(step) + total.astype(wide)).astype(narrow))
    total = after(total, input_grad, shared_gate_grad)
    attn_own = (attn_part(0) + total.astype(wide)).astype(narrow)
    attn_held = [jnp.concatenate([attn_own, small_rows()], axis=0)]
    ties = [(shared_up_grad, expert_down_grad), (expert_gate_grad,)]
    swapped, sums = [], None

    def placed(first, last, before):
        blocks, places_at = [], []
        for step in range(first, last):
            blocks += [attn_held[step], swapped[step]]
            places_at += [source * piece for source in sources[step]]
        return assemble(blocks, jnp.stack(places_at), piece, before)

    for step in range(chips - 1):
        swapped.append(swap_core(attn_held[-1]))
        block = ring_next(attn_held[-1])
        if step == 1:
            sums = placed(0, 1, None)
        if step < len(ties):
            block, swapped, sums = pin((block, swapped, sums, ties[step]))[:3]
        attn_held.append(block)
    swapped.append(swap_core(attn_held[-1]))
    q_sum, k_sum, v_sum, o_sum = placed(1, chips, sums)
    small = 0.0
    for chip in range(chips):
        rows_of = sum(
            jnp.where(at == chip, block[piece:].astype(wide), 0.0)
            for block, at in zip(attn_held, ring_places)
        )
        small = small + rows_of
    half = small.shape[0] // 2
    small = (small[:half] + small[half:]).reshape(-1)

    attn_gain_grad, mlp_gain_grad, shared_router_grad = (small[i * D : (i + 1) * D] for i in range(3))
    teacher_loss = small[3 * D] / (valid_count * D)
    biases = small[3 * D + 128 :]
    return (
        result.astype(narrow),
        teacher_loss,
        input_grad,
        attn_gain_grad,
        q_sum,
        biases[:width],
        k_sum,
        biases[width : 2 * width],
        v_sum,
        biases[2 * width : 3 * width],
        o_sum,
        mlp_gain_grad,
        expert_gate_grad,
        expert_up_grad,
        expert_down_grad,
        shared_gate_grad,
        shared_up_grad,
        shared_down_grad,
        shared_router_grad,
    )


def solution(mesh):
    return jax.shard_map(
        shards,
        mesh=mesh,
        in_specs=(
            P(("dp", "tensor"), None),
            P(),
            P(None, "tensor"),
            P("tensor"),
            P(None, "tensor"),
            P("tensor"),
            P(None, "tensor"),
            P("tensor"),
            P("tensor", None),
            P(),
            P("dp", None, "tensor"),
            P("dp", None, "tensor"),
            P("dp", "tensor", None),
            P(None, "tensor"),
            P(None, "tensor"),
            P("tensor", None),
            P(),
            P("dp", None),
            P("dp", None),
            P(),
            P(),
            P(("dp", "tensor"), None),
            P(("dp", "tensor"), None),
        ),
        out_specs=(
            P(("dp", "tensor"), None),
            P(),
            P(("dp", "tensor"), None),
            P(),
            P(None, "tensor"),
            P("tensor"),
            P(None, "tensor"),
            P("tensor"),
            P(None, "tensor"),
            P("tensor"),
            P("tensor", None),
            P(),
            P("dp", None, "tensor"),
            P("dp", None, "tensor"),
            P("dp", "tensor", None),
            P(None, "tensor"),
            P(None, "tensor"),
            P("tensor", None),
            P(),
        ),
        check_vma=False,
    )
```

```python
import functools
import math

import jax
import jax.numpy as jnp
from jax import lax
from jax.experimental import pallas as pl
from jax.experimental.pallas import tpu as pltpu
from jax.sharding import PartitionSpec as P

D = 2048
HD = 128
PROMPT = 512
SLOT = 128
CONTS = 2
GROUP = 768


EPSILON = 1e-06
ROTARY_BASE = 1000000.0
WIDE = jnp.float32
NARROW = jnp.bfloat16
VMEM_BYTES = 60 * 1024 * 1024


def slot_layout(lengths_row, position):
    offset = jnp.maximum(position - PROMPT, 0)
    in_prompt = position < PROMPT
    segment = jnp.where(in_prompt, 0, 1 + offset // SLOT)
    rotary_place = jnp.where(in_prompt, position, PROMPT + offset % SLOT)
    matches = segment[:, None] - 1 == jnp.arange(CONTS, dtype=jnp.int32)[None, :]
    length_here = jnp.sum(jnp.where(matches, lengths_row[None, :], 0), axis=1)
    living = in_prompt | (offset % SLOT < length_here)
    return (segment, rotary_place, living)


def visible_keys(position, segment, living):
    causal = position[None, :] <= position[:, None]
    same_part = (segment[None, :] == segment[:, None]) | (segment[None, :] == 0)
    return causal & same_part & living[None, :]


def rotary_tables(rotary_place):
    freqs = jnp.exp(jnp.arange(HD // 2, dtype=jnp.float32) * (-2.0 * math.log(ROTARY_BASE) / HD))
    angles = rotary_place.astype(jnp.float32)[:, None] * freqs[None, :]
    angles = jnp.concatenate([angles, angles], axis=1)
    return (jnp.cos(angles), jnp.sin(angles))


def rotate(values, cosine, sine):
    half = values.shape[-1] // 2
    flipped = jnp.concatenate([-values[..., half:], values[..., :half]], axis=-1)
    return values * cosine[:, None, :] + flipped * sine[:, None, :]


def rotate_back(grads, cosine, sine):
    half = grads.shape[-1] // 2
    turned = grads * sine[:, None, :]
    flipped = jnp.concatenate([turned[..., half:], -turned[..., :half]], axis=-1)
    return grads * cosine[:, None, :] + flipped


def attention_scores(query_low, key_low, visible, scale):
    scores = (
        jnp.einsum("thd,shd->hts", query_low, key_low, preferred_element_type=jnp.float32) * scale
    )
    return jnp.where(visible[None], scores, -1e30)


def dot_nt(left, right):
    return lax.dot_general(left, right, (((1,), (1,)), ((), ())), preferred_element_type=WIDE)


def dot_nn(left, right):
    return lax.dot_general(left, right, (((1,), (0,)), ((), ())), preferred_element_type=WIDE)


def dot_tn(left, right):
    return lax.dot_general(left, right, (((0,), (0,)), ((), ())), preferred_element_type=WIDE)


def pin(values):
    return lax.optimization_barrier(values)


def after(value, *others):
    return pin((value,) + others)[0]


def flip(value, bit):
    size = lax.axis_size("tensor")
    return lax.ppermute(value, "tensor", [(i, i ^ bit) for i in range(size)])


def split_at(rows):
    return rows // 32 * 16


def plane_gather(value):
    size = lax.axis_size("tensor")
    if size == 4:
        cut = split_at(value.shape[0])
        one, two = flip(value, 1), flip(value, 2)
        low, high = flip(two[:cut], 1), flip(one[cut:], 2)
        return [value, one, two, jnp.concatenate([low, high], axis=0)]
    blocks, bit = [value], 1
    while bit < size:
        blocks = blocks + [flip(block, bit) for block in blocks]
        bit *= 2
    return blocks


def plane_scatter(parts):
    size = lax.axis_size("tensor")
    if size == 4:
        cut = split_at(parts[3].shape[0])
        far = parts[3].astype(NARROW)
        low, high = flip(far[:cut], 1), flip(far[cut:], 2)
        two = jnp.concatenate(
            [(parts[2][:cut].astype(WIDE) + low.astype(WIDE)).astype(NARROW), parts[2][cut:].astype(NARROW)], axis=0
        )
        one = jnp.concatenate(
            [parts[1][:cut].astype(NARROW), (parts[1][cut:].astype(WIDE) + high.astype(WIDE)).astype(NARROW)], axis=0
        )
        return parts[0].astype(WIDE) + flip(one, 1).astype(WIDE) + flip(two, 2).astype(WIDE)
    parts = [part.astype(WIDE) for part in parts]
    bit = size // 2
    while bit >= 1:
        parts = [parts[j] + flip(parts[bit + j].astype(NARROW), bit).astype(WIDE) for j in range(bit)]
        bit //= 2
    return parts[0]


def plane_gather_spare(value):
    if lax.axis_size("tensor") != 4:
        return plane_gather(value)
    one, two = flip(value, 1), flip(value, 2)
    return [value, one, two, flip(one, 2)]


def ring_order(chips):
    odd = list(range(1, chips, 2))
    even = list(range(2, chips, 2))
    return [0] + odd + even[::-1]


def ring_next(value):
    chips = lax.axis_size("dp") // 2
    order = ring_order(chips)
    pairs = [
        (2 * order[i] + c, 2 * order[(i + 1) % chips] + c) for i in range(chips) for c in range(2)
    ]
    return lax.ppermute(value, "dp", pairs)


def swap_core(value):
    size = lax.axis_size("dp")
    return lax.ppermute(value, "dp", [(i, i ^ 1) for i in range(size)])


def both_ways(value, bit):
    n_dp, size = lax.axis_size("dp"), lax.axis_size("tensor")
    pairs = [(d * size + t, (d ^ 1) * size + (t ^ bit)) for d in range(n_dp) for t in range(size)]
    return lax.ppermute(value, ("dp", "tensor"), pairs)


def ring_chips():
    chips = lax.axis_size("dp") // 2
    order = ring_order(chips)
    chip = lax.axis_index("dp") // 2
    sources = []
    for step in range(chips):
        table = [0] * chips
        for place, here in enumerate(order):
            table[here] = order[(place - step) % chips]
        sources.append(jnp.asarray(table, jnp.int32)[chip])
    return sources


def ring_sources():
    core = lax.axis_index("dp") % 2
    return [(2 * chip + core, 2 * chip + 1 - core) for chip in ring_chips()]


def ring_gather(value):
    chips = lax.axis_size("dp") // 2
    held = [value]
    for _ in range(chips - 1):
        held.append(ring_next(held[-1]))
    return [(block, swap_core(block)) for block in held]


def ring_scatter(parts):
    chips = len(parts)
    total = None
    for step in list(range(1, chips)) + [0]:
        mine, other = parts[step]
        here = mine.astype(WIDE) + swap_core(other.astype(NARROW)).astype(WIDE)
        if total is not None:
            here = here + total.astype(WIDE)
        if step == 0:
            return here
        total = ring_next(here.astype(NARROW))


def plane_bits():
    size = lax.axis_size("tensor")
    bits = [1 << i for i in range(size.bit_length() - 1)]
    return bits[:1] + bits[2:], bits[1:2]


def bits_gather(value, bits):
    blocks = [value]
    for bit in bits:
        blocks = blocks + [flip(block, bit) for block in blocks]
    return blocks


def bits_scatter(parts, bits):
    for bit in bits[::-1]:
        half = len(parts) // 2
        parts = [
            parts[j].astype(WIDE) + flip(parts[half + j].astype(NARROW), bit).astype(WIDE)
            for j in range(half)
        ]
    return parts[0]


def bits_offsets(bits):
    offsets = [0]
    for bit in bits:
        offsets = offsets + [offset ^ bit for offset in offsets]
    return offsets


def chain_gather(value):
    held = [value]
    for _ in range(lax.axis_size("dp") // 2 - 1):
        held.append(ring_next(held[-1]))
    return held


def chain_scatter(parts):
    total = None
    for step in list(range(1, len(parts))) + [0]:
        here = parts[step].astype(WIDE)
        if total is not None:
            here = here + total.astype(WIDE)
        if step == 0:
            return here
        total = ring_next(here.astype(NARROW))


def sum_over_plane(vector):
    bit = 1
    while bit < lax.axis_size("tensor"):
        vector = vector + flip(vector, bit)
        bit *= 2
    return vector


class Copies:
    def __init__(self, sems):
        self.sems, self.used = sems, 0

    def start(self, source, target):
        copy = pltpu.make_async_copy(source, target, self.sems.at[self.used])
        self.used += 1
        copy.start()
        return copy


def weight_places(parts, count, cut):
    half = count // 2
    left = parts - cut
    chunks = [
        [(b, 0, cut, b * cut) for b in range(half)],
        [(b, 0, cut, (b - half) * cut) for b in range(half, count)],
        [(b, cut, left, b * left) for b in range(count)],
    ]
    sizes = [half * cut, half * cut, count * left]
    starts = [0, half * cut, count * cut]
    return [
        (start, size, [(b, at, n, start + place) for b, at, n, place in chunk])
        for start, size, chunk in zip(starts, sizes, chunks)
    ]


def piece_moves(moves, piece_rows):
    found = []
    for block, at, size, place in moves:
        first = 0
        for piece, (owner, rows) in enumerate(piece_rows):
            if owner != block:
                continue
            low, high = max(at, first), min(at + size, first + rows)
            if low < high:
                found.append((piece, low - first, high - low, place + low - at))
            first += rows
    return found


def flat_pieces(weights):
    pieces = [piece for blocks in weights for block in blocks for piece in block]
    rows = [
        [(b, piece.shape[0]) for b, block in enumerate(blocks) for piece in block]
        for blocks in weights
    ]
    return pieces, rows


def column(mix):
    return mix[...].T[:, :1]


def forward_body(rows, count, places, piece_rows, *refs):
    x_refs, refs = refs[:count], refs[count:]
    weights = []
    for held in piece_rows:
        weights.append(refs[: len(held)])
        refs = refs[len(held) :]
    mix_one, mix_two, router = refs[:3]
    out_refs, refs = refs[3 : 3 + count], refs[3 + count :]
    kept_refs, factor_ref, refs = refs[:9], refs[9], refs[10:]
    xs, gate_s, up_s, down_s, ys = refs[:5]
    kept, sems = refs[5:14], refs[14]
    copies = Copies(sems)
    x_in = [copies.start(x_refs[i], xs.at[pl.ds(i * rows, rows)]) for i in range(count)]
    w_in = [
        [
            [
                copies.start(weights[n][b].at[pl.ds(at, size)], held.at[pl.ds(place, size)])
                for b, at, size, place in piece_moves(moves, piece_rows[n])
            ]
            for n, held in enumerate((gate_s, up_s, down_s))
        ]
        for _, _, moves in places
    ]
    for copy in x_in:
        copy.wait()
    x = xs[...]
    router_gate = jax.nn.sigmoid(jnp.sum(x.astype(WIDE) * router[...], axis=1, keepdims=True))
    factor_ref[...] = router_gate
    factors = (column(mix_one), column(mix_two), router_gate)
    away, products, total = [], [], None
    for at in range(len(places) + 1):
        if at < len(places):
            start, size, _ = places[at]
            for copy in w_in[at][0] + w_in[at][1]:
                copy.wait()
        if at > 0:
            for copy in w_in[at - 1][2]:
                copy.wait()
        if at < len(places):
            products.append(
                (dot_nt(x, gate_s[pl.ds(start, size)]), dot_nt(x, up_s[pl.ds(start, size)]))
            )
        if at > 0:
            gate_in, up_in = products[at - 1]
            hidden = (gate_in * jax.nn.sigmoid(gate_in) * up_in * factors[at - 1]).astype(NARROW)
            for n, value in enumerate((gate_in, up_in, hidden)):
                kept[3 * n + at - 1][...] = value.astype(NARROW)
            start, size, _ = places[at - 1]
            part = dot_nn(hidden, down_s[pl.ds(start, size)])
            total = part if total is None else total + part
            for n in range(3):
                away.append(copies.start(kept[3 * n + at - 1], kept_refs[3 * n + at - 1]))
    ys[...] = total.astype(NARROW)
    away += [copies.start(ys.at[pl.ds(i * rows, rows)], out_refs[i]) for i in range(count)]
    for copy in away:
        copy.wait()


def forward_step(x_blocks, weights, mix_one, mix_two, router, cut):
    count, (rows, width) = len(x_blocks), x_blocks[0].shape
    pieces, piece_rows = flat_pieces(weights)
    blocks, parts = len(weights[0]), sum(piece.shape[0] for piece in weights[0][0])
    places = weight_places(parts, blocks, cut)
    total, hidden = count * rows, blocks * parts
    anywhere, local = pl.BlockSpec(memory_space=pl.ANY), pl.BlockSpec(memory_space=pltpu.VMEM)
    shape = jax.ShapeDtypeStruct
    outs = pl.pallas_call(
        functools.partial(forward_body, rows, count, places, piece_rows),
        out_shape=[shape((rows, width), NARROW)] * count
        + [shape((total, size), NARROW) for _ in range(3) for _, size, _ in places]
        + [shape((total, 1), WIDE)],
        in_specs=[anywhere] * (count + len(pieces)) + [local] * 3,
        out_specs=[anywhere] * (count + 9) + [local],
        scratch_shapes=[pltpu.VMEM((total, width), NARROW)]
        + [pltpu.VMEM((hidden, width), NARROW)] * 3
        + [pltpu.VMEM((total, width), NARROW)]
        + [pltpu.VMEM((total, size), NARROW) for _ in range(3) for _, size, _ in places]
        + [pltpu.SemaphoreType.DMA((2 * count + 3 * len(pieces) + 9,))],
        compiler_params=pltpu.CompilerParams(vmem_limit_bytes=VMEM_BYTES),
        cost_estimate=pl.CostEstimate(
            flops=6 * total * hidden * width,
            bytes_accessed=6 * hidden * width + 4 * total * width + 6 * total * hidden,
            transcendentals=total * hidden,
        ),
        name="ffn_forward",
    )(*x_blocks, *pieces, mix_one, mix_two, router)
    outs, kept = outs[:count], outs[count:]
    return outs, kept[:3], kept[3:6], kept[6:9], kept[9]


def backward_body(rows, count, places, piece_rows, *refs):
    g_refs, refs = refs[:count], refs[count:]
    weights = []
    for held in piece_rows:
        weights.append(refs[: len(held)])
        refs = refs[len(held) :]
    kept_refs, refs = refs[:6], refs[6:]
    mix_one, mix_two, rg, router = refs[:4]
    out_refs, refs = refs[4 : 4 + count], refs[4 + count :]
    grad_refs, logit_ref, refs = refs[:6], refs[6], refs[7:]
    xs, gate_s, up_s, down_s, ys = refs[:5]
    kept, sems = refs[5:11], refs[11]
    copies = Copies(sems)
    g_in = [copies.start(g_refs[i], xs.at[pl.ds(i * rows, rows)]) for i in range(count)]
    w_in, kept_in = [], []
    for at, (start, size, moves) in enumerate(places):
        arriving = []
        for n, held in ((2, down_s), (0, gate_s), (1, up_s)):
            arriving.append(
                [
                    copies.start(weights[n][b].at[pl.ds(first, n_rows)], held.at[pl.ds(place, n_rows)])
                    for b, first, n_rows, place in piece_moves(moves, piece_rows[n])
                ]
            )
            if n == 2:
                kept_in.append([copies.start(kept_refs[3 * i + at], kept[3 * i + at]) for i in range(2)])
        w_in.append(arriving)
    for copy in g_in:
        copy.wait()
    grad = xs[...]
    factors = (column(mix_one), column(mix_two), rg[...])
    away, products, total = [], [], None
    for at in range(len(places) + 1):
        if at < len(places):
            start, size, _ = places[at]
            for copy in w_in[at][0] + kept_in[at]:
                copy.wait()
        if at > 0:
            for copy in w_in[at - 1][1] + w_in[at - 1][2]:
                copy.wait()
        if at < len(places):
            products.append(dot_nt(grad, down_s[pl.ds(start, size)]))
        if at > 0:
            grad_hidden = products[at - 1] * factors[at - 1]
            gate_in, up_in = kept[at - 1][...].astype(WIDE), kept[2 + at][...].astype(WIDE)
            squash = jax.nn.sigmoid(gate_in)
            up_grad = grad_hidden * gate_in * squash
            gate_grad = grad_hidden * up_in * squash * (1.0 + gate_in * (1.0 - squash))
            logit = jnp.sum(up_grad * up_in, axis=1, keepdims=True)
            gate_grad, up_grad = gate_grad.astype(NARROW), up_grad.astype(NARROW)
            kept[at - 1][...] = gate_grad
            kept[2 + at][...] = up_grad
            start, size, _ = places[at - 1]
            span = pl.ds(start, size)
            part = dot_nn(gate_grad, gate_s[span]) + dot_nn(up_grad, up_s[span])
            total = part if total is None else total + part
            for n in range(2):
                away.append(copies.start(kept[3 * n + at - 1], grad_refs[3 * n + at - 1]))
    logit = logit * (1.0 - rg[...])
    logit_ref[...] = logit
    ys[...] = (total + logit * router[...]).astype(NARROW)
    away += [copies.start(ys.at[pl.ds(i * rows, rows)], out_refs[i]) for i in range(count)]
    for copy in away:
        copy.wait()


def backward_step(g_blocks, weights, gate_in, up_in, mix_one, mix_two, rg, router, cut):
    count, (rows, width) = len(g_blocks), g_blocks[0].shape
    pieces, piece_rows = flat_pieces(weights)
    blocks, parts = len(weights[0]), sum(piece.shape[0] for piece in weights[0][0])
    places = weight_places(parts, blocks, cut)
    total, hidden = count * rows, blocks * parts
    anywhere, local = pl.BlockSpec(memory_space=pl.ANY), pl.BlockSpec(memory_space=pltpu.VMEM)
    shape = jax.ShapeDtypeStruct
    outs = pl.pallas_call(
        functools.partial(backward_body, rows, count, places, piece_rows),
        out_shape=[shape((rows, width), NARROW)] * count
        + [shape((total, size), NARROW) for _ in range(2) for _, size, _ in places]
        + [shape((total, 1), WIDE)],
        in_specs=[anywhere] * (count + len(pieces) + 6) + [local] * 4,
        out_specs=[anywhere] * (count + 6) + [local],
        scratch_shapes=[pltpu.VMEM((total, width), NARROW)]
        + [pltpu.VMEM((hidden, width), NARROW)] * 3
        + [pltpu.VMEM((total, width), NARROW)]
        + [pltpu.VMEM((total, size), NARROW) for _ in range(2) for _, size, _ in places]
        + [pltpu.SemaphoreType.DMA((2 * count + 3 * len(pieces) + 12,))],
        compiler_params=pltpu.CompilerParams(vmem_limit_bytes=VMEM_BYTES),
        cost_estimate=pl.CostEstimate(
            flops=6 * total * hidden * width,
            bytes_accessed=6 * hidden * width + 4 * total * width + 8 * total * hidden,
            transcendentals=total * hidden,
        ),
        name="ffn_backward",
    )(
        *g_blocks,
        *pieces,
        *gate_in,
        *up_in,
        mix_one,
        mix_two,
        rg,
        router,
    )
    outs, kept = outs[:count], outs[count:]
    return outs, kept[:3], kept[3:6], kept[6]


def weight_body(rows, steps, blocks, shape, plan, *refs):
    groups, names = len(shape), sum(shape)
    x_refs, refs = refs[: groups * steps * blocks], refs[groups * steps * blocks :]
    left_refs, refs = refs[: names * steps], refs[names * steps :]
    out_refs, (xs, ls, os, sems) = refs[:-4], refs[-4:]
    copies = Copies(sems)
    part = blocks * rows
    x_in, left_in, n = [], [], 0
    for group, amount in enumerate(shape):
        arriving = []
        for i in range(steps * blocks):
            source = x_refs[group * steps * blocks + i]
            arriving.append(copies.start(source, xs.at[group, pl.ds(i * rows, rows)]))
        x_in.append(arriving)
        for _ in range(amount):
            left_in.append(
                [
                    copies.start(left_refs[n * steps + s], ls.at[n, pl.ds(s * part, part)])
                    for s in range(steps)
                ]
            )
            n += 1
    away, n = [], 0
    for group, amount in enumerate(shape):
        for copy in x_in[group]:
            copy.wait()
        for _ in range(amount):
            for copy in left_in[n]:
                copy.wait()
            os[n] = dot_tn(ls[n], xs[group]).astype(NARROW)
            for first, size, out, place in plan[n]:
                target = out_refs[out].at[pl.ds(place, size)]
                away.append(copies.start(os.at[n, pl.ds(first, size)], target))
            n += 1
    for copy in away:
        copy.wait()


def weight_grads(groups, plan=None, light=False):
    steps, blocks = len(groups[0][0]), len(groups[0][0][0])
    shape = [len(lefts) for _, lefts in groups]
    names = sum(shape)
    rows, width = groups[0][0][0][0].shape
    total, hidden = steps * blocks * rows, groups[0][1][0][0].shape[1]
    plan = plan or [[(0, hidden, n, 0)] for n in range(names)]
    sizes = {}
    for moves in plan:
        for _, size, out, place in moves:
            sizes[out] = max(sizes.get(out, 0), place + size)
    anywhere = pl.BlockSpec(memory_space=pl.ANY)
    outs = pl.pallas_call(
        functools.partial(weight_body, rows, steps, blocks, shape, plan),
        out_shape=[jax.ShapeDtypeStruct((sizes[out], width), NARROW) for out in range(len(sizes))],
        in_specs=[anywhere] * (steps * (len(groups) * blocks + names)),
        out_specs=[anywhere] * len(sizes),
        scratch_shapes=[
            pltpu.VMEM((len(groups), total, width), NARROW),
            pltpu.VMEM((names, total, hidden), NARROW),
            pltpu.VMEM((names, hidden, width), NARROW),
            pltpu.SemaphoreType.DMA(
                (steps * (len(groups) * blocks + names) + sum(len(moves) for moves in plan),)
            ),
        ],
        compiler_params=pltpu.CompilerParams(vmem_limit_bytes=VMEM_BYTES),
        cost_estimate=pl.CostEstimate(
            flops=0 if light else 2 * names * total * hidden * width,
            bytes_accessed=0 if light else 2 * total * width + 2 * names * (total + width) * hidden,
            transcendentals=0,
        ),
        name="weight_grads",
    )(
        *[b for x_blocks, _ in groups for step in x_blocks for b in step],
        *[a for _, lefts in groups for left in lefts for a in left],
    )
    return list(outs)


def attention_body(piece, order, normed, grads, hidden, mixed, mine_ref, other_ref):
    width = mixed.shape[1]
    half = mine_ref.shape[0]
    for i in range(2 * half):
        target = mine_ref if i < half else other_ref
        span = pl.ds(pl.multiple_of(order[i] * piece, 128), piece)
        target[i % half, :, : 3 * width] = dot_tn(normed[:, span], grads[...]).astype(NARROW)
        target[i % half, :, 3 * width :] = dot_tn(hidden[:, span], mixed[...]).astype(NARROW)


def attention_grads(order, normed, grads, hidden, mixed):
    count = order.shape[0]
    group, depth = normed.shape
    width = mixed.shape[1]
    piece = depth // count
    local = pl.BlockSpec(memory_space=pltpu.VMEM)
    return pl.pallas_call(
        functools.partial(attention_body, piece),
        out_shape=[jax.ShapeDtypeStruct((count // 2, piece, 4 * width), NARROW)] * 2,
        in_specs=[pl.BlockSpec(memory_space=pltpu.SMEM)] + [local] * 4,
        out_specs=[local] * 2,
        compiler_params=pltpu.CompilerParams(vmem_limit_bytes=VMEM_BYTES),
        cost_estimate=pl.CostEstimate(
            flops=8 * group * depth * width,
            bytes_accessed=4 * group * depth + 8 * group * width + 8 * depth * width,
            transcendentals=0,
        ),
        name="attention_grads",
    )(order, normed, grads, hidden, mixed)


def assemble_body(count, rows, *refs):
    places, blocks, refs = refs[0], refs[1 : 1 + count], refs[1 + count :]
    outs, (held, straight, turned, sems) = refs[-8:-4], refs[-4:]
    copies = Copies(sems)
    width = straight.shape[3]
    moved = []
    for i in range(count):
        moved.append(copies.start(blocks[i].at[pl.ds(0, rows)], held.at[i]))
    away = []
    for i in range(count):
        moved[i].wait()
        place = pl.multiple_of(places[i], 128)
        for j in range(3):
            straight[i, j] = held[i, :, j * width : (j + 1) * width].astype(WIDE)
            away.append(copies.start(straight.at[i, j], outs[j].at[pl.ds(place, rows)]))
        turned[i] = held[i, :, 3 * width :].astype(WIDE).T
        away.append(copies.start(turned.at[i], outs[3].at[:, pl.ds(place, rows)]))
    for copy in away:
        copy.wait()


def assemble(blocks, places, rows, before):
    count, wide = len(blocks), blocks[0].shape[1]
    width = wide // 4
    depth = D
    shapes = [jax.ShapeDtypeStruct((depth, width), WIDE)] * 3
    anywhere = pl.BlockSpec(memory_space=pl.ANY)
    before = [] if before is None else list(before)
    return pl.pallas_call(
        functools.partial(assemble_body, count, rows),
        out_shape=shapes + [jax.ShapeDtypeStruct((width, depth), WIDE)],
        in_specs=[pl.BlockSpec(memory_space=pltpu.SMEM)] + [anywhere] * (count + len(before)),
        out_specs=[anywhere] * 4,
        scratch_shapes=[
            pltpu.VMEM((count, rows, wide), NARROW),
            pltpu.VMEM((count, 3, rows, width), WIDE),
            pltpu.VMEM((count, width, rows), WIDE),
            pltpu.SemaphoreType.DMA((5 * count,)),
        ],
        input_output_aliases={1 + count + i: i for i in range(len(before))},
        compiler_params=pltpu.CompilerParams(vmem_limit_bytes=VMEM_BYTES),
        name="assemble",
    )(places, *blocks, *before)


def turn_body(x_ref, out_ref):
    count, _, rows, width = x_ref.shape
    out_ref[...] = x_ref[...].reshape(count * rows, width).astype(WIDE).T


def turn(value, count, which, rows):
    width = value.shape[1]
    value = value.reshape(count, 2, -1, width)
    if value.shape[2] != rows or (count * rows) % 128:
        return value[:, which, :rows].reshape(count * rows, width).T.astype(WIDE)
    return pl.pallas_call(
        turn_body,
        grid=(width // 256,),
        out_shape=jax.ShapeDtypeStruct((width, count * rows), WIDE),
        in_specs=[pl.BlockSpec((count, 1, rows, 256), lambda i: (0, which, 0, i))],
        out_specs=pl.BlockSpec((256, count * rows), lambda i: (i, 0)),
        compiler_params=pltpu.CompilerParams(vmem_limit_bytes=VMEM_BYTES),
        name="turn",
    )(value)


def shards(
    hidden_in,
    attn_gain,
    q_weight,
    q_bias,
    k_weight,
    k_bias,
    v_weight,
    v_bias,
    o_weight,
    mlp_gain,
    expert_gate,
    expert_up,
    expert_down,
    shared_gate,
    shared_up,
    shared_down,
    shared_router,
    routes,
    gate_weights,
    lengths,
    loss_mask,
    teacher,
    cotangent,
):
    wide = WIDE
    narrow = NARROW
    data_index = lax.axis_index("dp")
    slice_index = lax.axis_index("tensor")
    n_dp = lax.axis_size("dp")
    n_tensor = lax.axis_size("tensor")
    rows = hidden_in.shape[0]
    heads = q_weight.shape[1] // HD
    f_expert = expert_gate.shape[2]
    f_shared = shared_gate.shape[1] // n_dp
    f_pad = -(-f_shared // 16) * 16
    scale = 1.0 / math.sqrt(HD)

    position = jnp.concatenate(
        [(slice_index ^ j) * rows + jnp.arange(rows, dtype=jnp.int32) for j in range(n_tensor)]
    )
    own_lengths = lax.dynamic_index_in_dim(lengths, data_index, 0, keepdims=False)
    segment, rotary_place, living = slot_layout(own_lengths, position)
    visible = visible_keys(position, segment, living)
    cosine, sine = rotary_tables(rotary_place)
    every = jnp.arange(GROUP, dtype=jnp.int32)
    living_all = jax.vmap(lambda row: slot_layout(row, every)[2])(lengths)
    valid_count = jnp.sum((living_all.reshape(-1) & (loss_mask == 1)).astype(wide))
    own_mask = lax.dynamic_slice_in_dim(loss_mask, data_index * GROUP + slice_index * rows, rows, 0)
    valid_own = living[:rows] & (own_mask == 1)

    own_input = hidden_in.astype(wide)
    inverse_one = lax.rsqrt(jnp.mean(own_input * own_input, axis=1, keepdims=True) + EPSILON)
    hat_one = own_input * inverse_one
    normed_own = (hat_one * attn_gain).astype(narrow)

    def pack(expert_rows, shared_rows):
        if f_pad != f_shared:
            shared_rows = jnp.pad(shared_rows, ((0, f_pad - f_shared), (0, 0)))
        return jnp.concatenate([expert_rows, shared_rows], axis=0)

    shared_at = data_index * f_shared
    own_gate = pack(
        expert_gate[0].T, lax.dynamic_slice_in_dim(shared_gate, shared_at, f_shared, 1).T
    )
    own_up = pack(expert_up[0].T, lax.dynamic_slice_in_dim(shared_up, shared_at, f_shared, 1).T)
    own_down = pack(expert_down[0], lax.dynamic_slice_in_dim(shared_down, shared_at, f_shared, 0))

    w_bits, r_bits = plane_bits()

    def both_cores(blocks):
        return blocks + [swap_core(block) for block in blocks]

    staged = n_tensor == 4 and n_dp == 8
    if staged:
        cut = split_at(own_down.shape[0])
        low = flip((expert_down[0] if cut <= f_expert else own_down)[:cut], w_bits[0])
        one, two = flip(normed_own, 1), flip(normed_own, 2)
        one, two, low, own_gate, own_down = pin((one, two, low, own_gate, own_down))
        normed_one_blocks = [normed_own, one, two, flip(one, 2)]
        high = flip(own_down[cut:], w_bits[0])
    else:
        normed_one_blocks = plane_gather(normed_own)
        high = own_down
    gate_blocks = bits_gather(own_gate, w_bits)
    normed_one = jnp.concatenate(normed_one_blocks, axis=0)

    row_slices = [slice_index ^ offset for offset in bits_offsets(r_bits)]
    mixing = jnp.sum(
        jnp.where(
            routes[None, :, :] == jnp.arange(n_dp, dtype=jnp.int32)[:, None, None],
            gate_weights[None, :, :],
            0.0,
        ),
        axis=2,
    )
    mixing = after(mixing, normed_one_blocks[-1])
    mixing_all = jnp.stack(chain_gather(mixing))
    experts = jnp.arange(n_dp, dtype=jnp.int32)
    slices = jnp.arange(n_tensor, dtype=jnp.int32)

    def mixing_of(expert):
        chosen = jnp.sum(
            jnp.where((experts == expert)[None, :, None], mixing_all, 0.0), axis=1
        ).reshape(-1, n_tensor, rows)
        chosen = jnp.stack(
            [jnp.sum(jnp.where((slices == at)[None, :, None], chosen, 0.0), axis=1) for at in row_slices],
            axis=1,
        )
        chosen = chosen.reshape(-1, 1, len(row_slices) * rows)
        return jnp.broadcast_to(chosen, (chosen.shape[0], 8, chosen.shape[2]))

    mix_one, mix_two = mixing_of(data_index), mixing_of(data_index ^ 1)

    query_lin = dot_nn(normed_one, q_weight) + q_bias
    key_lin = dot_nn(normed_one, k_weight) + k_bias
    value_low = (dot_nn(normed_one, v_weight) + v_bias).astype(narrow).reshape(GROUP, heads, HD)
    query_low = rotate(query_lin.reshape(GROUP, heads, HD), cosine, sine).astype(narrow)
    key_low = rotate(key_lin.reshape(GROUP, heads, HD), cosine, sine).astype(narrow)
    scores = attention_scores(query_low, key_low, visible, scale)
    top_score = jnp.max(scores, axis=2, keepdims=True)
    expo = jnp.exp(scores - top_score)
    total_expo = jnp.sum(expo, axis=2, keepdims=True)
    log_total = top_score + jnp.log(total_expo)
    probs_low = (expo / total_expo).astype(narrow)
    mixed = jnp.einsum("hts,shd->thd", probs_low, value_low, preferred_element_type=wide)
    mixed_low = mixed.reshape(GROUP, heads * HD).astype(narrow)
    own_swaps = [swap_core(own) for own in (own_gate, own_up, own_down)]
    mix_one, mix_two = ([mix[i] for i in range(n_dp // 2)] for mix in (mix_one, mix_two))
    mixed_low, mix_one, mix_two, own_swaps = pin((mixed_low, mix_one, mix_two, own_swaps))
    head_part = dot_nn(mixed_low, o_weight).astype(narrow)
    parts = [head_part[j * rows : (j + 1) * rows] for j in range(n_tensor)]
    if n_tensor == 4:
        far = [flip(part, 2) for part in parts[2:]]
        near = (parts[1].astype(wide) + far[1].astype(wide)).astype(narrow)
        near, gate_blocks, own_up, high = pin((near, gate_blocks, own_up, high))
        attn_own = parts[0].astype(wide) + far[0].astype(wide) + flip(near, 1).astype(wide)
    else:
        attn_own = plane_scatter(parts)

    hidden_mid = own_input + attn_own
    inverse_two = lax.rsqrt(jnp.mean(hidden_mid * hidden_mid, axis=1, keepdims=True) + EPSILON)
    hat_two = hidden_mid * inverse_two
    normed_two = (hat_two * mlp_gain).astype(narrow)
    chips = n_dp // 2
    x_chain = [normed_two, ring_next(normed_two)]
    x_steps = [bits_gather(normed_two, r_bits)]
    if staged:
        up_low = flip(own_up[:cut], w_bits[0])
        x_chain[1], x_steps, own_up = pin((x_chain[1], x_steps, own_up))
        x_chain.append(ring_next(x_chain[1]))
        x_steps.append(bits_gather(x_chain[1], r_bits))
        up_high = flip(own_up[cut:], w_bits[0])
        x_chain[2], x_steps, up_low = pin((x_chain[2], x_steps, up_low))
        up_high = after(up_high, x_chain[2])
        x_chain.append(ring_next(x_chain[2]))
        x_steps.append(bits_gather(x_chain[2], r_bits))
        x_steps.append(bits_gather(x_chain[3], r_bits))
        arrived = ([gate_blocks[1]], [up_low, up_high], [low, high])
        weights = [
            [[own], pieces, [swapped], [swap_core(piece) for piece in pieces]]
            for own, pieces, swapped in zip((own_gate, own_up, own_down), arrived, own_swaps)
        ]
    else:
        while len(x_chain) < chips:
            x_chain.append(ring_next(x_chain[-1]))
        x_steps += [bits_gather(block, r_bits) for block in x_chain[1:]]
        up_blocks, down_blocks = bits_gather(own_up, w_bits), bits_gather(own_down, w_bits)
        weights = [
            [[block] for block in blocks + [swapped] + [swap_core(block) for block in blocks[1:]]]
            for blocks, swapped in zip((gate_blocks, up_blocks, down_blocks), own_swaps)
        ]
    n_blocks, n_hidden = len(weights[0]), len(weights[0]) // 2
    places = weight_places(f_expert + f_shared, n_blocks, f_expert)

    router_row = shared_router.astype(wide)[None]
    forward, out_sums, total = {}, {}, None
    order = list(range(1, chips)) + [0]
    for place, step in enumerate(order):
        x, ready = x_steps[step], []
        if place == 0:
            ready = [x_chain[order[1]], *x_steps[0]]
        if place >= 1:
            ready = list(forward[order[place - 1]][0])
            ready += x_steps[order[min(place + 1, chips - 1)]]
        if place >= 2:
            done = order[place - 2]
            out_sums[done] = bits_scatter(forward[done][0], r_bits)
            ready.append(out_sums[done])
            if total is not None:
                ready.append(total)
        x = list(lax.optimization_barrier((*x, *ready)))
        if place >= 2:
            kept = x[len(x) - (2 if total is not None else 1) :]
            here = kept[0].astype(wide)
            if total is not None:
                here = here + kept[1].astype(wide)
            total = ring_next(here.astype(narrow))
        x = x[: len(x_steps[step])]
        forward[step] = forward_step(
            x, weights, mix_one[step], mix_two[step], router_row, f_expert
        )
    for done in order[-2:]:
        out_sums[done] = bits_scatter(forward[done][0], r_bits)
    total = ring_next((out_sums[order[-2]].astype(wide) + total.astype(wide)).astype(narrow))
    branch_own = out_sums[0].astype(wide) + total.astype(wide)
    result = hidden_mid + branch_own

    difference = result - teacher.astype(wide)
    squared_own = jnp.sum(jnp.where(valid_own[:, None], difference * difference, 0.0))
    result_grad = cotangent.astype(wide) + jnp.where(
        valid_own[:, None], difference * (2.0 / (valid_count * D)), 0.0
    )
    grad_own = result_grad.astype(narrow)

    def core_parts(mine, other, first, size):
        return [
            mine[first + j * size : first + (j + 1) * size].astype(wide)
            + other[first + j * size : first + (j + 1) * size].astype(wide)
            for j in range(n_hidden)
        ]

    def shared_sum(parts):
        return bits_scatter(parts, w_bits).astype(narrow)

    def expert_sum(mine, other):
        return bits_scatter(core_parts(mine, other, 0, f_expert), w_bits)

    hidden_of = [[forward[step][3][part] for step in range(chips)] for part in range(3)]
    g_chain = chain_gather(grad_own)
    g_steps = [bits_gather(block, r_bits) for block in g_chain]
    backward, dx_sums, total = [], {}, None
    for step in range(chips):
        ready = []
        if step + 1 < chips:
            ready.append(g_chain[step + 1])
        if step >= 1:
            ready.append(backward[step - 1][0])
        if step >= 2:
            dx_sums[step - 2] = bits_scatter(backward[step - 2][0], r_bits)
            ready.append(dx_sums[step - 2])
        g, ready = pin((g_steps[step], ready))
        if step >= 2:
            dx_sums[step - 2] = ready[2 if step + 1 < chips else 1]
        backward.append(
            backward_step(
                g,
                weights,
                forward[step][1],
                forward[step][2],
                mix_one[step],
                mix_two[step],
                forward[step][4],
                router_row,
                f_expert,
            )
        )
    gate_of, up_of = (
        [[backward[step][n][part] for step in range(chips)] for part in range(3)] for n in (1, 2)
    )
    for step in range(1, chips - 2):
        here = dx_sums[step].astype(wide)
        total = ring_next((here if total is None else here + total.astype(wide)).astype(narrow))
    dx_sums[chips - 2] = bits_scatter(backward[chips - 2][0], r_bits)
    x_steps, g_steps, dx_sums[chips - 2], total, _ = pin(
        (x_steps, g_steps, dx_sums[chips - 2], total, backward[-1][0])
    )
    near, far = n_blocks, n_blocks + 1
    plan = [[(b * f_pad, f_pad, b, 0) for b in range(n_blocks)]]
    plan += [
        [
            (b * f_pad, f_pad, near if b < n_hidden else far, (b % n_hidden * 2 + n) * f_pad)
            for b in range(n_blocks)
        ]
        for n in range(2)
    ]
    *down_pieces, shared_mine, shared_other = weight_grads(
        [(g_steps, [hidden_of[2]]), (x_steps, [gate_of[2], up_of[2]])], plan
    )
    total = ring_next((dx_sums[chips - 2].astype(wide) + total.astype(wide)).astype(narrow))
    dx_sums[chips - 1] = bits_scatter(backward[chips - 1][0], r_bits)
    g_steps, dx_sums[chips - 1], total, shared_mine, shared_other, down_pieces = pin(
        (g_steps, dx_sums[chips - 1], total, shared_mine, shared_other, down_pieces)
    )
    here = (dx_sums[chips - 1].astype(wide) + total.astype(wide)).astype(narrow)
    here, g_steps, down_pieces = pin((here, g_steps, down_pieces))
    total = ring_next(here)
    if n_hidden == 2:
        bit = w_bits[0]
        parts = [
            down_pieces[0],
            flip(down_pieces[1], bit),
            swap_core(down_pieces[2]),
            both_ways(down_pieces[3], bit),
        ]
        down_experts = weight_grads([(g_steps, hidden_of[:2])])
        total, parts, down_experts = pin((total, parts, down_experts))
        shared_down_own = sum(part.astype(wide) for part in parts)[:f_shared].astype(narrow)
    else:
        parts = [
            mine.astype(wide) + swap_core(other).astype(wide)
            for mine, other in zip(down_pieces[:n_hidden], down_pieces[n_hidden:])
        ]
        down_experts = weight_grads([(g_steps, hidden_of[:2])])
        shared_down_own = shared_sum(parts)[:f_shared]
    shared_down_all = lax.all_gather(shared_down_own, "dp", axis=0, tiled=True)
    normed_two_grad = dx_sums[0].astype(wide) + total.astype(wide)

    grad_wide = grad_own.astype(wide)
    mlp_gain_part = jnp.sum(normed_two_grad * hat_two, axis=0)
    scaled_two = normed_two_grad * mlp_gain
    hidden_grad = grad_wide + inverse_two * (
        scaled_two - hat_two * jnp.mean(scaled_two * hat_two, axis=1, keepdims=True)
    )
    router_grad_part = sum(
        jnp.sum(backward[step][3][i * rows : (i + 1) * rows] * block.astype(wide), axis=0)
        for step in range(chips)
        for i, block in enumerate(x_steps[step])
    )
    own_low = hidden_grad.astype(narrow)
    if n_tensor == 4:
        own_low, x_steps = pin((own_low, x_steps))
        shared_other = swap_core(shared_other)
        one, two = flip(own_low, 1), flip(own_low, 2)
        gate_experts = weight_grads([(x_steps, gate_of[:2])])
        one, two, gate_experts, shared_mine, shared_other = pin(
            (one, two, gate_experts, shared_mine, shared_other)
        )
        grad_blocks = [own_low, one, two, flip(one, 2)]
    else:
        gate_experts = weight_grads([(x_steps, gate_of[:2])])
        shared_other = swap_core(shared_other)
        grad_blocks = plane_gather(own_low)
    both = core_parts(shared_mine, shared_other, 0, 2 * f_pad)
    shared_two_own = shared_sum([both[0]] + [part.astype(narrow) for part in both[1:]])
    grad_blocks, gate_experts = pin((grad_blocks, gate_experts))
    hidden_grad_low = jnp.concatenate(grad_blocks, axis=0)

    mixed_grad = dot_nt(hidden_grad_low, o_weight).astype(narrow).reshape(GROUP, heads, HD)
    scores_again = attention_scores(query_low, key_low, visible, scale)
    probs = jnp.exp(scores_again - log_total)
    probs_grad = jnp.einsum("thd,shd->hts", mixed_grad, value_low, preferred_element_type=wide)
    value_grad = jnp.einsum(
        "hts,thd->shd", probs.astype(narrow), mixed_grad, preferred_element_type=wide
    )
    inner = jnp.sum(probs * probs_grad, axis=2, keepdims=True)
    inner, shared_two_own = pin((inner, shared_two_own))
    shared_two_all = lax.all_gather(shared_two_own, "dp", axis=0, tiled=True)
    scores_grad = (probs * (probs_grad - inner)).astype(narrow)
    query_grad = (
        jnp.einsum("hts,shd->thd", scores_grad, key_low, preferred_element_type=wide) * scale
    )
    key_grad = (
        jnp.einsum("hts,thd->shd", scores_grad, query_low, preferred_element_type=wide) * scale
    )
    query_grad, down_experts, gate_experts = pin((query_grad, down_experts, gate_experts))
    for experts_of in (down_experts, gate_experts):
        experts_of[1] = swap_core(experts_of[1])
    query_lin_grad = rotate_back(query_grad, cosine, sine).reshape(GROUP, heads * HD).astype(narrow)
    key_lin_grad = rotate_back(key_grad, cosine, sine).reshape(GROUP, heads * HD).astype(narrow)
    value_lin_grad = value_grad.reshape(GROUP, heads * HD).astype(narrow)
    width = heads * HD
    piece = D // n_dp
    sources = ring_sources()
    ring_places = ring_chips()
    lin_grads = jnp.concatenate([query_lin_grad, key_lin_grad, value_lin_grad], axis=1)
    attn_mine, attn_other = attention_grads(
        jnp.stack([at[0] for at in sources] + [at[1] for at in sources]).astype(jnp.int32),
        normed_one,
        lin_grads,
        hidden_grad_low,
        mixed_low,
    )
    attn_other = swap_core(attn_other)
    attn_other, lin_grads, x_steps = pin((attn_other, lin_grads, x_steps))

    def attn_part(step):
        return attn_mine[step].astype(wide) + attn_other[step].astype(wide)

    total = ring_next(attn_part(1).astype(narrow))
    up_experts = weight_grads([(x_steps, up_of[:2])])
    up_experts[1] = swap_core(up_experts[1])
    norm_one_part = sum(
        dot_nt(lin_grads[:, i * width : (i + 1) * width], weight)
        for i, weight in enumerate((q_weight, k_weight, v_weight))
    ).astype(narrow)
    normed_one_grad = plane_scatter(
        [norm_one_part[j * rows : (j + 1) * rows] for j in range(n_tensor)]
    )
    attn_gain_part = jnp.sum(normed_one_grad * hat_one, axis=0)
    scaled_one = normed_one_grad * attn_gain
    input_grad = hidden_grad + inverse_one * (
        scaled_one - hat_one * jnp.mean(scaled_one * hat_one, axis=1, keepdims=True)
    )

    gains = sum_over_plane(
        jnp.concatenate(
            [
                attn_gain_part,
                mlp_gain_part,
                router_grad_part,
                jnp.broadcast_to(squared_own, (128,)),
            ]
        )
    )
    gains, down_experts, gate_experts, up_experts = pin(
        (gains, down_experts, gate_experts, up_experts)
    )

    def small_rows():
        biases = [
            jnp.sum(grad.astype(wide), axis=0)
            for grad in (query_lin_grad, key_lin_grad, value_lin_grad)
        ]
        small = jnp.concatenate([gains, *biases])
        small = small + swap_core(small)
        lanes = 4 * width
        count = -(-small.shape[0] // (8 * lanes)) * 8
        small = jnp.pad(small, (0, count * lanes - small.shape[0])).reshape(count, lanes)
        high = small.astype(narrow)
        return jnp.concatenate([high, (small - high.astype(wide)).astype(narrow)], axis=0)

    expert_down_grad = expert_sum(*down_experts)[None]
    expert_gate_grad = expert_sum(*gate_experts).T[None]
    expert_up_grad = expert_sum(*up_experts).T[None]
    shared_down_grad = shared_down_all.astype(wide)
    shared_gate_grad = turn(shared_two_all, n_dp, 0, f_shared)
    shared_up_grad = turn(shared_two_all, n_dp, 1, f_shared)
    ties = [(), (shared_down_grad,)]
    for step in range(2, chips):
        if step - 2 < len(ties):
            total = after(total, *ties[step - 2])
        total = ring_next((attn_part(step) + total.astype(wide)).astype(narrow))
    total = after(total, input_grad, shared_gate_grad)
    attn_own = (attn_part(0) + total.astype(wide)).astype(narrow)
    attn_held = [jnp.concatenate([attn_own, small_rows()], axis=0)]
    ties = [(shared_up_grad, expert_down_grad), (expert_gate_grad,)]
    swapped, sums = [], None

    def placed(first, last, before):
        blocks, places_at = [], []
        for step in range(first, last):
            blocks += [attn_held[step], swapped[step]]
            places_at += [source * piece for source in sources[step]]
        return assemble(blocks, jnp.stack(places_at), piece, before)

    for step in range(chips - 1):
        swapped.append(swap_core(attn_held[-1]))
        block = ring_next(attn_held[-1])
        if step == 1:
            sums = placed(0, 1, None)
        if step < len(ties):
            block, swapped, sums = pin((block, swapped, sums, ties[step]))[:3]
        attn_held.append(block)
    swapped.append(swap_core(attn_held[-1]))
    q_sum, k_sum, v_sum, o_sum = placed(1, chips, sums)
    small = 0.0
    for chip in range(chips):
        rows_of = sum(
            jnp.where(at == chip, block[piece:].astype(wide), 0.0)
            for block, at in zip(attn_held, ring_places)
        )
        small = small + rows_of
    half = small.shape[0] // 2
    small = (small[:half] + small[half:]).reshape(-1)

    attn_gain_grad, mlp_gain_grad, shared_router_grad = (small[i * D : (i + 1) * D] for i in range(3))
    teacher_loss = small[3 * D] / (valid_count * D)
    biases = small[3 * D + 128 :]
    return (
        result.astype(narrow),
        teacher_loss,
        input_grad,
        attn_gain_grad,
        q_sum,
        biases[:width],
        k_sum,
        biases[width : 2 * width],
        v_sum,
        biases[2 * width : 3 * width],
        o_sum,
        mlp_gain_grad,
        expert_gate_grad,
        expert_up_grad,
        expert_down_grad,
        shared_gate_grad,
        shared_up_grad,
        shared_down_grad,
        shared_router_grad,
    )


def solution(mesh):
    return jax.shard_map(
        shards,
        mesh=mesh,
        in_specs=(
            P(("dp", "tensor"), None),
            P(),
            P(None, "tensor"),
            P("tensor"),
            P(None, "tensor"),
            P("tensor"),
            P(None, "tensor"),
            P("tensor"),
            P("tensor", None),
            P(),
            P("dp", None, "tensor"),
            P("dp", None, "tensor"),
            P("dp", "tensor", None),
            P(None, "tensor"),
            P(None, "tensor"),
            P("tensor", None),
            P(),
            P("dp", None),
            P("dp", None),
            P(),
            P(),
            P(("dp", "tensor"), None),
            P(("dp", "tensor"), None),
        ),
        out_specs=(
            P(("dp", "tensor"), None),
            P(),
            P(("dp", "tensor"), None),
            P(),
            P(None, "tensor"),
            P("tensor"),
            P(None, "tensor"),
            P("tensor"),
            P(None, "tensor"),
            P("tensor"),
            P("tensor", None),
            P(),
            P("dp", None, "tensor"),
            P("dp", None, "tensor"),
            P("dp", "tensor", None),
            P(None, "tensor"),
            P(None, "tensor"),
            P("tensor", None),
            P(),
        ),
        check_vma=False,
    )
```
